32 devices in a mesh: pts: 8 (over z, y), tile: 4 (over x, core).
Axes of the slice: x: 2, y: 2, z: 4, core: 2. Of those that a mesh axis runs over, the one named last changes fastest.
Arguments:
- values: float32 [32, 64, 1024], P(('pts', 'tile')), may hold values from -6 to 6
- cycle_taps: float32 [32, 64, 8, 1024], P(('pts', 'tile')), may hold values from 0 to 1
- phi_taps: float32 [32, 64, 8, 1024], P(('pts', 'tile')), may hold values from 0 to 1
- cycle_start: int32 [32, 64, 1024], P(('pts', 'tile')), may hold values from 0 to 24
- phi_start: int32 [32, 64, 1024], P(('pts', 'tile')), may hold values from 0 to 1016
- tile_list: int32 [32, 8, 8], replicated, may hold values from 0 to 255, as said below
- response: float32 [4097], replicated, may hold values from 0.05 to 1
Outputs:
- filtered_grid: float32 [256, 32, 8192], P(None, 'tile', 'pts')
- gradient: float32 [32, 64, 1024], P(('pts', 'tile'))
The draws below stay inside these ranges and needn't reach their ends.
Inputs may be any that keep to these rules, and one draw needn't show every extreme that they name: For each point block b and phi column q the 8 entries tile_list[b, q, :] are distinct cycle blocks; slot q * 8 + k of block b holds exactly 1024 points, all of whose taps lie in the tile of cycle block tile_list[b, q, k] and phi column q.
All inputs are finite; a program needn't handle non-finite values.
Results may differ from the reference program's by a relative error of at most 0.0003.
Values sent between devices are 32-bit elements; how exact they have to be, the bound alone decides.
No kernel may reach another device: no remote copies, remote signals or barrier semaphores. Data moves between devices by JAX's collectives and lax.ppermute only.
A program may use at most 128 MiB of HBM per device.

```python
import math
import jax
import jax.numpy as jnp
from jax import lax

NPHI = 8192
TR = 32
TAPS = 8
NJ = 256
SLOTS_DEV = 64
PPS = 1024
COLS = 8
BLOCKS = 32
SLOT = 8
TP = 1024
FREQS = 4097


def draw_tile_list(key, part):
    scores = jax.random.randint(key, (BLOCKS, COLS, NJ), 0, 1048576, dtype=jnp.int32)
    ranked = scores * NJ + lax.broadcasted_iota(jnp.int32, (BLOCKS, COLS, NJ), 2)
    ordering = jnp.argsort(ranked, axis=-1, stable=True)
    return ordering[:, :, :SLOT].astype(jnp.int32)


def with_ends(values, own_key, least, top_value):
    dims = values.shape
    spot = [jax.random.randint(jax.random.fold_in(own_key, axis), (), 0, dims[axis]) for axis in range(len(dims))]
    values = values.at[tuple(spot)].set(least)
    longest = dims.index(max(dims))
    spot[longest] = (spot[longest] + 1) % dims[longest]
    return values.at[tuple(spot)].set(top_value)


def block_scale(stream_key, extent, shards, smallest, largest):
    gain, own = 1.0, jax.random.fold_in(stream_key, 6)
    for axis_at, shards_of in shards:
        draws = jnp.exp(jax.random.uniform(jax.random.fold_in(own, axis_at), (shards_of,), jnp.float32, smallest / len(shards), largest / len(shards)))
        gain = gain * jnp.repeat(draws, extent[axis_at] // shards_of).reshape([-1 if axis == axis_at else 1 for axis in range(len(extent))])
    return gain


def gaussian(own_key, shape, deviation, limit, pieces=(), kind=jnp.bfloat16):
    entries = deviation * jax.random.normal(own_key, shape, jnp.float32)
    if pieces:
        entries = entries * block_scale(own_key, shape, pieces, -0.22, 0.18)
    return jnp.clip(entries, -limit, limit).astype(kind)


def setup_inputs(seed: int = 0) -> dict:
    splits = jax.random.split(jax.random.key(seed), 8)
    return {
        "values": gaussian(splits[0], (BLOCKS, SLOTS_DEV, PPS), 1.0, 6.0, ((0, 32),), jnp.float32),
        "cycle_taps": jnp.clip(1.0 * jax.random.uniform(splits[1], (BLOCKS, SLOTS_DEV, TAPS, PPS), jnp.float32) ** block_scale(splits[1], (BLOCKS, SLOTS_DEV, TAPS, PPS), ((0, 32),), -0.2, 0.2), 0.0, 1.0),
        "phi_taps": jnp.clip(1.0 * jax.random.uniform(splits[2], (BLOCKS, SLOTS_DEV, TAPS, PPS), jnp.float32) ** block_scale(splits[2], (BLOCKS, SLOTS_DEV, TAPS, PPS), ((0, 32),), -0.2, 0.2), 0.0, 1.0),
        "cycle_start": with_ends(jax.random.randint(splits[3], (BLOCKS, SLOTS_DEV, PPS), 0, TR - TAPS + 1), jax.random.fold_in(splits[3], 1), 0, TR - TAPS).astype(jnp.int32),
        "phi_start": with_ends(jax.random.randint(splits[4], (BLOCKS, SLOTS_DEV, PPS), 0, TP - TAPS + 1), jax.random.fold_in(splits[4], 1), 0, TP - TAPS).astype(jnp.int32),
        "tile_list": draw_tile_list(jax.random.fold_in(splits[7], 71), 0),
        "response": jnp.clip(jnp.exp(jax.random.uniform(splits[6], (FREQS,), jnp.float32, math.log(0.05), math.log(1.0))), 0.05, 1.0),
    }


def cell_layout(block_index, tile_list, cycle_start, phi_start):
    slot_column = jnp.arange(SLOTS_DEV, dtype=jnp.int32) // SLOT
    slot_rank = jnp.arange(SLOTS_DEV, dtype=jnp.int32) % SLOT
    tap_offsets = jnp.arange(TAPS, dtype=jnp.int32)
    listing = tile_list[block_index]
    tile_ids = listing[slot_column, slot_rank].astype(jnp.int32)
    cycle_cells = tile_ids[:, None, None] * TR + cycle_start[block_index][:, None, :] + tap_offsets[None, :, None]
    phi_cells = slot_column[:, None, None] * TP + phi_start[block_index][:, None, :] + tap_offsets[None, :, None]
    return (cycle_cells[:, :, None, :] * NPHI + phi_cells[:, None, :, :]).astype(jnp.int32)


def tap_weights(block_index, cycle_taps, phi_taps):
    return cycle_taps[block_index][:, :, None, :] * phi_taps[block_index][:, None, :, :]


def reference(values, cycle_taps, phi_taps, cycle_start, phi_start, tile_list, response):
    def spread_block(block_index, grid_flat):
        block_index = jnp.asarray(block_index).astype(jnp.int32)
        cell_index = cell_layout(block_index, tile_list, cycle_start, phi_start)
        weight = tap_weights(block_index, cycle_taps, phi_taps) * values[block_index][:, None, None, :]
        return grid_flat.at[cell_index.reshape(-1)].add(weight.reshape(-1))

    grid_flat = lax.fori_loop(0, BLOCKS, spread_block, jnp.zeros((NJ * TR * NPHI,), jnp.float32))
    cycle_rows = grid_flat.reshape(NJ * TR, NPHI)
    spectrum = jnp.fft.rfft(cycle_rows, axis=1) * response[None, :]
    filtered = jnp.fft.irfft(spectrum, n=NPHI, axis=1).astype(jnp.float32)
    filtered_flat = filtered.reshape(-1)

    def read_block(block_index):
        cell_index = cell_layout(block_index, tile_list, cycle_start, phi_start)
        weight = tap_weights(block_index, cycle_taps, phi_taps)
        return jnp.sum(filtered_flat[cell_index] * weight, axis=(1, 2))

    gradient = lax.map(read_block, jnp.arange(BLOCKS, dtype=jnp.int32))
    return filtered.reshape(NJ, TR, NPHI), gradient
```

```python
import functools
import math

import jax
import jax.numpy as jnp
import numpy as np
from jax import lax
from jax.experimental import pallas as pl
from jax.experimental.pallas import tpu as pltpu
from jax.sharding import PartitionSpec as P

NPHI = 8192
TR = 32
TAPS = 8
LANES = 128
GROUPS = 8
RADIX = 64
STEP_SLOTS = 8
VMEM_LIMIT = 50 * 1024 * 1024

f32 = jnp.float32
bf16 = jnp.bfloat16


def split(x):
    high = x.astype(bf16)
    low = (x - high.astype(f32)).astype(bf16)
    return high, low


def split_f32(x):
    high = x.astype(bf16).astype(f32)
    return high, x - high


def shifted_window(taps, shift):
    n = taps.shape[1]
    window = jnp.concatenate([taps, jnp.zeros((8, n), f32)], axis=0)
    both = jnp.concatenate([shift, shift], axis=0)
    for bit in (1, 2, 4):
        moved = pltpu.roll(window, bit, 0)
        window = jnp.where((both & bit) != 0, moved, window)
    return window[:8], window[8:]


def cycle_factor(taps, starts):
    cycle_start, phi_start = starts
    first, second = shifted_window(taps, cycle_start & 7)
    block = cycle_start >> 3
    rows = []
    for h in range(TR // 8):
        rows.append(jnp.where(block == h, first, jnp.where(block == h - 1, second, 0.0)))
    rows = jnp.concatenate(rows, axis=0)
    n = rows.shape[1]
    mine = lax.broadcasted_iota(jnp.int32, (GROUPS, n), 0) == (phi_start >> 7)
    parts = []
    for part in split_f32(rows):
        spread = jnp.where(mine[None], part[:, None, :], 0.0)
        parts.append(spread.reshape(TR * GROUPS, n).astype(bf16))
    return parts


def spread_kernel(values, cycle_taps, phi_taps, cycle_start, phi_start, out):
    n = values.shape[1]

    def one(k, carry):
        cycle_at = jnp.broadcast_to(cycle_start[pl.ds(k, 1), :], (8, n))
        phi_at = jnp.broadcast_to(phi_start[pl.ds(k, 1), :], (8, n))
        loaded = cycle_taps[k] * values[pl.ds(k, 1), :]
        left_high, left_low = cycle_factor(loaded, (cycle_at, phi_at))
        lane = phi_at & 127
        first, second = shifted_window(phi_taps[k], lane & 7)
        block = lane >> 3
        pieces = []
        for h in range(17):
            pieces.append(jnp.where(block == h, first, jnp.where(block == h - 1, second, 0.0)))
        pieces.append(jnp.zeros((256 - 17 * 8, n), f32))
        right_high, right_low = split(jnp.concatenate(pieces, axis=0))
        dims = (((1,), (1,)), ((), ()))
        product = lax.dot_general(left_high, right_high, dims, preferred_element_type=f32)
        product += lax.dot_general(left_high, right_low, dims, preferred_element_type=f32)
        product += lax.dot_general(left_low, right_high, dims, preferred_element_type=f32)
        tile = product[:, :128] + pltpu.roll(product[:, 128:], 1, 0)
        parts = out.shape[1]
        for r in range(TR):
            out[r % GROUPS, r // GROUPS, k] = tile[r * 8 : r * 8 + 8]
        return carry

    lax.fori_loop(0, STEP_SLOTS, one, 0)


def spread_tiles(values, cycle_taps, phi_taps, cycle_start, phi_start, part_count):
    slots, n = values.shape
    flat = pl.BlockSpec((STEP_SLOTS, n), lambda i: (i, 0))
    taps = pl.BlockSpec((STEP_SLOTS, TAPS, n), lambda i: (i, 0, 0))
    rows = TR // part_count
    return pl.pallas_call(
        spread_kernel,
        grid=(slots // STEP_SLOTS,),
        in_specs=[flat, taps, taps, flat, flat],
        out_specs=pl.BlockSpec((rows, part_count, STEP_SLOTS, 8, LANES), lambda i: (0, 0, i, 0, 0)),
        out_shape=jax.ShapeDtypeStruct((rows, part_count, slots, 8, LANES), f32),
        compiler_params=pltpu.CompilerParams(vmem_limit_bytes=VMEM_LIMIT),
        cost_estimate=pl.CostEstimate(
            flops=slots * 2 * 3 * 256 * 256 * n, bytes_accessed=slots * (19 + 32) * n * 4, transcendentals=0
        ),
        name="spread",
    )(values, cycle_taps, phi_taps, cycle_start, phi_start)


def read_kernel(cycle_taps, phi_taps, cycle_start, phi_start, tiles, out):
    n = cycle_start.shape[1]

    def one(k, carry):
        cycle_at = jnp.broadcast_to(cycle_start[pl.ds(k, 1), :], (8, n))
        phi_at = jnp.broadcast_to(phi_start[pl.ds(k, 1), :], (8, n))
        right_high, right_low = cycle_factor(cycle_taps[k], (cycle_at, phi_at))
        tile = jnp.concatenate([tiles[r % GROUPS, r // GROUPS, k] for r in range(TR)], axis=0)
        following = pltpu.roll(tile, TR * GROUPS - 1, 0)
        wide = jnp.concatenate([tile.T, following[:, :128].T[:16]], axis=0)
        left_high, left_low = split(wide)
        dims = (((1,), (0,)), ((), ()))
        picked = lax.dot_general(left_high, right_high, dims, preferred_element_type=f32)
        picked += lax.dot_general(left_low, right_high, dims, preferred_element_type=f32)
        picked += lax.dot_general(left_high, right_low, dims, preferred_element_type=f32)
        lane = phi_at & 127
        first, second = shifted_window(phi_taps[k], lane & 7)
        block = lane >> 3
        low = picked[:8]
        high = picked[8:16]
        for h in range(1, 16):
            here = block == h
            low = jnp.where(here, picked[h * 8 : h * 8 + 8], low)
            high = jnp.where(here, picked[h * 8 + 8 : h * 8 + 16], high)
        out[pl.ds(k, 1), :] = jnp.sum(low * first + high * second, axis=0, keepdims=True)
        return carry

    lax.fori_loop(0, STEP_SLOTS, one, 0)


def read_points(cycle_taps, phi_taps, cycle_start, phi_start, tiles):
    slots, n = cycle_start.shape
    flat = pl.BlockSpec((STEP_SLOTS, n), lambda i: (i, 0))
    taps = pl.BlockSpec((STEP_SLOTS, TAPS, n), lambda i: (i, 0, 0))
    rows, part_count = tiles.shape[:2]
    return pl.pallas_call(
        read_kernel,
        grid=(slots // STEP_SLOTS,),
        in_specs=[
            taps,
            taps,
            flat,
            flat,
            pl.BlockSpec((rows, part_count, STEP_SLOTS, 8, LANES), lambda i: (0, 0, i, 0, 0)),
        ],
        out_specs=flat,
        out_shape=jax.ShapeDtypeStruct((slots, n), f32),
        compiler_params=pltpu.CompilerParams(vmem_limit_bytes=VMEM_LIMIT),
        cost_estimate=pl.CostEstimate(
            flops=slots * 2 * 3 * 256 * 256 * n, bytes_accessed=slots * (19 + 32) * n * 4, transcendentals=0
        ),
        name="read_back",
    )(cycle_taps, phi_taps, cycle_start, phi_start, tiles)


def collect_kernel(tile_list, arrived, out):
    step = pl.program_id(0)
    sources = arrived.shape[0]
    columns, per_column = tile_list.shape[1], tile_list.shape[2]

    @pl.when(step == 0)
    def _():
        def clear(j, carry):
            out[j] = jnp.zeros(out.shape[1:], f32)
            return carry

        lax.fori_loop(0, out.shape[0], clear, 0)

    def one(b, carry):
        for q in range(columns):
            owners = [tile_list[step * sources + b, q, k] for k in range(per_column)]
            sums = [out[owners[k], q] + arrived[b, q * per_column + k] for k in range(per_column)]
            for k in range(per_column):
                out[owners[k], q] = sums[k]
        return carry

    lax.fori_loop(0, sources, one, 0)


def collect(arrived, tile_list, cycle_blocks):
    blocks, slots = arrived.shape[:2]
    columns = tile_list.shape[1]
    step = 4
    return pl.pallas_call(
        collect_kernel,
        grid=(blocks // step,),
        in_specs=[
            pl.BlockSpec(memory_space=pltpu.SMEM),
            pl.BlockSpec((step, slots, 8, LANES), lambda i: (i, 0, 0, 0)),
        ],
        out_specs=pl.BlockSpec((cycle_blocks, columns, 8, LANES), lambda i: (0, 0, 0, 0)),
        out_shape=jax.ShapeDtypeStruct((cycle_blocks, columns, 8, LANES), f32),
        compiler_params=pltpu.CompilerParams(vmem_limit_bytes=VMEM_LIMIT),
        cost_estimate=pl.CostEstimate(flops=blocks * slots * 1024, bytes_accessed=16 * 2**20, transcendentals=0),
        name="collect",
    )(tile_list, arrived)


def pick_kernel(tile_list, filtered, out):
    step = pl.program_id(0)
    columns, per_column = tile_list.shape[1], tile_list.shape[2]

    def one(b, carry):
        for q in range(columns):
            for k in range(per_column):
                out[b, q * per_column + k] = filtered[q, tile_list[step * out.shape[0] + b, q, k]]
        return carry

    lax.fori_loop(0, out.shape[0], one, 0)


def pick(filtered, tile_list):
    blocks, columns, per_column = tile_list.shape
    slots = columns * per_column
    step = 4
    return pl.pallas_call(
        pick_kernel,
        grid=(blocks // step,),
        in_specs=[
            pl.BlockSpec(memory_space=pltpu.SMEM),
            pl.BlockSpec(filtered.shape, lambda i: (0, 0, 0, 0)),
        ],
        out_specs=pl.BlockSpec((step, slots, 8, LANES), lambda i: (i, 0, 0, 0)),
        out_shape=jax.ShapeDtypeStruct((blocks, slots, 8, LANES), f32),
        compiler_params=pltpu.CompilerParams(vmem_limit_bytes=VMEM_LIMIT),
        cost_estimate=pl.CostEstimate(flops=0, bytes_accessed=16 * 2**20, transcendentals=0),
        name="pick",
    )(tile_list, filtered)


def merge_kernel(arrived, out):
    rows, blocks = arrived.shape[:2]
    for c in range(8):
        for j in range(blocks):
            out[j, :, c * LANES : (c + 1) * LANES] = arrived[:, j, c, :]


def merge_rows(arrived):
    rows, blocks = arrived.shape[:2]
    step = 32
    return pl.pallas_call(
        merge_kernel,
        grid=(blocks // step,),
        in_specs=[pl.BlockSpec((rows, step, 8, LANES), lambda i: (0, i, 0, 0))],
        out_specs=pl.BlockSpec((step, rows, 8 * LANES), lambda i: (i, 0, 0)),
        out_shape=jax.ShapeDtypeStruct((blocks, rows, 8 * LANES), f32),
        compiler_params=pltpu.CompilerParams(vmem_limit_bytes=VMEM_LIMIT),
        cost_estimate=pl.CostEstimate(flops=0, bytes_accessed=16 * 2**20, transcendentals=0),
        name="merge_rows",
    )(arrived)


@functools.cache
def dft_tables():
    a = np.arange(RADIX)
    b = np.arange(LANES)
    first = 2.0 * np.pi / RADIX * (np.outer(a, a) % RADIX)
    twist = 2.0 * np.pi / NPHI * np.outer(a, b)
    second = 2.0 * np.pi / LANES * (np.outer(b, b) % LANES)
    c1, s1, c2, s2 = np.cos(first), np.sin(first), np.cos(second), np.sin(second)
    ahead_first = np.block([[c1, s1], [-s1, c1]])
    back_first = np.block([[c1, -s1], [s1, c1]])
    ahead_second = np.block([[c2, -s2], [s2, c2]])
    back_second = np.block([[c2, s2], [-s2, c2]])

    def pair(table):
        high = np.asarray(table, np.float32).astype(bf16)
        low = (table - high.astype(np.float64)).astype(np.float32).astype(bf16)
        return high, low

    def wide(table):
        high, low = pair(table)
        return np.concatenate([high, high, low], axis=1)

    def stacked(table):
        return np.stack(pair(table))

    return (
        wide(ahead_first),
        wide(back_first),
        stacked(ahead_second),
        stacked(back_second),
        np.cos(twist).astype(np.float32),
        np.sin(twist).astype(np.float32),
    )


def dot(lhs, rhs):
    return lax.dot_general(lhs, rhs, (((1,), (0,)), ((), ())), preferred_element_type=f32)


def filter_kernel(ahead_first, back_first, ahead_second, back_second, cos_twist, sin_twist, gain, grid, out):
    blocks = grid.shape[0]
    pairs = blocks // 2
    cos_t, sin_t = cos_twist[...], sin_twist[...]
    middle = []
    for p in range(pairs):
        cell = jnp.concatenate([grid[2 * p].reshape(RADIX, LANES), grid[2 * p + 1].reshape(RADIX, LANES)], axis=0)
        high, low = split(cell)
        turned = dot(ahead_first[...], jnp.concatenate([high, low, high], axis=0))
        real, imag = turned[:RADIX], turned[RADIX:]
        middle.append(jnp.concatenate([real * cos_t + imag * sin_t, imag * cos_t - real * sin_t], axis=1))
    middle = jnp.concatenate(middle, axis=0)

    def second(x, table):
        high, low = split(x)
        return dot(high, table[0]) + dot(low, table[0]) + dot(high, table[1])

    spectrum = second(middle, ahead_second)
    spectrum = (spectrum.reshape(pairs, RADIX, 2 * LANES) * gain[...][None]).reshape(pairs * RADIX, 2 * LANES)
    middle = second(spectrum, back_second)
    for p in range(pairs):
        real, imag = middle[p * RADIX : (p + 1) * RADIX, :LANES], middle[p * RADIX : (p + 1) * RADIX, LANES:]
        cell = jnp.concatenate([real * cos_t - imag * sin_t, imag * cos_t + real * sin_t], axis=0)
        high, low = split(cell)
        turned = dot(back_first[...], jnp.concatenate([high, low, high], axis=0))
        for q in range(8):
            out[q, 2 * p] = turned[q * 8 : q * 8 + 8]
            out[q, 2 * p + 1] = turned[RADIX + q * 8 : RADIX + q * 8 + 8]


def filter_cycles(grid, response):
    tables = dft_tables()
    full = jnp.concatenate([response, response[-2:0:-1]])
    gain = full.reshape(LANES, RADIX).T * (1.0 / NPHI)
    gain = jnp.concatenate([gain, gain], axis=1)
    blocks = grid.shape[0]
    step = 16
    whole = [
        pl.BlockSpec(t.shape, functools.partial(lambda nd, i: (0,) * nd, t.ndim)) for t in tables + (gain,)
    ]
    return pl.pallas_call(
        filter_kernel,
        grid=(blocks // step,),
        in_specs=whole + [pl.BlockSpec((step, 8, 8, LANES), lambda i: (i, 0, 0, 0))],
        out_specs=pl.BlockSpec((8, step, 8, LANES), lambda i: (0, i, 0, 0)),
        out_shape=jax.ShapeDtypeStruct((8, blocks, 8, LANES), f32),
        compiler_params=pltpu.CompilerParams(vmem_limit_bytes=VMEM_LIMIT),
        cost_estimate=pl.CostEstimate(
            flops=blocks // 2 * 3 * 2 * 2 * (128 * 128 * 128 + 64 * 256 * 256),
            bytes_accessed=16 * 2**20,
            transcendentals=0,
        ),
        name="filter_cycles",
    )(*[jnp.asarray(t) for t in tables], gain, grid)


def row_owner_plan(values, cycle_taps, phi_taps, cycle_start, phi_start, tile_list, response):
    part_count = lax.axis_size("tile")
    rows = TR // part_count
    blocks, columns, per_column = tile_list.shape
    slots = columns * per_column
    cycle_blocks = 256
    values, cycle_taps, phi_taps = values[0], cycle_taps[0], phi_taps[0]
    cycle_start, phi_start = cycle_start[0], phi_start[0]
    tiles = spread_tiles(values, cycle_taps, phi_taps, cycle_start, phi_start, part_count)
    tiles = tiles.reshape(rows * part_count, slots, 8, LANES)
    arrived = lax.all_to_all(tiles, ("pts", "tile"), 0, 0, tiled=True)
    grid = collect(arrived, tile_list, cycle_blocks)
    filtered = filter_cycles(grid, response)
    picked = pick(filtered, tile_list)
    returned = lax.all_to_all(picked, ("pts", "tile"), 0, 0, tiled=True)
    rows_here = lax.all_to_all(filtered, "pts", 0, 0, tiled=True)
    gradient = read_points(
        cycle_taps, phi_taps, cycle_start, phi_start, returned.reshape(rows, part_count, slots, 8, LANES)
    )
    return merge_rows(rows_here), gradient[None]


precise = lax.Precision.HIGHEST


def contract(formula, lhs_array, rhs_array):
    return jnp.einsum(formula, lhs_array, rhs_array, precision=precise)


def spread_matrix(weights, starts, extent):
    offsets = lax.broadcasted_iota(jnp.int32, (1, 1, extent), 2) - starts[:, :, None]
    result = jnp.zeros(starts.shape + (extent,), jnp.float32)
    for tap_index in range(weights.shape[1]):
        result = result + jnp.where(offsets == tap_index, weights[:, tap_index, :, None], 0.0)
    return result


def angle_table(rows_count, cols_count, modulus):
    left_index = lax.broadcasted_iota(jnp.int32, (rows_count, cols_count), 0)
    right_index = lax.broadcasted_iota(jnp.int32, (rows_count, cols_count), 1)
    phase_int = left_index * right_index % modulus
    angles = phase_int.astype(jnp.float32) * (2.0 * math.pi / modulus)
    return (jnp.cos(angles), jnp.sin(angles))


def filter_by_einsum(cycle_rows, response):
    length = cycle_rows.shape[-1]
    second = length // RADIX
    cos_first, sin_first = angle_table(RADIX, RADIX, RADIX)
    cos_twist, sin_twist = angle_table(RADIX, second, length)
    cos_second, sin_second = angle_table(second, second, second)
    blocks = cycle_rows.reshape(cycle_rows.shape[:2] + (RADIX, second))
    real_one = contract("giab,ak->gikb", blocks, cos_first)
    imag_one = -contract("giab,ak->gikb", blocks, sin_first)
    real_two = real_one * cos_twist + imag_one * sin_twist
    imag_two = imag_one * cos_twist - real_one * sin_twist
    real_freq = contract("gikb,bm->gikm", real_two, cos_second) + contract(
        "gikb,bm->gikm", imag_two, sin_second
    )
    imag_freq = contract("gikb,bm->gikm", imag_two, cos_second) - contract(
        "gikb,bm->gikm", real_two, sin_second
    )
    full_response = jnp.concatenate([response, response[-2:0:-1]])
    gain_table = full_response.reshape(second, RADIX).T
    real_freq = real_freq * gain_table
    imag_freq = imag_freq * gain_table
    real_back = contract("gikm,bm->gikb", real_freq, cos_second) - contract(
        "gikm,bm->gikb", imag_freq, sin_second
    )
    imag_back = contract("gikm,bm->gikb", imag_freq, cos_second) + contract(
        "gikm,bm->gikb", real_freq, sin_second
    )
    real_turn = real_back * cos_twist - imag_back * sin_twist
    imag_turn = imag_back * cos_twist + real_back * sin_twist
    spatial = contract("gikb,ka->giab", real_turn, cos_first) - contract(
        "gikb,ka->giab", imag_turn, sin_first
    )
    return (spatial / length).reshape(cycle_rows.shape)


def accumulate(arrived, wanted, cycle_blocks):
    selector = (
        lax.broadcasted_iota(jnp.int32, (cycle_blocks, wanted.size), 0) == wanted.reshape(1, -1)
    ).astype(jnp.float32)
    flattened = arrived.reshape(wanted.size, -1)
    return jnp.dot(selector, flattened, precision=precise).reshape(
        (cycle_blocks,) + arrived.shape[2:]
    )


def column_owner_plan(values, cycle_taps, phi_taps, cycle_start, phi_start, tile_list, response):
    columns = lax.axis_size("pts")
    part_count = lax.axis_size("tile")
    column = lax.axis_index("pts")
    per_column = values.shape[1] // columns
    tile_width = NPHI // columns
    cycle_part = TR // part_count
    cycle_weights = spread_matrix(cycle_taps[0], cycle_start[0], TR)
    phi_weights = spread_matrix(phi_taps[0], phi_start[0], tile_width)
    loaded = cycle_weights * values[0][:, :, None]
    cycle_split = cycle_weights.reshape(columns, per_column, values.shape[2], part_count, cycle_part)
    loaded_split = loaded.reshape(columns, per_column, values.shape[2], part_count, cycle_part)
    phi_split = phi_weights.reshape(columns, per_column, values.shape[2], tile_width)
    partial_value = contract("qkitr,qkic->qtkrc", loaded_split, phi_split)
    partial_value = partial_value.reshape(columns * part_count, per_column, cycle_part, tile_width)
    arrived = lax.all_to_all(
        partial_value, ("pts", "tile"), split_axis=0, concat_axis=0, tiled=True
    )
    wanted = lax.dynamic_index_in_dim(tile_list, column, 1, keepdims=False)
    owned_tiles = accumulate(arrived, wanted, 256)
    whole_cycles = filter_by_einsum(
        lax.all_to_all(owned_tiles, "pts", split_axis=0, concat_axis=2, tiled=True), response
    )
    filtered = lax.all_to_all(whole_cycles, "pts", split_axis=2, concat_axis=0, tiled=True)
    picked = jnp.take(filtered, wanted.reshape(-1), axis=0)
    picked = picked.reshape(columns * part_count, per_column, cycle_part, tile_width)
    returned = lax.all_to_all(picked, ("pts", "tile"), split_axis=0, concat_axis=0, tiled=True)
    returned = returned.reshape(columns, part_count, per_column, cycle_part, tile_width)
    rows_read = contract("qkitr,qtkrc->qkic", cycle_split, returned)
    gradient = jnp.sum(rows_read * phi_split, axis=-1).reshape(values.shape[1], values.shape[2])
    return (filtered, gradient[None])


def solution(mesh):
    columns, part_count = mesh.shape["pts"], mesh.shape["tile"]
    rows_fit = columns * part_count == TR and NPHI // columns == GROUPS * LANES
    return jax.shard_map(
        row_owner_plan if rows_fit else column_owner_plan,
        mesh=mesh,
        in_specs=(
            P(("pts", "tile"), None, None),
            P(("pts", "tile"), None, None, None),
            P(("pts", "tile"), None, None, None),
            P(("pts", "tile"), None, None),
            P(("pts", "tile"), None, None),
            P(),
            P(),
        ),
        out_specs=(P(None, "tile", "pts"), P(("pts", "tile"), None, None)),
        check_vma=False,
    )
```

```python
import functools
import math

import jax
import jax.numpy as jnp
import numpy as np
from jax import lax
from jax.experimental import pallas as pl
from jax.experimental.pallas import tpu as pltpu
from jax.sharding import PartitionSpec as P

NPHI = 8192
TR = 32
TAPS = 8
LANES = 128
GROUPS = 8
RADIX = 64
STEP_SLOTS = 8
VMEM_LIMIT = 50 * 1024 * 1024

f32 = jnp.float32
bf16 = jnp.bfloat16


def split(x):
    high = x.astype(bf16)
    low = (x - high.astype(f32)).astype(bf16)
    return high, low


def split_f32(x):
    high = x.astype(bf16).astype(f32)
    return high, x - high


def shifted_window(taps, shift):
    n = taps.shape[1]
    window = jnp.concatenate([taps, jnp.zeros((8, n), f32)], axis=0)
    both = jnp.concatenate([shift, shift], axis=0)
    for bit in (1, 2, 4):
        moved = pltpu.roll(window, bit, 0)
        window = jnp.where((both & bit) != 0, moved, window)
    return window[:8], window[8:]


def cycle_factor(taps, starts):
    cycle_start, phi_start = starts
    first, second = shifted_window(taps, cycle_start & 7)
    block = cycle_start >> 3
    rows = []
    for h in range(TR // 8):
        rows.append(jnp.where(block == h, first, jnp.where(block == h - 1, second, 0.0)))
    rows = jnp.concatenate(rows, axis=0)
    n = rows.shape[1]
    mine = lax.broadcasted_iota(jnp.int32, (GROUPS, n), 0) == (phi_start >> 7)
    parts = []
    for part in split_f32(rows):
        spread = jnp.where(mine[None], part[:, None, :], 0.0)
        parts.append(spread.reshape(TR * GROUPS, n).astype(bf16))
    return parts


def spread_kernel(values, cycle_taps, phi_taps, cycle_start, phi_start, out):
    n = values.shape[1]

    def one(k, carry):
        cycle_at = jnp.broadcast_to(cycle_start[pl.ds(k, 1), :], (8, n))
        phi_at = jnp.broadcast_to(phi_start[pl.ds(k, 1), :], (8, n))
        loaded = cycle_taps[k] * values[pl.ds(k, 1), :]
        left_high, left_low = cycle_factor(loaded, (cycle_at, phi_at))
        lane = phi_at & 127
        first, second = shifted_window(phi_taps[k], lane & 7)
        block = lane >> 3
        pieces = []
        for h in range(17):
            pieces.append(jnp.where(block == h, first, jnp.where(block == h - 1, second, 0.0)))
        pieces.append(jnp.zeros((256 - 17 * 8, n), f32))
        right_high, right_low = split(jnp.concatenate(pieces, axis=0))
        dims = (((1,), (1,)), ((), ()))
        product = lax.dot_general(left_high, right_high, dims, preferred_element_type=f32)
        product += lax.dot_general(left_high, right_low, dims, preferred_element_type=f32)
        product += lax.dot_general(left_low, right_high, dims, preferred_element_type=f32)
        tile = product[:, :128] + pltpu.roll(product[:, 128:], 1, 0)
        parts = out.shape[1]
        for r in range(TR):
            out[r % GROUPS, r // GROUPS, k] = tile[r * 8 : r * 8 + 8]
        return carry

    lax.fori_loop(0, STEP_SLOTS, one, 0)


def spread_tiles(values, cycle_taps, phi_taps, cycle_start, phi_start, part_count, first, slots):
    n = values.shape[1]
    begin = first // STEP_SLOTS
    flat = pl.BlockSpec((STEP_SLOTS, n), lambda i: (begin + i, 0))
    taps = pl.BlockSpec((STEP_SLOTS, TAPS, n), lambda i: (begin + i, 0, 0))
    rows = TR // part_count
    return pl.pallas_call(
        spread_kernel,
        grid=(slots // STEP_SLOTS,),
        in_specs=[flat, taps, taps, flat, flat],
        out_specs=pl.BlockSpec((rows, part_count, STEP_SLOTS, 8, LANES), lambda i: (0, 0, i, 0, 0)),
        out_shape=jax.ShapeDtypeStruct((rows, part_count, slots, 8, LANES), f32),
        compiler_params=pltpu.CompilerParams(vmem_limit_bytes=VMEM_LIMIT),
        cost_estimate=pl.CostEstimate(
            flops=slots * 2 * 3 * 256 * 256 * n, bytes_accessed=slots * (19 + 32) * n * 4, transcendentals=0
        ),
        name="spread",
    )(values, cycle_taps, phi_taps, cycle_start, phi_start)


def read_kernel(cycle_taps, phi_taps, cycle_start, phi_start, tiles, out):
    n = cycle_start.shape[1]

    def one(k, carry):
        cycle_at = jnp.broadcast_to(cycle_start[pl.ds(k, 1), :], (8, n))
        phi_at = jnp.broadcast_to(phi_start[pl.ds(k, 1), :], (8, n))
        right_high, right_low = cycle_factor(cycle_taps[k], (cycle_at, phi_at))
        tile = jnp.concatenate([tiles[r % GROUPS, r // GROUPS, k] for r in range(TR)], axis=0)
        following = pltpu.roll(tile, TR * GROUPS - 1, 0)
        wide = jnp.concatenate([tile.T, following[:, :128].T[:16]], axis=0)
        left_high, left_low = split(wide)
        dims = (((1,), (0,)), ((), ()))
        picked = lax.dot_general(left_high, right_high, dims, preferred_element_type=f32)
        picked += lax.dot_general(left_low, right_high, dims, preferred_element_type=f32)
        picked += lax.dot_general(left_high, right_low, dims, preferred_element_type=f32)
        lane = phi_at & 127
        first, second = shifted_window(phi_taps[k], lane & 7)
        block = lane >> 3
        low = picked[:8]
        high = picked[8:16]
        for h in range(1, 16):
            here = block == h
            low = jnp.where(here, picked[h * 8 : h * 8 + 8], low)
            high = jnp.where(here, picked[h * 8 + 8 : h * 8 + 16], high)
        out[pl.ds(k, 1), :] = jnp.sum(low * first + high * second, axis=0, keepdims=True)
        return carry

    lax.fori_loop(0, STEP_SLOTS, one, 0)


def read_points(cycle_taps, phi_taps, cycle_start, phi_start, tiles):
    slots, n = cycle_start.shape
    flat = pl.BlockSpec((STEP_SLOTS, n), lambda i: (i, 0))
    taps = pl.BlockSpec((STEP_SLOTS, TAPS, n), lambda i: (i, 0, 0))
    rows, part_count = tiles.shape[:2]
    return pl.pallas_call(
        read_kernel,
        grid=(slots // STEP_SLOTS,),
        in_specs=[
            taps,
            taps,
            flat,
            flat,
            pl.BlockSpec((rows, part_count, STEP_SLOTS, 8, LANES), lambda i: (0, 0, i, 0, 0)),
        ],
        out_specs=flat,
        out_shape=jax.ShapeDtypeStruct((slots, n), f32),
        compiler_params=pltpu.CompilerParams(vmem_limit_bytes=VMEM_LIMIT),
        cost_estimate=pl.CostEstimate(
            flops=slots * 2 * 3 * 256 * 256 * n, bytes_accessed=slots * (19 + 32) * n * 4, transcendentals=0
        ),
        name="read_back",
    )(cycle_taps, phi_taps, cycle_start, phi_start, tiles)


def collect_kernel(first_column, tile_list, arrived, *rest):
    out = rest[-1]
    step = pl.program_id(0)
    sources, slots = arrived.shape[:2]
    per_column = tile_list.shape[2]

    @pl.when(step == 0)
    def _():
        def clear(j, carry):
            out[j] = rest[0][j] if len(rest) == 2 else jnp.zeros(out.shape[1:], f32)
            return carry

        lax.fori_loop(0, out.shape[0], clear, 0, unroll=8)

    def one(b, carry):
        for c in range(slots // per_column):
            q = first_column + c
            owners = [tile_list[step * sources + b, q, k] for k in range(per_column)]
            sums = [out[owners[k], q] + arrived[b, c * per_column + k] for k in range(per_column)]
            for k in range(per_column):
                out[owners[k], q] = sums[k]
        return carry

    lax.fori_loop(0, sources, one, 0)


def collect(arrived, tile_list, first_column, so_far, cycle_blocks):
    blocks, slots = arrived.shape[:2]
    columns = tile_list.shape[1]
    step = 4
    whole = pl.BlockSpec((cycle_blocks, columns, 8, LANES), lambda i: (0, 0, 0, 0))
    given = [] if so_far is None else [so_far]
    return pl.pallas_call(
        functools.partial(collect_kernel, first_column),
        grid=(blocks // step,),
        in_specs=[
            pl.BlockSpec(memory_space=pltpu.SMEM),
            pl.BlockSpec((step, slots, 8, LANES), lambda i: (i, 0, 0, 0)),
        ]
        + [whole] * len(given),
        out_specs=whole,
        out_shape=jax.ShapeDtypeStruct((cycle_blocks, columns, 8, LANES), f32),
        compiler_params=pltpu.CompilerParams(vmem_limit_bytes=VMEM_LIMIT),
        cost_estimate=pl.CostEstimate(flops=blocks * slots * 1024, bytes_accessed=16 * 2**20, transcendentals=0),
        name="collect",
    )(tile_list, arrived, *given)


def pick_kernel(tile_list, *refs):
    filtered, out = refs[:-1], refs[-1]
    step = pl.program_id(0)
    columns, per_column = tile_list.shape[1], tile_list.shape[2]
    extent = filtered[0].shape[1]

    def one(b, carry):
        for q in range(columns):
            for k in range(per_column):
                j = tile_list[step * out.shape[0] + b, q, k]
                inside = lax.rem(j, extent)
                tile = filtered[0][q, inside]
                for part in range(1, len(filtered)):
                    tile = jnp.where(j >= part * extent, filtered[part][q, inside], tile)
                out[b, q * per_column + k] = tile
        return carry

    lax.fori_loop(0, out.shape[0], one, 0)


def pick(filtered, tile_list):
    blocks, columns, per_column = tile_list.shape
    slots = columns * per_column
    step = 4
    return pl.pallas_call(
        pick_kernel,
        grid=(blocks // step,),
        in_specs=[pl.BlockSpec(memory_space=pltpu.SMEM)]
        + [pl.BlockSpec(part.shape, lambda i: (0, 0, 0, 0)) for part in filtered],
        out_specs=pl.BlockSpec((step, slots, 8, LANES), lambda i: (i, 0, 0, 0)),
        out_shape=jax.ShapeDtypeStruct((blocks, slots, 8, LANES), f32),
        compiler_params=pltpu.CompilerParams(vmem_limit_bytes=VMEM_LIMIT),
        cost_estimate=pl.CostEstimate(flops=0, bytes_accessed=16 * 2**20, transcendentals=0),
        name="pick",
    )(tile_list, *filtered)


def merge_kernel(arrived, *rest):
    out = rest[-1]
    rows, blocks = arrived.shape[:2]
    for c in range(8):
        for j in range(blocks):
            out[j, :, c * LANES : (c + 1) * LANES] = arrived[:, j, c, :]


def merge_rows(arrived, first, cycle_blocks, so_far):
    rows, blocks = arrived.shape[:2]
    step = 32
    begin = first // step
    given = [] if so_far is None else [so_far]
    return pl.pallas_call(
        merge_kernel,
        grid=(blocks // step,),
        in_specs=[pl.BlockSpec((rows, step, 8, LANES), lambda i: (0, i, 0, 0))]
        + [pl.BlockSpec(memory_space=pl.ANY)] * len(given),
        out_specs=pl.BlockSpec((step, rows, 8 * LANES), lambda i: (begin + i, 0, 0)),
        out_shape=jax.ShapeDtypeStruct((cycle_blocks, rows, 8 * LANES), f32),
        input_output_aliases={1: 0} if given else {},
        compiler_params=pltpu.CompilerParams(vmem_limit_bytes=VMEM_LIMIT),
        cost_estimate=pl.CostEstimate(flops=0, bytes_accessed=8 * blocks * rows * 1024, transcendentals=0),
        name="merge_rows",
    )(arrived, *given)


@functools.cache
def dft_tables():
    a = np.arange(RADIX)
    b = np.arange(LANES)
    first = 2.0 * np.pi / RADIX * (np.outer(a, a) % RADIX)
    twist = 2.0 * np.pi / NPHI * np.outer(a, b)
    second = 2.0 * np.pi / LANES * (np.outer(b, b) % LANES)
    c1, s1, c2, s2 = np.cos(first), np.sin(first), np.cos(second), np.sin(second)
    ahead_first = np.block([[c1, s1], [-s1, c1]])
    back_first = np.block([[c1, -s1], [s1, c1]])
    ahead_second = np.block([[c2, -s2], [s2, c2]])
    back_second = np.block([[c2, s2], [-s2, c2]])

    def pair(table):
        high = np.asarray(table, np.float32).astype(bf16)
        low = (table - high.astype(np.float64)).astype(np.float32).astype(bf16)
        return high, low

    def wide(table):
        high, low = pair(table)
        return np.concatenate([high, high, low], axis=1)

    def stacked(table):
        return np.stack(pair(table))

    return (
        wide(ahead_first),
        wide(back_first),
        stacked(ahead_second),
        stacked(back_second),
        np.cos(twist).astype(np.float32),
        np.sin(twist).astype(np.float32),
    )


def dot(lhs, rhs):
    return lax.dot_general(lhs, rhs, (((1,), (0,)), ((), ())), preferred_element_type=f32)


def filter_kernel(ahead_first, back_first, ahead_second, back_second, cos_twist, sin_twist, gain, grid, out):
    blocks = grid.shape[0]
    pairs = blocks // 2
    cos_t, sin_t = cos_twist[...], sin_twist[...]
    middle = []
    for p in range(pairs):
        cell = jnp.concatenate([grid[2 * p].reshape(RADIX, LANES), grid[2 * p + 1].reshape(RADIX, LANES)], axis=0)
        high, low = split(cell)
        turned = dot(ahead_first[...], jnp.concatenate([high, low, high], axis=0))
        real, imag = turned[:RADIX], turned[RADIX:]
        middle.append(jnp.concatenate([real * cos_t + imag * sin_t, imag * cos_t - real * sin_t], axis=1))
    middle = jnp.concatenate(middle, axis=0)

    def second(x, table):
        high, low = split(x)
        return dot(high, table[0]) + dot(low, table[0]) + dot(high, table[1])

    spectrum = second(middle, ahead_second)
    spectrum = (spectrum.reshape(pairs, RADIX, 2 * LANES) * gain[...][None]).reshape(pairs * RADIX, 2 * LANES)
    middle = second(spectrum, back_second)
    for p in range(pairs):
        real, imag = middle[p * RADIX : (p + 1) * RADIX, :LANES], middle[p * RADIX : (p + 1) * RADIX, LANES:]
        cell = jnp.concatenate([real * cos_t - imag * sin_t, imag * cos_t + real * sin_t], axis=0)
        high, low = split(cell)
        turned = dot(back_first[...], jnp.concatenate([high, low, high], axis=0))
        for q in range(8):
            out[q, 2 * p] = turned[q * 8 : q * 8 + 8]
            out[q, 2 * p + 1] = turned[RADIX + q * 8 : RADIX + q * 8 + 8]


def filter_cycles(grid, gain, first, blocks):
    tables = dft_tables()
    step = 16
    begin = first // step
    whole = [
        pl.BlockSpec(t.shape, functools.partial(lambda nd, i: (0,) * nd, t.ndim)) for t in tables + (gain,)
    ]
    return pl.pallas_call(
        filter_kernel,
        grid=(blocks // step,),
        in_specs=whole + [pl.BlockSpec((step, 8, 8, LANES), lambda i: (begin + i, 0, 0, 0))],
        out_specs=pl.BlockSpec((8, step, 8, LANES), lambda i: (0, i, 0, 0)),
        out_shape=jax.ShapeDtypeStruct((8, blocks, 8, LANES), f32),
        compiler_params=pltpu.CompilerParams(vmem_limit_bytes=VMEM_LIMIT),
        cost_estimate=pl.CostEstimate(
            flops=blocks // 2 * 3 * 2 * 2 * (128 * 128 * 128 + 64 * 256 * 256),
            bytes_accessed=blocks * 2**16,
            transcendentals=0,
        ),
        name="filter_cycles",
    )(*[jnp.asarray(t) for t in tables], gain, grid)


def gain_table(response):
    full = jnp.concatenate([response, response[-2:0:-1]])
    gain = full.reshape(LANES, RADIX).T * (1.0 / NPHI)
    return jnp.concatenate([gain, gain], axis=1)


SLOT_CHUNKS = (16, 48)
FILTER_PARTS = 2


def row_owner_plan(values, cycle_taps, phi_taps, cycle_start, phi_start, tile_list, response):
    part_count = lax.axis_size("tile")
    rows = TR // part_count
    blocks, columns, per_column = tile_list.shape
    slots = columns * per_column
    cycle_blocks = 256
    points = [x[0] for x in (values, cycle_taps, phi_taps, cycle_start, phi_start)]
    gain = gain_table(response)

    grid, at = None, 0
    for extent in SLOT_CHUNKS:
        tiles = spread_tiles(*points, part_count, at, extent)
        tiles = tiles.reshape(rows * part_count, extent, 8, LANES)
        arrived = lax.all_to_all(tiles, ("pts", "tile"), 0, 0, tiled=True)
        grid = collect(arrived, tile_list, at // per_column, grid, cycle_blocks)
        at += extent

    part_size = cycle_blocks // FILTER_PARTS
    filtered = [filter_cycles(grid, gain, p * part_size, part_size) for p in range(FILTER_PARTS)]
    picked = pick(filtered, tile_list)
    shares = [lax.all_to_all(filtered[0], "pts", 0, 0, tiled=True)]
    picked, shares[0] = lax.optimization_barrier((picked, shares[0]))
    returned = lax.all_to_all(picked, ("pts", "tile"), 0, 0, tiled=True)
    for part in filtered[1:]:
        part, returned = lax.optimization_barrier((part, returned))
        shares.append(lax.all_to_all(part, "pts", 0, 0, tiled=True))
    gradient = read_points(*points[1:], returned.reshape(rows, part_count, slots, 8, LANES))
    whole = None
    for p, share in enumerate(shares):
        whole = merge_rows(share, p * part_size, cycle_blocks, whole)
    return whole, gradient[None]


precise = lax.Precision.HIGHEST


def contract(formula, lhs_array, rhs_array):
    return jnp.einsum(formula, lhs_array, rhs_array, precision=precise)


def spread_matrix(weights, starts, extent):
    offsets = lax.broadcasted_iota(jnp.int32, (1, 1, extent), 2) - starts[:, :, None]
    result = jnp.zeros(starts.shape + (extent,), jnp.float32)
    for tap_index in range(weights.shape[1]):
        result = result + jnp.where(offsets == tap_index, weights[:, tap_index, :, None], 0.0)
    return result


def angle_table(rows_count, cols_count, modulus):
    left_index = lax.broadcasted_iota(jnp.int32, (rows_count, cols_count), 0)
    right_index = lax.broadcasted_iota(jnp.int32, (rows_count, cols_count), 1)
    phase_int = left_index * right_index % modulus
    angles = phase_int.astype(jnp.float32) * (2.0 * math.pi / modulus)
    return (jnp.cos(angles), jnp.sin(angles))


def filter_by_einsum(cycle_rows, response):
    length = cycle_rows.shape[-1]
    second = length // RADIX
    cos_first, sin_first = angle_table(RADIX, RADIX, RADIX)
    cos_twist, sin_twist = angle_table(RADIX, second, length)
    cos_second, sin_second = angle_table(second, second, second)
    blocks = cycle_rows.reshape(cycle_rows.shape[:2] + (RADIX, second))
    real_one = contract("giab,ak->gikb", blocks, cos_first)
    imag_one = -contract("giab,ak->gikb", blocks, sin_first)
    real_two = real_one * cos_twist + imag_one * sin_twist
    imag_two = imag_one * cos_twist - real_one * sin_twist
    real_freq = contract("gikb,bm->gikm", real_two, cos_second) + contract(
        "gikb,bm->gikm", imag_two, sin_second
    )
    imag_freq = contract("gikb,bm->gikm", imag_two, cos_second) - contract(
        "gikb,bm->gikm", real_two, sin_second
    )
    full_response = jnp.concatenate([response, response[-2:0:-1]])
    gain_table = full_response.reshape(second, RADIX).T
    real_freq = real_freq * gain_table
    imag_freq = imag_freq * gain_table
    real_back = contract("gikm,bm->gikb", real_freq, cos_second) - contract(
        "gikm,bm->gikb", imag_freq, sin_second
    )
    imag_back = contract("gikm,bm->gikb", imag_freq, cos_second) + contract(
        "gikm,bm->gikb", real_freq, sin_second
    )
    real_turn = real_back * cos_twist - imag_back * sin_twist
    imag_turn = imag_back * cos_twist + real_back * sin_twist
    spatial = contract("gikb,ka->giab", real_turn, cos_first) - contract(
        "gikb,ka->giab", imag_turn, sin_first
    )
    return (spatial / length).reshape(cycle_rows.shape)


def accumulate(arrived, wanted, cycle_blocks):
    selector = (
        lax.broadcasted_iota(jnp.int32, (cycle_blocks, wanted.size), 0) == wanted.reshape(1, -1)
    ).astype(jnp.float32)
    flattened = arrived.reshape(wanted.size, -1)
    return jnp.dot(selector, flattened, precision=precise).reshape(
        (cycle_blocks,) + arrived.shape[2:]
    )


def column_owner_plan(values, cycle_taps, phi_taps, cycle_start, phi_start, tile_list, response):
    columns = lax.axis_size("pts")
    part_count = lax.axis_size("tile")
    column = lax.axis_index("pts")
    per_column = values.shape[1] // columns
    tile_width = NPHI // columns
    cycle_part = TR // part_count
    cycle_weights = spread_matrix(cycle_taps[0], cycle_start[0], TR)
    phi_weights = spread_matrix(phi_taps[0], phi_start[0], tile_width)
    loaded = cycle_weights * values[0][:, :, None]
    cycle_split = cycle_weights.reshape(columns, per_column, values.shape[2], part_count, cycle_part)
    loaded_split = loaded.reshape(columns, per_column, values.shape[2], part_count, cycle_part)
    phi_split = phi_weights.reshape(columns, per_column, values.shape[2], tile_width)
    partial_value = contract("qkitr,qkic->qtkrc", loaded_split, phi_split)
    partial_value = partial_value.reshape(columns * part_count, per_column, cycle_part, tile_width)
    arrived = lax.all_to_all(
        partial_value, ("pts", "tile"), split_axis=0, concat_axis=0, tiled=True
    )
    wanted = lax.dynamic_index_in_dim(tile_list, column, 1, keepdims=False)
    owned_tiles = accumulate(arrived, wanted, 256)
    whole_cycles = filter_by_einsum(
        lax.all_to_all(owned_tiles, "pts", split_axis=0, concat_axis=2, tiled=True), response
    )
    filtered = lax.all_to_all(whole_cycles, "pts", split_axis=2, concat_axis=0, tiled=True)
    picked = jnp.take(filtered, wanted.reshape(-1), axis=0)
    picked = picked.reshape(columns * part_count, per_column, cycle_part, tile_width)
    returned = lax.all_to_all(picked, ("pts", "tile"), split_axis=0, concat_axis=0, tiled=True)
    returned = returned.reshape(columns, part_count, per_column, cycle_part, tile_width)
    rows_read = contract("qkitr,qtkrc->qkic", cycle_split, returned)
    gradient = jnp.sum(rows_read * phi_split, axis=-1).reshape(values.shape[1], values.shape[2])
    return (filtered, gradient[None])


def solution(mesh):
    columns, part_count = mesh.shape["pts"], mesh.shape["tile"]
    rows_fit = columns * part_count == TR and NPHI // columns == GROUPS * LANES
    return jax.shard_map(
        row_owner_plan if rows_fit else column_owner_plan,
        mesh=mesh,
        in_specs=(
            P(("pts", "tile"), None, None),
            P(("pts", "tile"), None, None, None),
            P(("pts", "tile"), None, None, None),
            P(("pts", "tile"), None, None),
            P(("pts", "tile"), None, None),
            P(),
            P(),
        ),
        out_specs=(P(None, "tile", "pts"), P(("pts", "tile"), None, None)),
        check_vma=False,
    )
```

```python
import functools
import math

import jax
import jax.numpy as jnp
import numpy as np
from jax import lax
from jax.experimental import pallas as pl
from jax.experimental.pallas import tpu as pltpu
from jax.sharding import Mesh
from jax.sharding import PartitionSpec as P

NPHI = 8192
TR = 32
TAPS = 8
LANES = 128
GROUPS = 8
RADIX = 64
STEP_SLOTS = 8
VMEM_LIMIT = 50 * 1024 * 1024

f32 = jnp.float32
bf16 = jnp.bfloat16


def split(x):
    high = x.astype(bf16)
    low = (x - high.astype(f32)).astype(bf16)
    return high, low


def split_f32(x):
    high = x.astype(bf16).astype(f32)
    return high, x - high


def shifted_window(taps, shift):
    n = taps.shape[1]
    window = jnp.concatenate([taps, jnp.zeros((8, n), f32)], axis=0)
    both = jnp.concatenate([shift, shift], axis=0)
    for bit in (1, 2, 4):
        moved = pltpu.roll(window, bit, 0)
        window = jnp.where((both & bit) != 0, moved, window)
    return window[:8], window[8:]


def twice(x):
    return jnp.concatenate([x, x], axis=0)


def cycle_factor(taps, cycle_start, phi_start):
    first, second = shifted_window(taps, cycle_start & 7)
    block = cycle_start >> 3
    rows = []
    for h in range(TR // 8):
        rows.append(jnp.where(block == h, first, jnp.where(block == h - 1, second, 0.0)))
    group = twice((phi_start >> 7).astype(f32)).astype(bf16)
    masks = [group == g for g in range(GROUPS)]
    zero = jnp.zeros(group.shape, bf16)
    parts = []
    for part in split(jnp.concatenate(rows, axis=0)):
        pieces = []
        for mask in masks:
            pieces += [jnp.where(mask, part[at : at + 16], zero) for at in range(0, TR, 16)]
        parts.append(jnp.concatenate(pieces, axis=0))
    return parts


def phi_factor(taps, phi_start):
    first, second = shifted_window(taps, phi_start & 7)
    odd = (phi_start & 8) != 0
    zero = jnp.zeros(first.shape, f32)
    near = jnp.concatenate([jnp.where(odd, zero, first), jnp.where(odd, first, second)], axis=0)
    far = jnp.concatenate([jnp.where(odd, second, zero), zero], axis=0)
    block = twice(((phi_start & 127) >> 4).astype(f32)).astype(bf16)
    masks = [block == h for h in range(8)]
    zero = jnp.zeros(block.shape, bf16)
    parts = []
    for low, high in zip(split(near), split(far)):
        pieces = [jnp.where(masks[0], low, zero)]
        for h in range(1, 8):
            pieces.append(jnp.where(masks[h], low, jnp.where(masks[h - 1], high, zero)))
        pieces.append(jnp.where(masks[7], high, zero))
        parts.append(jnp.concatenate(pieces, axis=0))
    return parts


def spread_kernel(values, cycle_taps, phi_taps, cycle_start, phi_start, out, turn):
    n = values.shape[1]
    shares, parts, rows = out.shape[:3]
    for k in range(STEP_SLOTS):
        cycle_at = jnp.broadcast_to(cycle_start[k : k + 1, :], (8, n))
        phi_at = jnp.broadcast_to(phi_start[k : k + 1, :], (8, n))
        loaded = cycle_taps[k] * values[k : k + 1, :]
        left_high, left_low = cycle_factor(loaded, cycle_at, phi_at)
        empty = jnp.zeros((256 - 144, n), bf16)
        right_high, right_low = [jnp.concatenate([x, empty], axis=0) for x in phi_factor(phi_taps[k], phi_at)]
        left = jnp.concatenate([left_high, left_high, left_low], axis=1)
        right = jnp.concatenate([right_high, right_low, right_high], axis=1)
        product = lax.dot_general(left, right, (((1,), (1,)), ((), ())), preferred_element_type=f32)
        for g in range(GROUPS):
            tile = product[g * TR : (g + 1) * TR, :LANES]
            if g:
                tile = tile + product[(g - 1) * TR : g * TR, LANES:]
            for at in range(0, TR, 8):
                turn[k, pl.ds(at * GROUPS + g, 8, stride=GROUPS), :] = tile[at : at + 8]
        for r in range(TR):
            t, p, row = r // (shares * rows), r // rows % shares, r % rows
            out[p, t, row, k] = turn[k, r * GROUPS : (r + 1) * GROUPS, :]


def point_specs(place, n):
    flat = pl.BlockSpec((STEP_SLOTS, n), lambda *at: (place(*at), 0))
    taps = pl.BlockSpec((STEP_SLOTS, TAPS, n), lambda *at: (place(*at), 0, 0))
    return [flat, taps, taps, flat, flat]


def spread_tiles(points, shares, part_count, first, slots):
    n = points[0].shape[1]
    begin = first // STEP_SLOTS
    heads = (shares, part_count, TR // (shares * part_count))
    return pl.pallas_call(
        spread_kernel,
        grid=(slots // STEP_SLOTS,),
        in_specs=point_specs(lambda i: begin + i, n),
        out_specs=pl.BlockSpec(heads + (STEP_SLOTS, 8, LANES), lambda i: (0, 0, 0, i, 0, 0)),
        out_shape=jax.ShapeDtypeStruct(heads + (slots, 8, LANES), f32),
        scratch_shapes=[pltpu.VMEM((STEP_SLOTS, TR * GROUPS, LANES), f32)],
        compiler_params=pltpu.CompilerParams(vmem_limit_bytes=VMEM_LIMIT),
        cost_estimate=pl.CostEstimate(
            flops=slots * 2 * 3 * 256 * 256 * n, bytes_accessed=slots * (19 + 32) * n * 4, transcendentals=0
        ),
        name="spread",
    )(*points)


def read_kernel(row_of, begin, cycle_taps, phi_taps, cycle_start, phi_start, tiles, *rest):
    out, turn = rest[-2:]
    n = cycle_start.shape[1]
    for k in range(STEP_SLOTS):
        cycle_at = jnp.broadcast_to(cycle_start[k : k + 1, :], (8, n))
        phi_at = jnp.broadcast_to(phi_start[k : k + 1, :], (8, n))
        right_high, right_low = cycle_factor(cycle_taps[k], cycle_at, phi_at)
        for r in range(TR):
            turn[k, r * GROUPS : (r + 1) * GROUPS, :] = tiles[row_of(r, k)]
        pieces = [
            turn[k, pl.ds(at * GROUPS + g, 8, stride=GROUPS), :] for g in range(GROUPS) for at in range(0, TR, 8)
        ]
        tile = jnp.concatenate(pieces, axis=0).T
        following = pltpu.roll(tile[:16], TR * (GROUPS - 1), 1)
        left_high, left_low = split(jnp.concatenate([tile, following], axis=0))
        left = jnp.concatenate([left_high, left_low, left_high], axis=1)
        right = jnp.concatenate([right_high, right_high, right_low], axis=0)
        picked = dot(left, right)
        lane = phi_at & 127
        first, second = shifted_window(phi_taps[k], lane & 7)
        block = lane >> 3
        low = picked[:8]
        high = picked[8:16]
        for h in range(1, 16):
            here = block == h
            low = jnp.where(here, picked[h * 8 : h * 8 + 8], low)
            high = jnp.where(here, picked[h * 8 + 8 : h * 8 + 16], high)
        out[k : k + 1, :] = jnp.sum(low * first + high * second, axis=0, keepdims=True)


def read_points(points, begin, slots, tiles, tile_spec, row_of, so_far):
    total, n = points[0].shape
    given = [] if so_far is None else [so_far]
    return pl.pallas_call(
        functools.partial(read_kernel, row_of),
        grid_spec=pltpu.PrefetchScalarGridSpec(
            num_scalar_prefetch=1,
            grid=(slots // STEP_SLOTS,),
            in_specs=point_specs(lambda i, at: at[0] + i, n)[1:]
            + [tile_spec]
            + [pl.BlockSpec(memory_space=pl.ANY)] * len(given),
            out_specs=pl.BlockSpec((STEP_SLOTS, n), lambda i, at: (at[0] + i, 0)),
            scratch_shapes=[pltpu.VMEM((STEP_SLOTS, TR * GROUPS, LANES), f32)],
        ),
        out_shape=jax.ShapeDtypeStruct((total, n), f32),
        input_output_aliases={6: 0} if given else {},
        compiler_params=pltpu.CompilerParams(vmem_limit_bytes=VMEM_LIMIT),
        cost_estimate=pl.CostEstimate(
            flops=slots * 2 * 3 * 256 * 256 * n, bytes_accessed=slots * (19 + 32) * n * 4, transcendentals=0
        ),
        name="read_back",
    )(begin // STEP_SLOTS, *points[1:], tiles, *given)


def pick_far_kernel(tile_list, *refs):
    filtered, out = refs[:-1], refs[-1]
    step = pl.program_id(0)
    blocks, columns, per_column = tile_list.shape
    first = filtered[0].shape[1]

    def one(d, carry):
        block = step * out.shape[0] + d
        other = (1 - block // (blocks // 2)) * (columns // 2)
        for c in range(columns // 2):
            for k in range(per_column):
                j = tile_list[block, other + c, k]
                early = filtered[0][other + c, jnp.minimum(j, first - 1)]
                late = filtered[1][other + c, jnp.maximum(j - first, 0)]
                out[d, c * per_column + k] = jnp.where(j < first, early, late)
        return carry

    lax.fori_loop(0, out.shape[0], one, 0)


def pick_far(filtered, tile_list):
    blocks, columns, per_column = tile_list.shape
    shape = (blocks, columns // 2 * per_column, 8, LANES)
    step = 4
    return pl.pallas_call(
        pick_far_kernel,
        grid=(blocks // step,),
        in_specs=[pl.BlockSpec(memory_space=pltpu.SMEM)]
        + [pl.BlockSpec(part.shape, lambda i: (0, 0, 0, 0)) for part in filtered],
        out_specs=pl.BlockSpec((step,) + shape[1:], lambda i: (i, 0, 0, 0)),
        out_shape=jax.ShapeDtypeStruct(shape, f32),
        compiler_params=pltpu.CompilerParams(vmem_limit_bytes=VMEM_LIMIT),
        cost_estimate=pl.CostEstimate(flops=0, bytes_accessed=12 * 2**20, transcendentals=0),
        name="pick_far",
    )(tile_list, *filtered)


def pick_near_kernel(place, tile_list, *refs):
    shares, out = refs[:-1], refs[-1]
    step = pl.program_id(0)
    per_column = tile_list.shape[2]
    rows, first = shares[0].shape[:2]

    def one(d, carry):
        block = place[0] + step * out.shape[0] + d
        for k in range(per_column):
            j = tile_list[block, place[1], k]
            for row in range(rows):
                early = shares[0][row, jnp.minimum(j, first - 1)]
                late = shares[1][row, jnp.maximum(j - first, 0)]
                out[d, k, row] = jnp.where(j < first, early, late)
        return carry

    lax.fori_loop(0, out.shape[0], one, 0)


def pick_near(shares, place, tile_list):
    blocks, columns, per_column = tile_list.shape
    shape = (blocks // 2, per_column, shares[0].shape[0], 8, LANES)
    step = 4
    return pl.pallas_call(
        pick_near_kernel,
        grid=(shape[0] // step,),
        in_specs=[pl.BlockSpec(memory_space=pltpu.SMEM)] * 2
        + [pl.BlockSpec(part.shape, lambda i: (0, 0, 0, 0)) for part in shares],
        out_specs=pl.BlockSpec((step,) + shape[1:], lambda i: (i, 0, 0, 0, 0)),
        out_shape=jax.ShapeDtypeStruct(shape, f32),
        compiler_params=pltpu.CompilerParams(vmem_limit_bytes=VMEM_LIMIT),
        cost_estimate=pl.CostEstimate(flops=0, bytes_accessed=12 * 2**20, transcendentals=0),
        name="pick_near",
    )(place, tile_list, *shares)


def merge_kernel(arrived, *rest):
    out = rest[-1]
    rows, blocks = arrived.shape[:2]
    for c in range(8):
        for j in range(blocks):
            out[j, :, c * LANES : (c + 1) * LANES] = arrived[:, j, c, :]


def merge_rows(arrived, first, cycle_blocks, so_far):
    rows, blocks = arrived.shape[:2]
    step = 32
    begin = first // step
    given = [] if so_far is None else [so_far]
    return pl.pallas_call(
        merge_kernel,
        grid=(blocks // step,),
        in_specs=[pl.BlockSpec((rows, step, 8, LANES), lambda i: (0, i, 0, 0))]
        + [pl.BlockSpec(memory_space=pl.ANY)] * len(given),
        out_specs=pl.BlockSpec((step, rows, 8 * LANES), lambda i: (begin + i, 0, 0)),
        out_shape=jax.ShapeDtypeStruct((cycle_blocks, rows, 8 * LANES), f32),
        input_output_aliases={1: 0} if given else {},
        compiler_params=pltpu.CompilerParams(vmem_limit_bytes=VMEM_LIMIT),
        cost_estimate=pl.CostEstimate(flops=0, bytes_accessed=8 * blocks * rows * 1024, transcendentals=0),
        name="merge_rows",
    )(arrived, *given)


@functools.cache
def dft_tables():
    a = np.arange(RADIX)
    b = np.arange(LANES)
    first = 2.0 * np.pi / RADIX * (np.outer(a, a) % RADIX)
    twist = 2.0 * np.pi / NPHI * np.outer(a, b)
    second = 2.0 * np.pi / LANES * (np.outer(b, b) % LANES)
    c1, s1, c2, s2 = np.cos(first), np.sin(first), np.cos(second), np.sin(second)
    ahead_first = np.block([[c1, s1], [-s1, c1]])
    back_first = np.block([[c1, -s1], [s1, c1]])
    ahead_second = np.block([[c2, -s2], [s2, c2]])
    back_second = np.block([[c2, s2], [-s2, c2]])

    def pair(table):
        high = np.asarray(table, np.float32).astype(bf16)
        low = (table - high.astype(np.float64)).astype(np.float32).astype(bf16)
        return high, low

    def wide(table):
        high, low = pair(table)
        return np.concatenate([high, high, low], axis=1)

    def stacked(table):
        high, low = pair(table)
        return np.concatenate([high, high, low], axis=0)

    return (
        wide(ahead_first),
        wide(back_first),
        stacked(ahead_second),
        stacked(back_second),
        np.cos(twist).astype(np.float32),
        np.sin(twist).astype(np.float32),
    )


def dot(lhs, rhs):
    return lax.dot_general(lhs, rhs, (((1,), (0,)), ((), ())), preferred_element_type=f32)


def first_dots(table, cells):
    turned = []
    for at in range(0, len(cells), 2):
        high, low = split(jnp.concatenate(cells[at : at + 2], axis=1))
        both = dot(table, jnp.concatenate([high, low, high], axis=0))
        turned += [both[:, :LANES], both[:, LANES:]]
    return turned


def filter_block(tables, cells):
    ahead_first, back_first, ahead_second, back_second, cos_twist, sin_twist, gain = tables
    count = len(cells)
    cos_t, sin_t = cos_twist[...], sin_twist[...]
    middle = []
    for turned in first_dots(ahead_first[...], cells):
        real, imag = turned[:RADIX], turned[RADIX:]
        middle.append(jnp.concatenate([real * cos_t + imag * sin_t, imag * cos_t - real * sin_t], axis=1))
    middle = jnp.concatenate(middle, axis=0)

    def second(x, table):
        high, low = split(x)
        return dot(jnp.concatenate([high, low, high], axis=1), table[...])

    spectrum = second(middle, ahead_second)
    spectrum = (spectrum.reshape(count, RADIX, 2 * LANES) * gain[...][None]).reshape(count * RADIX, 2 * LANES)
    middle = second(spectrum, back_second)
    cells = []
    for c in range(count):
        real, imag = middle[c * RADIX : (c + 1) * RADIX, :LANES], middle[c * RADIX : (c + 1) * RADIX, LANES:]
        cells.append(jnp.concatenate([real * cos_t - imag * sin_t, imag * cos_t + real * sin_t], axis=0))
    return first_dots(back_first[...], cells)


FILTER_STEP = 32


def filter_into(tables, grid, first, out):
    cells = [grid[first + j].reshape(RADIX, LANES) for j in range(FILTER_STEP)]
    cells = [jnp.concatenate(cells[j : j + 2], axis=0) for j in range(0, FILTER_STEP, 2)]
    for p, turned in enumerate(filter_block(tables, cells)):
        for part in range(2):
            for c in range(8):
                at = part * RADIX + c * 8
                out[c, 2 * p + part] = turned[at : at + 8]


def filter_kernel(*refs):
    filter_into(refs[:7], refs[7], 0, refs[8])


def whole_specs(arrays):
    return [pl.BlockSpec(x.shape, functools.partial(lambda nd, i: (0,) * nd, x.ndim)) for x in arrays]


def filter_cost(blocks):
    return pl.CostEstimate(
        flops=blocks * 3 * 2 * (128 * 128 * 128 + 64 * 256 * 256), bytes_accessed=blocks * 2**16, transcendentals=0
    )


def filter_cycles(grid, tables):
    blocks, columns = grid.shape[:2]
    return pl.pallas_call(
        filter_kernel,
        grid=(blocks // FILTER_STEP,),
        in_specs=whole_specs(tables) + [pl.BlockSpec((FILTER_STEP, columns, 8, LANES), lambda i: (i, 0, 0, 0))],
        out_specs=pl.BlockSpec((columns, FILTER_STEP, 8, LANES), lambda i: (0, i, 0, 0)),
        out_shape=jax.ShapeDtypeStruct((columns, blocks, 8, LANES), f32),
        compiler_params=pltpu.CompilerParams(vmem_limit_bytes=VMEM_LIMIT),
        cost_estimate=filter_cost(blocks),
        name="filter_cycles",
    )(*tables, grid)


COLLECT_STEP = 4


def collect_kernel(chunks, tile_list, *refs):
    arrived, rest = refs[: len(chunks)], refs[len(chunks) :]
    tables, (out, others, total, sem) = rest[:7], rest[7:]
    step = pl.program_id(0)
    per_column = tile_list.shape[2]
    cycle_blocks = total.shape[0]
    collecting = tile_list.shape[0] // COLLECT_STEP
    first = cycle_blocks - others.shape[0]

    @pl.when(step == 0)
    def _():
        def clear(j, carry):
            total[j] = jnp.zeros(total.shape[1:], f32)
            return carry

        lax.fori_loop(0, cycle_blocks, clear, 0, unroll=8)

    @pl.when(step < collecting)
    def _():
        for d in range(COLLECT_STEP):
            for ref, begin in zip(arrived, chunks):
                for c in range(ref.shape[1] // per_column):
                    q = begin // per_column + c
                    owners = [tile_list[step * COLLECT_STEP + d, q, k] for k in range(per_column)]
                    sums = [total[owners[k], q] + ref[d, c * per_column + k] for k in range(per_column)]
                    for k in range(per_column):
                        total[owners[k], q] = sums[k]

    hand_over = pltpu.make_async_copy(total.at[pl.ds(first, others.shape[0])], others, sem)

    @pl.when(step >= collecting)
    def _():
        @pl.when(step == collecting)
        def _():
            hand_over.start()

        filter_into(tables, total, (step - collecting) * FILTER_STEP, out)

        @pl.when(step == pl.num_programs(0) - 1)
        def _():
            hand_over.wait()


def collect_and_filter(arrived, chunks, tile_list, tables, cycle_blocks, part):
    blocks, columns, per_column = tile_list.shape
    collecting = blocks // COLLECT_STEP
    steps = part // FILTER_STEP
    return pl.pallas_call(
        functools.partial(collect_kernel, chunks),
        grid=(collecting + steps,),
        in_specs=[pl.BlockSpec(memory_space=pltpu.SMEM)]
        + [
            pl.BlockSpec((COLLECT_STEP,) + x.shape[1:], lambda i: (jnp.minimum(i, collecting - 1), 0, 0, 0))
            for x in arrived
        ]
        + whole_specs(tables),
        out_specs=[
            pl.BlockSpec((columns, FILTER_STEP, 8, LANES), lambda i: (0, jnp.maximum(i - collecting, 0), 0, 0)),
            pl.BlockSpec(memory_space=pl.ANY),
        ],
        out_shape=[
            jax.ShapeDtypeStruct((columns, part, 8, LANES), f32),
            jax.ShapeDtypeStruct((cycle_blocks - part, columns, 8, LANES), f32),
        ],
        scratch_shapes=[pltpu.VMEM((cycle_blocks, columns, 8, LANES), f32), pltpu.SemaphoreType.DMA],
        compiler_params=pltpu.CompilerParams(vmem_limit_bytes=VMEM_LIMIT),
        cost_estimate=filter_cost(part + 64),
        name="collect_filter",
    )(tile_list, *arrived, *tables)


def gain_table(response):
    full = jnp.concatenate([response, response[-2:0:-1]])
    gain = full.reshape(LANES, RADIX).T * (1.0 / NPHI)
    return jnp.concatenate([gain, gain], axis=1)


SLOT_CHUNKS = (8, 56)
FILTER_FIRST = 64
AXES = ("half", "share", "tile")


def after(x, *others):
    return lax.optimization_barrier((x, *others))[0]


def row_owner_plan(values, cycle_taps, phi_taps, cycle_start, phi_start, tile_list, response):
    half, share = lax.axis_index("half"), lax.axis_index("share")
    shares, part_count = lax.axis_size("share"), lax.axis_size("tile")
    blocks, columns, per_column = tile_list.shape
    near_slots = shares * per_column
    cycle_blocks = 256
    points = [x[0] for x in (values, cycle_taps, phi_taps, cycle_start, phi_start)]
    tables = [jnp.asarray(t) for t in dft_tables()] + [gain_table(response)]
    place = jnp.stack([half * (blocks // 2), half * shares + share]).astype(jnp.int32)

    def exchange(x, axes):
        return lax.all_to_all(x, axes, 0, 0, tiled=True)

    arrived, begins, at = [], [], 0
    for extent in SLOT_CHUNKS:
        tiles = spread_tiles(points, columns, part_count, at, extent)
        arrived.append(exchange(tiles.reshape(blocks, extent, 8, LANES), AXES))
        begins.append(at)
        at += extent
    early, others = collect_and_filter(arrived, begins, tile_list, tables, cycle_blocks, FILTER_FIRST)
    late = filter_cycles(others, tables)

    early_share = exchange(early, AXES[:2])
    far = pick_far([early, late], tile_list)
    late_share = exchange(after(late, early_share), AXES[:2])
    far_tiles = exchange(after(far, late_share), AXES)
    near = pick_near([early_share, late_share], place, tile_list)
    near_tiles = exchange(after(near, far_tiles), AXES[1:])

    far_tiles = far_tiles.reshape(columns, part_count, near_slots, 8, LANES)
    far_spec = pl.BlockSpec((columns, part_count, STEP_SLOTS, 8, LANES), lambda i, at: (0, 0, i, 0, 0))
    far_begin = ((1 - half) * near_slots).astype(jnp.int32).reshape(1)
    gradient = read_points(
        points, far_begin, near_slots, far_tiles, far_spec, lambda r, k: (r % columns, r // columns, k), None
    )
    near_tiles = near_tiles.reshape(shares, part_count, per_column, columns, 8, LANES)
    near_spec = pl.BlockSpec((None,) + near_tiles.shape[1:], lambda i, at: (i, 0, 0, 0, 0, 0))
    near_begin = (half * near_slots).astype(jnp.int32).reshape(1)
    gradient = read_points(
        points, near_begin, near_slots, near_tiles, near_spec, lambda r, k: (r // columns, k, r % columns), gradient
    )
    whole = merge_rows(early_share, 0, cycle_blocks, None)
    whole = merge_rows(late_share, FILTER_FIRST, cycle_blocks, whole)
    return whole, gradient[None]


precise = lax.Precision.HIGHEST


def contract(formula, lhs_array, rhs_array):
    return jnp.einsum(formula, lhs_array, rhs_array, precision=precise)


def spread_matrix(weights, starts, extent):
    offsets = lax.broadcasted_iota(jnp.int32, (1, 1, extent), 2) - starts[:, :, None]
    result = jnp.zeros(starts.shape + (extent,), jnp.float32)
    for tap_index in range(weights.shape[1]):
        result = result + jnp.where(offsets == tap_index, weights[:, tap_index, :, None], 0.0)
    return result


def angle_table(rows_count, cols_count, modulus):
    left_index = lax.broadcasted_iota(jnp.int32, (rows_count, cols_count), 0)
    right_index = lax.broadcasted_iota(jnp.int32, (rows_count, cols_count), 1)
    phase_int = left_index * right_index % modulus
    angles = phase_int.astype(jnp.float32) * (2.0 * math.pi / modulus)
    return (jnp.cos(angles), jnp.sin(angles))


def filter_by_einsum(cycle_rows, response):
    length = cycle_rows.shape[-1]
    second = length // RADIX
    cos_first, sin_first = angle_table(RADIX, RADIX, RADIX)
    cos_twist, sin_twist = angle_table(RADIX, second, length)
    cos_second, sin_second = angle_table(second, second, second)
    blocks = cycle_rows.reshape(cycle_rows.shape[:2] + (RADIX, second))
    real_one = contract("giab,ak->gikb", blocks, cos_first)
    imag_one = -contract("giab,ak->gikb", blocks, sin_first)
    real_two = real_one * cos_twist + imag_one * sin_twist
    imag_two = imag_one * cos_twist - real_one * sin_twist
    real_freq = contract("gikb,bm->gikm", real_two, cos_second) + contract(
        "gikb,bm->gikm", imag_two, sin_second
    )
    imag_freq = contract("gikb,bm->gikm", imag_two, cos_second) - contract(
        "gikb,bm->gikm", real_two, sin_second
    )
    full_response = jnp.concatenate([response, response[-2:0:-1]])
    gain_table = full_response.reshape(second, RADIX).T
    real_freq = real_freq * gain_table
    imag_freq = imag_freq * gain_table
    real_back = contract("gikm,bm->gikb", real_freq, cos_second) - contract(
        "gikm,bm->gikb", imag_freq, sin_second
    )
    imag_back = contract("gikm,bm->gikb", imag_freq, cos_second) + contract(
        "gikm,bm->gikb", real_freq, sin_second
    )
    real_turn = real_back * cos_twist - imag_back * sin_twist
    imag_turn = imag_back * cos_twist + real_back * sin_twist
    spatial = contract("gikb,ka->giab", real_turn, cos_first) - contract(
        "gikb,ka->giab", imag_turn, sin_first
    )
    return (spatial / length).reshape(cycle_rows.shape)


def accumulate(arrived, wanted, cycle_blocks):
    selector = (
        lax.broadcasted_iota(jnp.int32, (cycle_blocks, wanted.size), 0) == wanted.reshape(1, -1)
    ).astype(jnp.float32)
    flattened = arrived.reshape(wanted.size, -1)
    return jnp.dot(selector, flattened, precision=precise).reshape(
        (cycle_blocks,) + arrived.shape[2:]
    )


def column_owner_plan(values, cycle_taps, phi_taps, cycle_start, phi_start, tile_list, response):
    columns = lax.axis_size("pts")
    part_count = lax.axis_size("tile")
    column = lax.axis_index("pts")
    per_column = values.shape[1] // columns
    tile_width = NPHI // columns
    cycle_part = TR // part_count
    cycle_weights = spread_matrix(cycle_taps[0], cycle_start[0], TR)
    phi_weights = spread_matrix(phi_taps[0], phi_start[0], tile_width)
    loaded = cycle_weights * values[0][:, :, None]
    cycle_split = cycle_weights.reshape(columns, per_column, values.shape[2], part_count, cycle_part)
    loaded_split = loaded.reshape(columns, per_column, values.shape[2], part_count, cycle_part)
    phi_split = phi_weights.reshape(columns, per_column, values.shape[2], tile_width)
    partial_value = contract("qkitr,qkic->qtkrc", loaded_split, phi_split)
    partial_value = partial_value.reshape(columns * part_count, per_column, cycle_part, tile_width)
    arrived = lax.all_to_all(
        partial_value, ("pts", "tile"), split_axis=0, concat_axis=0, tiled=True
    )
    wanted = lax.dynamic_index_in_dim(tile_list, column, 1, keepdims=False)
    owned_tiles = accumulate(arrived, wanted, 256)
    whole_cycles = filter_by_einsum(
        lax.all_to_all(owned_tiles, "pts", split_axis=0, concat_axis=2, tiled=True), response
    )
    filtered = lax.all_to_all(whole_cycles, "pts", split_axis=2, concat_axis=0, tiled=True)
    picked = jnp.take(filtered, wanted.reshape(-1), axis=0)
    picked = picked.reshape(columns * part_count, per_column, cycle_part, tile_width)
    returned = lax.all_to_all(picked, ("pts", "tile"), split_axis=0, concat_axis=0, tiled=True)
    returned = returned.reshape(columns, part_count, per_column, cycle_part, tile_width)
    rows_read = contract("qkitr,qtkrc->qkic", cycle_split, returned)
    gradient = jnp.sum(rows_read * phi_split, axis=-1).reshape(values.shape[1], values.shape[2])
    return (filtered, gradient[None])


def solution(mesh):
    columns, part_count = mesh.shape["pts"], mesh.shape["tile"]
    step, pts, tile = column_owner_plan, "pts", "tile"
    if columns * part_count == TR and columns % 2 == 0 and NPHI // columns == GROUPS * LANES:
        mesh = Mesh(mesh.devices.reshape(2, columns // 2, part_count), AXES)
        step, pts = row_owner_plan, ("half", "share")
    block = (pts, tile) if pts == "pts" else AXES
    return jax.shard_map(
        step,
        mesh=mesh,
        in_specs=(
            P(block, None, None),
            P(block, None, None, None),
            P(block, None, None, None),
            P(block, None, None),
            P(block, None, None),
            P(),
            P(),
        ),
        out_specs=(P(None, tile, pts), P(block, None, None)),
        check_vma=False,
    )
```

```python
import functools
import math

import jax
import jax.numpy as jnp
import numpy as np
from jax import lax
from jax.experimental import pallas as pl
from jax.experimental.pallas import tpu as pltpu
from jax.sharding import Mesh
from jax.sharding import PartitionSpec as P

NPHI = 8192
TR = 32
TAPS = 8
LANES = 128
GROUPS = 8
RADIX = 64
STEP_SLOTS = 8
VMEM_LIMIT = 60 * 1024 * 1024

f32 = jnp.float32
bf16 = jnp.bfloat16


def split(x):
    high = x.astype(bf16)
    low = (x - high.astype(f32)).astype(bf16)
    return high, low


def split_f32(x):
    high = x.astype(bf16).astype(f32)
    return high, x - high


def shifted_window(taps, shift):
    n = taps.shape[1]
    window = jnp.concatenate([taps, jnp.zeros((8, n), f32)], axis=0)
    both = jnp.concatenate([shift, shift], axis=0)
    for bit in (1, 2, 4):
        moved = pltpu.roll(window, bit, 0)
        window = jnp.where((both & bit) != 0, moved, window)
    return window[:8], window[8:]


def twice(x):
    return jnp.concatenate([x, x], axis=0)


def cycle_factor(taps, cycle_start, phi_start):
    first, second = shifted_window(taps, cycle_start & 7)
    block = cycle_start >> 3
    rows = []
    for h in range(TR // 8):
        rows.append(jnp.where(block == h, first, jnp.where(block == h - 1, second, 0.0)))
    group = twice((phi_start >> 7).astype(f32)).astype(bf16)
    masks = [group == g for g in range(GROUPS)]
    zero = jnp.zeros(group.shape, bf16)
    parts = []
    for part in split(jnp.concatenate(rows, axis=0)):
        pieces = []
        for mask in masks:
            pieces += [jnp.where(mask, part[at : at + 16], zero) for at in range(0, TR, 16)]
        parts.append(jnp.concatenate(pieces, axis=0))
    return parts


def phi_factor(taps, phi_start):
    first, second = shifted_window(taps, phi_start & 7)
    odd = (phi_start & 8) != 0
    zero = jnp.zeros(first.shape, f32)
    near = jnp.concatenate([jnp.where(odd, zero, first), jnp.where(odd, first, second)], axis=0)
    far = jnp.concatenate([jnp.where(odd, second, zero), zero], axis=0)
    block = twice(((phi_start & 127) >> 4).astype(f32)).astype(bf16)
    masks = [block == h for h in range(8)]
    zero = jnp.zeros(block.shape, bf16)
    parts = []
    for low, high in zip(split(near), split(far)):
        pieces = [jnp.where(masks[0], low, zero)]
        for h in range(1, 8):
            pieces.append(jnp.where(masks[h], low, jnp.where(masks[h - 1], high, zero)))
        pieces.append(jnp.where(masks[7], high, zero))
        parts.append(jnp.concatenate(pieces, axis=0))
    return parts


def spread_kernel(values, cycle_taps, phi_taps, cycle_start, phi_start, out, turn):
    n = values.shape[1]
    shares, parts, rows = out.shape[:3]
    for k in range(STEP_SLOTS):
        cycle_at = jnp.broadcast_to(cycle_start[k : k + 1, :], (8, n))
        phi_at = jnp.broadcast_to(phi_start[k : k + 1, :], (8, n))
        loaded = cycle_taps[k] * values[k : k + 1, :]
        left_high, left_low = cycle_factor(loaded, cycle_at, phi_at)
        empty = jnp.zeros((256 - 144, n), bf16)
        right_high, right_low = [jnp.concatenate([x, empty], axis=0) for x in phi_factor(phi_taps[k], phi_at)]
        left = jnp.concatenate([left_high, left_high, left_low], axis=1)
        right = jnp.concatenate([right_high, right_low, right_high], axis=1)
        product = lax.dot_general(left, right, (((1,), (1,)), ((), ())), preferred_element_type=f32)
        for g in range(GROUPS):
            tile = product[g * TR : (g + 1) * TR, :LANES]
            if g:
                tile = tile + product[(g - 1) * TR : g * TR, LANES:]
            for at in range(0, TR, 8):
                turn[k, pl.ds(at * GROUPS + g, 8, stride=GROUPS), :] = tile[at : at + 8]
        for r in range(TR):
            t, p, row = r // (shares * rows), r // rows % shares, r % rows
            out[p, t, row, k] = turn[k, r * GROUPS : (r + 1) * GROUPS, :]


def point_specs(place, n):
    flat = pl.BlockSpec((STEP_SLOTS, n), lambda *at: (place(*at), 0))
    taps = pl.BlockSpec((STEP_SLOTS, TAPS, n), lambda *at: (place(*at), 0, 0))
    return [flat, taps, taps, flat, flat]


def spread_tiles(points, shares, part_count, first, slots):
    n = points[0].shape[1]
    begin = first // STEP_SLOTS
    heads = (shares, part_count, TR // (shares * part_count))
    return pl.pallas_call(
        spread_kernel,
        grid=(slots // STEP_SLOTS,),
        in_specs=point_specs(lambda i: begin + i, n),
        out_specs=pl.BlockSpec(heads + (STEP_SLOTS, 8, LANES), lambda i: (0, 0, 0, i, 0, 0)),
        out_shape=jax.ShapeDtypeStruct(heads + (slots, 8, LANES), f32),
        scratch_shapes=[pltpu.VMEM((STEP_SLOTS, TR * GROUPS, LANES), f32)],
        compiler_params=pltpu.CompilerParams(vmem_limit_bytes=VMEM_LIMIT),
        cost_estimate=pl.CostEstimate(
            flops=slots * 2 * 3 * 256 * 256 * n, bytes_accessed=slots * (19 + 32) * n * 4, transcendentals=0
        ),
        name="spread",
    )(*points)


def read_kernel(count, place_rows, begin, cycle_taps, phi_taps, cycle_start, phi_start, *rest):
    tiles, (out, turn) = rest[:count], rest[-2:]
    n = cycle_start.shape[1]
    for k in range(STEP_SLOTS):
        cycle_at = jnp.broadcast_to(cycle_start[k : k + 1, :], (8, n))
        phi_at = jnp.broadcast_to(phi_start[k : k + 1, :], (8, n))
        right_high, right_low = cycle_factor(cycle_taps[k], cycle_at, phi_at)
        for r, row in place_rows(begin, tiles, k):
            turn[k, pl.ds(r * GROUPS, GROUPS), :] = row
        pieces = [
            turn[k, pl.ds(at * GROUPS + g, 8, stride=GROUPS), :] for g in range(GROUPS) for at in range(0, TR, 8)
        ]
        tile = jnp.concatenate(pieces, axis=0).T
        following = pltpu.roll(tile[:16], TR * (GROUPS - 1), 1)
        left_high, left_low = split(jnp.concatenate([tile, following], axis=0))
        left = jnp.concatenate([left_high, left_low, left_high], axis=1)
        right = jnp.concatenate([right_high, right_high, right_low], axis=0)
        picked = dot(left, right)
        lane = phi_at & 127
        first, second = shifted_window(phi_taps[k], lane & 7)
        block = lane >> 3
        low = picked[:8]
        high = picked[8:16]
        for h in range(1, 16):
            here = block == h
            low = jnp.where(here, picked[h * 8 : h * 8 + 8], low)
            high = jnp.where(here, picked[h * 8 + 8 : h * 8 + 16], high)
        out[k : k + 1, :] = jnp.sum(low * first + high * second, axis=0, keepdims=True)


def read_points(points, begin, slots, tiles, tile_specs, place_rows, so_far):
    total, n = points[0].shape
    given = [] if so_far is None else [so_far]
    return pl.pallas_call(
        functools.partial(read_kernel, len(tile_specs), place_rows),
        grid_spec=pltpu.PrefetchScalarGridSpec(
            num_scalar_prefetch=1,
            grid=(slots // STEP_SLOTS,),
            in_specs=point_specs(lambda i, at: at[0] + i, n)[1:]
            + tile_specs
            + [pl.BlockSpec(memory_space=pl.ANY)] * len(given),
            out_specs=pl.BlockSpec((STEP_SLOTS, n), lambda i, at: (at[0] + i, 0)),
            scratch_shapes=[pltpu.VMEM((STEP_SLOTS, TR * GROUPS, LANES), f32)],
        ),
        out_shape=jax.ShapeDtypeStruct((total, n), f32),
        input_output_aliases={5 + len(tile_specs): 0} if given else {},
        compiler_params=pltpu.CompilerParams(vmem_limit_bytes=VMEM_LIMIT),
        cost_estimate=pl.CostEstimate(
            flops=slots * 2 * 3 * 256 * 256 * n, bytes_accessed=slots * (19 + 32) * n * 4, transcendentals=0
        ),
        name="read_back",
    )(begin, *points[1:], *tiles, *given)


def pick_far_kernel(tile_list, *refs):
    filtered, out = refs[:-1], refs[-1]
    step = pl.program_id(0)
    blocks, columns, per_column = tile_list.shape
    first = filtered[0].shape[1]

    def one(d, carry):
        block = step * out.shape[0] + d
        other = (1 - block // (blocks // 2)) * (columns // 2)
        for c in range(columns // 2):
            for k in range(per_column):
                j = tile_list[block, other + c, k]
                early = filtered[0][other + c, jnp.minimum(j, first - 1)]
                late = filtered[1][other + c, jnp.maximum(j - first, 0)]
                out[d, c * per_column + k] = jnp.where(j < first, early, late)
        return carry

    lax.fori_loop(0, out.shape[0], one, 0)


def pick_far(filtered, tile_list):
    blocks, columns, per_column = tile_list.shape
    shape = (blocks, columns // 2 * per_column, 8, LANES)
    step = 4
    return pl.pallas_call(
        pick_far_kernel,
        grid=(blocks // step,),
        in_specs=[pl.BlockSpec(memory_space=pltpu.SMEM)]
        + [pl.BlockSpec(part.shape, lambda i: (0, 0, 0, 0)) for part in filtered],
        out_specs=pl.BlockSpec((step,) + shape[1:], lambda i: (i, 0, 0, 0)),
        out_shape=jax.ShapeDtypeStruct(shape, f32),
        compiler_params=pltpu.CompilerParams(vmem_limit_bytes=VMEM_LIMIT),
        cost_estimate=pl.CostEstimate(flops=0, bytes_accessed=12 * 2**20, transcendentals=0),
        name="pick_far",
    )(tile_list, *filtered)


def pick_own_kernel(place, tile_list, *refs):
    filtered, outs = refs[:2], refs[2:]
    columns, per_column = tile_list.shape[1:]
    first = filtered[0].shape[1]

    for d, out in enumerate(outs):
        block = place[0] + (place[2] ^ d)

        def one(c, carry):
            column = place[4] + c
            for k in range(per_column):
                j = tile_list[block, column, k]
                inside, beyond = jnp.minimum(j, first - 1), jnp.maximum(j - first, 0)
                out[c * per_column + k] = jnp.where(j < first, filtered[0][column, inside], filtered[1][column, beyond])
            return carry

        lax.fori_loop(0, columns // 2, one, 0)


def pick_own(filtered, place, tile_list):
    blocks, columns, per_column = tile_list.shape
    shape = (columns // 2 * per_column, 8, LANES)
    return pl.pallas_call(
        pick_own_kernel,
        grid=(1,),
        in_specs=[pl.BlockSpec(memory_space=pltpu.SMEM)] * 2
        + [pl.BlockSpec(part.shape, lambda i: (0, 0, 0, 0)) for part in filtered],
        out_specs=[pl.BlockSpec(shape, lambda i: (0, 0, 0))] * (blocks // 2),
        out_shape=[jax.ShapeDtypeStruct(shape, f32)] * (blocks // 2),
        compiler_params=pltpu.CompilerParams(vmem_limit_bytes=VMEM_LIMIT),
        cost_estimate=pl.CostEstimate(flops=0, bytes_accessed=10 * 2**20, transcendentals=0),
        name="pick_own",
    )(place, tile_list, *filtered)


def pick_near_kernel(place, tile_list, *refs):
    shares, outs = refs[:2], refs[2:]
    per_column = tile_list.shape[2]
    first = shares[0].shape[1]
    rows = outs[0].shape[1]

    for d, out in enumerate(outs):
        block = place[0] + (place[2] ^ d)

        def one(k, carry):
            j = tile_list[block, place[1], k]
            inside, beyond = jnp.minimum(j, first - 1), jnp.maximum(j - first, 0)
            for row in range(rows):
                at = place[3] + row
                out[k, row] = jnp.where(j < first, shares[0][at, inside], shares[1][at, beyond])
            return carry

        lax.fori_loop(0, per_column, one, 0)


def pick_near(shares, place, tile_list):
    blocks, columns, per_column = tile_list.shape
    shape = (per_column, shares[0].shape[0] // 2, 8, LANES)
    return pl.pallas_call(
        pick_near_kernel,
        grid=(1,),
        in_specs=[pl.BlockSpec(memory_space=pltpu.SMEM)] * 2
        + [pl.BlockSpec(part.shape, lambda i: (0, 0, 0, 0)) for part in shares],
        out_specs=[pl.BlockSpec(shape, lambda i: (0, 0, 0, 0))] * (blocks // 2),
        out_shape=[jax.ShapeDtypeStruct(shape, f32)] * (blocks // 2),
        compiler_params=pltpu.CompilerParams(vmem_limit_bytes=VMEM_LIMIT),
        cost_estimate=pl.CostEstimate(flops=0, bytes_accessed=12 * 2**20, transcendentals=0),
        name="pick_near",
    )(place, tile_list, *shares)


def merge_kernel(arrived, *rest):
    out = rest[-1]
    rows, blocks = arrived.shape[:2]
    for c in range(8):
        for j in range(blocks):
            out[j, :, c * LANES : (c + 1) * LANES] = arrived[:, j, c, :]


def merge_rows(arrived, first, cycle_blocks, so_far):
    rows, blocks = arrived.shape[:2]
    step = 32
    begin = first // step
    given = [] if so_far is None else [so_far]
    return pl.pallas_call(
        merge_kernel,
        grid=(blocks // step,),
        in_specs=[pl.BlockSpec((rows, step, 8, LANES), lambda i: (0, i, 0, 0))]
        + [pl.BlockSpec(memory_space=pl.ANY)] * len(given),
        out_specs=pl.BlockSpec((step, rows, 8 * LANES), lambda i: (begin + i, 0, 0)),
        out_shape=jax.ShapeDtypeStruct((cycle_blocks, rows, 8 * LANES), f32),
        input_output_aliases={1: 0} if given else {},
        compiler_params=pltpu.CompilerParams(vmem_limit_bytes=VMEM_LIMIT),
        cost_estimate=pl.CostEstimate(flops=0, bytes_accessed=8 * blocks * rows * 1024, transcendentals=0),
        name="merge_rows",
    )(arrived, *given)


@functools.cache
def dft_tables():
    a = np.arange(RADIX)
    b = np.arange(LANES)
    first = 2.0 * np.pi / RADIX * (np.outer(a, a) % RADIX)
    twist = 2.0 * np.pi / NPHI * np.outer(a, b)
    second = 2.0 * np.pi / LANES * (np.outer(b, b) % LANES)
    c1, s1, c2, s2 = np.cos(first), np.sin(first), np.cos(second), np.sin(second)
    ahead_first = np.block([[c1, s1], [-s1, c1]])
    back_first = np.block([[c1, -s1], [s1, c1]])
    ahead_second = np.block([[c2, -s2], [s2, c2]])
    back_second = np.block([[c2, s2], [-s2, c2]])

    def pair(table):
        high = np.asarray(table, np.float32).astype(bf16)
        low = (table - high.astype(np.float64)).astype(np.float32).astype(bf16)
        return high, low

    def wide(table):
        high, low = pair(table)
        return np.concatenate([high, high, low], axis=1)

    def stacked(table):
        high, low = pair(table)
        return np.concatenate([high, high, low], axis=0)

    return (
        wide(ahead_first),
        wide(back_first),
        stacked(ahead_second),
        stacked(back_second),
        np.cos(twist).astype(np.float32),
        np.sin(twist).astype(np.float32),
    )


def dot(lhs, rhs):
    return lax.dot_general(lhs, rhs, (((1,), (0,)), ((), ())), preferred_element_type=f32)


def first_dots(table, cells):
    turned = []
    for at in range(0, len(cells), 2):
        high, low = split(jnp.concatenate(cells[at : at + 2], axis=1))
        both = dot(table, jnp.concatenate([high, low, high], axis=0))
        turned += [both[:, :LANES], both[:, LANES:]]
    return turned


def filter_block(tables, cells):
    ahead_first, back_first, ahead_second, back_second, cos_twist, sin_twist, gain = tables
    count = len(cells)
    cos_t, sin_t = cos_twist[...], sin_twist[...]
    middle = []
    for turned in first_dots(ahead_first[...], cells):
        real, imag = turned[:RADIX], turned[RADIX:]
        middle.append(jnp.concatenate([real * cos_t + imag * sin_t, imag * cos_t - real * sin_t], axis=1))
    middle = jnp.concatenate(middle, axis=0)

    def second(x, table):
        high, low = split(x)
        return dot(jnp.concatenate([high, low, high], axis=1), table[...])

    spectrum = second(middle, ahead_second)
    spectrum = (spectrum.reshape(count, RADIX, 2 * LANES) * gain[...][None]).reshape(count * RADIX, 2 * LANES)
    middle = second(spectrum, back_second)
    cells = []
    for c in range(count):
        real, imag = middle[c * RADIX : (c + 1) * RADIX, :LANES], middle[c * RADIX : (c + 1) * RADIX, LANES:]
        cells.append(jnp.concatenate([real * cos_t - imag * sin_t, imag * cos_t + real * sin_t], axis=0))
    return first_dots(back_first[...], cells)


FILTER_STEP = 32


def filter_into(tables, grid, first, out):
    cells = [grid[first + j].reshape(RADIX, LANES) for j in range(FILTER_STEP)]
    cells = [jnp.concatenate(cells[j : j + 2], axis=0) for j in range(0, FILTER_STEP, 2)]
    for p, turned in enumerate(filter_block(tables, cells)):
        for part in range(2):
            for c in range(8):
                at = part * RADIX + c * 8
                out[c, 2 * p + part] = turned[at : at + 8]


def filter_kernel(*refs):
    filter_into(refs[:7], refs[7], 0, refs[8])


def whole_specs(arrays):
    return [pl.BlockSpec(x.shape, functools.partial(lambda nd, i: (0,) * nd, x.ndim)) for x in arrays]


def filter_cost(blocks):
    return pl.CostEstimate(
        flops=blocks * 3 * 2 * (128 * 128 * 128 + 64 * 256 * 256), bytes_accessed=blocks * 2**16, transcendentals=0
    )


def filter_cycles(grid, tables):
    blocks, columns = grid.shape[:2]
    return pl.pallas_call(
        filter_kernel,
        grid=(blocks // FILTER_STEP,),
        in_specs=whole_specs(tables) + [pl.BlockSpec((FILTER_STEP, columns, 8, LANES), lambda i: (i, 0, 0, 0))],
        out_specs=pl.BlockSpec((columns, FILTER_STEP, 8, LANES), lambda i: (0, i, 0, 0)),
        out_shape=jax.ShapeDtypeStruct((columns, blocks, 8, LANES), f32),
        compiler_params=pltpu.CompilerParams(vmem_limit_bytes=VMEM_LIMIT),
        cost_estimate=filter_cost(blocks),
        name="filter_cycles",
    )(*tables, grid)


COLLECT_STEP = 4


def collect_kernel(chunks, tile_list, *refs):
    arrived, rest = refs[: len(chunks)], refs[len(chunks) :]
    tables, (out, others, total, sem) = rest[:7], rest[7:]
    step = pl.program_id(0)
    per_column = tile_list.shape[2]
    cycle_blocks = total.shape[0]
    collecting = tile_list.shape[0] // COLLECT_STEP
    first = cycle_blocks - others.shape[0]

    @pl.when(step == 0)
    def _():
        def clear(j, carry):
            total[j] = jnp.zeros(total.shape[1:], f32)
            return carry

        lax.fori_loop(0, cycle_blocks, clear, 0, unroll=8)

    @pl.when(step < collecting)
    def _():
        for d in range(COLLECT_STEP):
            for ref, begin in zip(arrived, chunks):
                for c in range(ref.shape[1] // per_column):
                    q = begin // per_column + c
                    owners = [tile_list[step * COLLECT_STEP + d, q, k] for k in range(per_column)]
                    sums = [total[owners[k], q] + ref[d, c * per_column + k] for k in range(per_column)]
                    for k in range(per_column):
                        total[owners[k], q] = sums[k]

    hand_over = pltpu.make_async_copy(total.at[pl.ds(first, others.shape[0])], others, sem)

    @pl.when(step >= collecting)
    def _():
        @pl.when(step == collecting)
        def _():
            hand_over.start()

        filter_into(tables, total, (step - collecting) * FILTER_STEP, out)

        @pl.when(step == pl.num_programs(0) - 1)
        def _():
            hand_over.wait()


def collect_and_filter(arrived, chunks, tile_list, tables, cycle_blocks, part):
    blocks, columns, per_column = tile_list.shape
    collecting = blocks // COLLECT_STEP
    steps = part // FILTER_STEP
    return pl.pallas_call(
        functools.partial(collect_kernel, chunks),
        grid=(collecting + steps,),
        in_specs=[pl.BlockSpec(memory_space=pltpu.SMEM)]
        + [
            pl.BlockSpec((COLLECT_STEP,) + x.shape[1:], lambda i: (jnp.minimum(i, collecting - 1), 0, 0, 0))
            for x in arrived
        ]
        + whole_specs(tables),
        out_specs=[
            pl.BlockSpec((columns, FILTER_STEP, 8, LANES), lambda i: (0, jnp.maximum(i - collecting, 0), 0, 0)),
            pl.BlockSpec(memory_space=pl.ANY),
        ],
        out_shape=[
            jax.ShapeDtypeStruct((columns, part, 8, LANES), f32),
            jax.ShapeDtypeStruct((cycle_blocks - part, columns, 8, LANES), f32),
        ],
        scratch_shapes=[pltpu.VMEM((cycle_blocks, columns, 8, LANES), f32), pltpu.SemaphoreType.DMA],
        compiler_params=pltpu.CompilerParams(vmem_limit_bytes=VMEM_LIMIT),
        cost_estimate=filter_cost(part + 64),
        name="collect_filter",
    )(tile_list, *arrived, *tables)


def gain_table(response):
    full = jnp.concatenate([response, response[-2:0:-1]])
    gain = full.reshape(LANES, RADIX).T * (1.0 / NPHI)
    return jnp.concatenate([gain, gain], axis=1)


SLOT_CHUNKS = (8, 56)
FILTER_FIRST = 32
AXES = ("half", "share", "tile")


def after(x, *others):
    return lax.optimization_barrier((x, *others))[0]


def row_owner_plan(values, cycle_taps, phi_taps, cycle_start, phi_start, tile_list, response):
    half, share = lax.axis_index("half"), lax.axis_index("share")
    shares, part_count = lax.axis_size("share"), lax.axis_size("tile")
    blocks, columns, per_column = tile_list.shape
    near_slots = shares * per_column
    cycle_blocks = 256
    points = [x[0] for x in (values, cycle_taps, phi_taps, cycle_start, phi_start)]
    tables = [jnp.asarray(t) for t in dft_tables()] + [gain_table(response)]
    index = share * part_count + lax.axis_index("tile")
    place = jnp.stack(
        [half * (blocks // 2), half * shares + share, index, (1 - half) * shares, half * shares]
    ).astype(jnp.int32)

    def exchange(x, axes):
        return lax.all_to_all(x, axes, 0, 0, tiled=True)

    arrived, begins, at = [], [], 0
    for extent in SLOT_CHUNKS:
        tiles = spread_tiles(points, columns, part_count, at, extent)
        arrived.append(exchange(tiles.reshape(blocks, extent, 8, LANES), AXES))
        begins.append(at)
        at += extent
    early, others = collect_and_filter(arrived, begins, tile_list, tables, cycle_blocks, FILTER_FIRST)
    late = filter_cycles(others, tables)

    def pass_on(parts):
        moved = [parts[0]]
        for d in range(1, blocks // 2):
            moved.append(lax.ppermute(parts[d], AXES[1:], [(i, i ^ d) for i in range(blocks // 2)]))
        return moved

    early_share = exchange(early, AXES[:2])
    far = pick_far([early, late], tile_list)
    late_share = exchange(after(late, early_share), AXES[:2])
    own = pass_on(pick_own([after(early, far), late], place, tile_list))
    far_tiles = exchange(after(far, late_share, *own[1:]), AXES)
    near = pass_on(pick_near([early_share, late_share], place, tile_list))

    far_tiles = far_tiles.reshape(columns, part_count, near_slots, 8, LANES)
    far_spec = pl.BlockSpec((columns, part_count, STEP_SLOTS, 8, LANES), lambda i, at: (0, 0, i, 0, 0))

    def far_rows(begin, tiles, k):
        return [(r, tiles[0][r % columns, r // columns, k]) for r in range(TR)]

    def near_rows(begin, tiles, k):
        step = pl.program_id(0)
        for t in range(part_count):
            for p in range(shares):
                source = begin[1] ^ (p * part_count + t)
                yield t * columns + begin[0] + p, tiles[0][source, step * STEP_SLOTS + k]
                source = begin[1] ^ (step * part_count + t)
                yield t * columns + (shares - begin[0]) + p, tiles[1][source, k, p]

    begin = jnp.stack([(1 - half) * shares, index]).astype(jnp.int32)
    gradient = read_points(points, begin, near_slots, [far_tiles], [far_spec], far_rows, None)
    near_tiles = [jnp.stack(own), jnp.stack(near)]
    near_specs = [
        pl.BlockSpec(x.shape, functools.partial(lambda nd, i, at: (0,) * nd, x.ndim)) for x in near_tiles
    ]
    begin = jnp.stack([half * shares, index]).astype(jnp.int32)
    gradient = read_points(points, begin, near_slots, near_tiles, near_specs, near_rows, gradient)
    whole = merge_rows(early_share, 0, cycle_blocks, None)
    whole = merge_rows(late_share, FILTER_FIRST, cycle_blocks, whole)
    return whole, gradient[None]


precise = lax.Precision.HIGHEST


def contract(formula, lhs_array, rhs_array):
    return jnp.einsum(formula, lhs_array, rhs_array, precision=precise)


def spread_matrix(weights, starts, extent):
    offsets = lax.broadcasted_iota(jnp.int32, (1, 1, extent), 2) - starts[:, :, None]
    result = jnp.zeros(starts.shape + (extent,), jnp.float32)
    for tap_index in range(weights.shape[1]):
        result = result + jnp.where(offsets == tap_index, weights[:, tap_index, :, None], 0.0)
    return result


def angle_table(rows_count, cols_count, modulus):
    left_index = lax.broadcasted_iota(jnp.int32, (rows_count, cols_count), 0)
    right_index = lax.broadcasted_iota(jnp.int32, (rows_count, cols_count), 1)
    phase_int = left_index * right_index % modulus
    angles = phase_int.astype(jnp.float32) * (2.0 * math.pi / modulus)
    return (jnp.cos(angles), jnp.sin(angles))


def filter_by_einsum(cycle_rows, response):
    length = cycle_rows.shape[-1]
    second = length // RADIX
    cos_first, sin_first = angle_table(RADIX, RADIX, RADIX)
    cos_twist, sin_twist = angle_table(RADIX, second, length)
    cos_second, sin_second = angle_table(second, second, second)
    blocks = cycle_rows.reshape(cycle_rows.shape[:2] + (RADIX, second))
    real_one = contract("giab,ak->gikb", blocks, cos_first)
    imag_one = -contract("giab,ak->gikb", blocks, sin_first)
    real_two = real_one * cos_twist + imag_one * sin_twist
    imag_two = imag_one * cos_twist - real_one * sin_twist
    real_freq = contract("gikb,bm->gikm", real_two, cos_second) + contract(
        "gikb,bm->gikm", imag_two, sin_second
    )
    imag_freq = contract("gikb,bm->gikm", imag_two, cos_second) - contract(
        "gikb,bm->gikm", real_two, sin_second
    )
    full_response = jnp.concatenate([response, response[-2:0:-1]])
    gain_table = full_response.reshape(second, RADIX).T
    real_freq = real_freq * gain_table
    imag_freq = imag_freq * gain_table
    real_back = contract("gikm,bm->gikb", real_freq, cos_second) - contract(
        "gikm,bm->gikb", imag_freq, sin_second
    )
    imag_back = contract("gikm,bm->gikb", imag_freq, cos_second) + contract(
        "gikm,bm->gikb", real_freq, sin_second
    )
    real_turn = real_back * cos_twist - imag_back * sin_twist
    imag_turn = imag_back * cos_twist + real_back * sin_twist
    spatial = contract("gikb,ka->giab", real_turn, cos_first) - contract(
        "gikb,ka->giab", imag_turn, sin_first
    )
    return (spatial / length).reshape(cycle_rows.shape)


def accumulate(arrived, wanted, cycle_blocks):
    selector = (
        lax.broadcasted_iota(jnp.int32, (cycle_blocks, wanted.size), 0) == wanted.reshape(1, -1)
    ).astype(jnp.float32)
    flattened = arrived.reshape(wanted.size, -1)
    return jnp.dot(selector, flattened, precision=precise).reshape(
        (cycle_blocks,) + arrived.shape[2:]
    )


def column_owner_plan(values, cycle_taps, phi_taps, cycle_start, phi_start, tile_list, response):
    columns = lax.axis_size("pts")
    part_count = lax.axis_size("tile")
    column = lax.axis_index("pts")
    per_column = values.shape[1] // columns
    tile_width = NPHI // columns
    cycle_part = TR // part_count
    cycle_weights = spread_matrix(cycle_taps[0], cycle_start[0], TR)
    phi_weights = spread_matrix(phi_taps[0], phi_start[0], tile_width)
    loaded = cycle_weights * values[0][:, :, None]
    cycle_split = cycle_weights.reshape(columns, per_column, values.shape[2], part_count, cycle_part)
    loaded_split = loaded.reshape(columns, per_column, values.shape[2], part_count, cycle_part)
    phi_split = phi_weights.reshape(columns, per_column, values.shape[2], tile_width)
    partial_value = contract("qkitr,qkic->qtkrc", loaded_split, phi_split)
    partial_value = partial_value.reshape(columns * part_count, per_column, cycle_part, tile_width)
    arrived = lax.all_to_all(
        partial_value, ("pts", "tile"), split_axis=0, concat_axis=0, tiled=True
    )
    wanted = lax.dynamic_index_in_dim(tile_list, column, 1, keepdims=False)
    owned_tiles = accumulate(arrived, wanted, 256)
    whole_cycles = filter_by_einsum(
        lax.all_to_all(owned_tiles, "pts", split_axis=0, concat_axis=2, tiled=True), response
    )
    filtered = lax.all_to_all(whole_cycles, "pts", split_axis=2, concat_axis=0, tiled=True)
    picked = jnp.take(filtered, wanted.reshape(-1), axis=0)
    picked = picked.reshape(columns * part_count, per_column, cycle_part, tile_width)
    returned = lax.all_to_all(picked, ("pts", "tile"), split_axis=0, concat_axis=0, tiled=True)
    returned = returned.reshape(columns, part_count, per_column, cycle_part, tile_width)
    rows_read = contract("qkitr,qtkrc->qkic", cycle_split, returned)
    gradient = jnp.sum(rows_read * phi_split, axis=-1).reshape(values.shape[1], values.shape[2])
    return (filtered, gradient[None])


def solution(mesh):
    columns, part_count = mesh.shape["pts"], mesh.shape["tile"]
    step, pts, tile = column_owner_plan, "pts", "tile"
    if columns * part_count == TR and columns % 2 == 0 and NPHI // columns == GROUPS * LANES:
        mesh = Mesh(mesh.devices.reshape(2, columns // 2, part_count), AXES)
        step, pts = row_owner_plan, ("half", "share")
    block = (pts, tile) if pts == "pts" else AXES
    return jax.shard_map(
        step,
        mesh=mesh,
        in_specs=(
            P(block, None, None),
            P(block, None, None, None),
            P(block, None, None, None),
            P(block, None, None),
            P(block, None, None),
            P(),
            P(),
        ),
        out_specs=(P(None, tile, pts), P(block, None, None)),
        check_vma=False,
    )
```

```python
import functools
import math

import jax
import jax.numpy as jnp
import numpy as np
from jax import lax
from jax.experimental import pallas as pl
from jax.experimental.pallas import tpu as pltpu
from jax.sharding import Mesh
from jax.sharding import PartitionSpec as P

NPHI = 8192
TR = 32
TAPS = 8
LANES = 128
GROUPS = 8
RADIX = 64
STEP_SLOTS = 8
VMEM_LIMIT = 60 * 1024 * 1024

f32 = jnp.float32
bf16 = jnp.bfloat16


def split(x):
    high = x.astype(bf16)
    low = (x - high.astype(f32)).astype(bf16)
    return high, low


def split_f32(x):
    high = x.astype(bf16).astype(f32)
    return high, x - high


def shifted_window(taps, shift):
    n = taps.shape[1]
    window = jnp.concatenate([taps, jnp.zeros((8, n), f32)], axis=0)
    both = jnp.concatenate([shift, shift], axis=0)
    for bit in (1, 2, 4):
        moved = pltpu.roll(window, bit, 0)
        window = jnp.where((both & bit) != 0, moved, window)
    return window[:8], window[8:]


def twice(x):
    return jnp.concatenate([x, x], axis=0)


def half_rows(groups, upper):
    first = lax.broadcasted_iota(jnp.int32, groups[0].shape, 0) < 4
    merged = []
    for at in range(0, len(groups), 2):
        left, right = groups[at : at + 2]
        lower = jnp.where(first, left, pltpu.roll(right, 4, 0))
        merged.append(jnp.where(upper, jnp.where(first, pltpu.roll(left, 4, 0), right), lower))
    return merged


def cycle_factor(taps, cycle_start, phi_start, upper=None):
    first, second = shifted_window(taps, cycle_start & 7)
    block = cycle_start >> 3
    rows = []
    for h in range(TR // 8):
        rows.append(jnp.where(block == h, first, jnp.where(block == h - 1, second, 0.0)))
    if upper is not None:
        rows = half_rows(rows, upper)
    group = twice((phi_start >> 7).astype(f32)).astype(bf16)
    masks = [group == g for g in range(GROUPS)]
    zero = jnp.zeros(group.shape, bf16)
    parts = []
    for part in split(jnp.concatenate(rows, axis=0)):
        pieces = []
        for mask in masks:
            pieces += [jnp.where(mask, part[at : at + 16], zero) for at in range(0, part.shape[0], 16)]
        parts.append(jnp.concatenate(pieces, axis=0))
    return parts


def phi_factor(taps, phi_start):
    first, second = shifted_window(taps, phi_start & 7)
    odd = (phi_start & 8) != 0
    zero = jnp.zeros(first.shape, f32)
    near = jnp.concatenate([jnp.where(odd, zero, first), jnp.where(odd, first, second)], axis=0)
    far = jnp.concatenate([jnp.where(odd, second, zero), zero], axis=0)
    block = twice(((phi_start & 127) >> 4).astype(f32)).astype(bf16)
    masks = [block == h for h in range(8)]
    zero = jnp.zeros(block.shape, bf16)
    parts = []
    for low, high in zip(split(near), split(far)):
        pieces = [jnp.where(masks[0], low, zero)]
        for h in range(1, 8):
            pieces.append(jnp.where(masks[h], low, jnp.where(masks[h - 1], high, zero)))
        pieces.append(jnp.where(masks[7], high, zero))
        parts.append(jnp.concatenate(pieces, axis=0))
    return parts


def spread_kernel(values, cycle_taps, phi_taps, cycle_start, phi_start, out, turn):
    n = values.shape[1]
    shares, parts, rows = out.shape[:3]
    for k in range(STEP_SLOTS):
        cycle_at = jnp.broadcast_to(cycle_start[k : k + 1, :], (8, n))
        phi_at = jnp.broadcast_to(phi_start[k : k + 1, :], (8, n))
        loaded = cycle_taps[k] * values[k : k + 1, :]
        left_high, left_low = cycle_factor(loaded, cycle_at, phi_at)
        empty = jnp.zeros((256 - 144, n), bf16)
        right_high, right_low = [jnp.concatenate([x, empty], axis=0) for x in phi_factor(phi_taps[k], phi_at)]
        left = jnp.concatenate([left_high, left_high, left_low], axis=1)
        right = jnp.concatenate([right_high, right_low, right_high], axis=1)
        product = lax.dot_general(left, right, (((1,), (1,)), ((), ())), preferred_element_type=f32)
        for g in range(GROUPS):
            tile = product[g * TR : (g + 1) * TR, :LANES]
            if g:
                tile = tile + product[(g - 1) * TR : g * TR, LANES:]
            for at in range(0, TR, 8):
                turn[k, pl.ds(at * GROUPS + g, 8, stride=GROUPS), :] = tile[at : at + 8]
        for r in range(TR):
            t, p, row = r // (shares * rows), r // rows % shares, r % rows
            out[p, t, row, k] = turn[k, r * GROUPS : (r + 1) * GROUPS, :]


def point_specs(place, n):
    flat = pl.BlockSpec((STEP_SLOTS, n), lambda *at: (place(*at), 0))
    taps = pl.BlockSpec((STEP_SLOTS, TAPS, n), lambda *at: (place(*at), 0, 0))
    return [flat, taps, taps, flat, flat]


def spread_tiles(points, shares, part_count, first, slots):
    n = points[0].shape[1]
    begin = first // STEP_SLOTS
    heads = (shares, part_count, TR // (shares * part_count))
    return pl.pallas_call(
        spread_kernel,
        grid=(slots // STEP_SLOTS,),
        in_specs=point_specs(lambda i: begin + i, n),
        out_specs=pl.BlockSpec(heads + (STEP_SLOTS, 8, LANES), lambda i: (0, 0, 0, i, 0, 0)),
        out_shape=jax.ShapeDtypeStruct(heads + (slots, 8, LANES), f32),
        scratch_shapes=[pltpu.VMEM((STEP_SLOTS, TR * GROUPS, LANES), f32)],
        compiler_params=pltpu.CompilerParams(vmem_limit_bytes=VMEM_LIMIT),
        cost_estimate=pl.CostEstimate(
            flops=slots * 2 * 3 * 256 * 256 * n, bytes_accessed=slots * (19 + 32) * n * 4, transcendentals=0
        ),
        name="spread",
    )(*points)


def read_kernel(count, cycles, place_rows, begin, cycle_taps, phi_taps, cycle_start, phi_start, *rest):
    tiles, so_far, (out, turn) = rest[:count], rest[count:-2], rest[-2:]
    n = cycle_start.shape[1]
    upper = None if cycles == TR else begin[2] != 0
    for k in range(STEP_SLOTS):
        cycle_at = jnp.broadcast_to(cycle_start[k : k + 1, :], (8, n))
        phi_at = jnp.broadcast_to(phi_start[k : k + 1, :], (8, n))
        right_high, right_low = cycle_factor(cycle_taps[k], cycle_at, phi_at, upper)
        for r, row in place_rows(begin, tiles, k):
            turn[k, r * GROUPS : (r + 1) * GROUPS, :] = row
        pieces = [
            turn[k, pl.ds(at * GROUPS + g, 8, stride=GROUPS), :] for g in range(GROUPS) for at in range(0, cycles, 8)
        ]
        tile = jnp.concatenate(pieces, axis=0).T
        following = pltpu.roll(tile[:16], cycles * (GROUPS - 1), 1)
        left_high, left_low = split(jnp.concatenate([tile, following], axis=0))
        left = jnp.concatenate([left_high, left_low, left_high], axis=1)
        right = jnp.concatenate([right_high, right_high, right_low], axis=0)
        picked = dot(left, right)
        lane = phi_at & 127
        first, second = shifted_window(phi_taps[k], lane & 7)
        block = lane >> 3
        low = picked[:8]
        high = picked[8:16]
        for h in range(1, 16):
            here = block == h
            low = jnp.where(here, picked[h * 8 : h * 8 + 8], low)
            high = jnp.where(here, picked[h * 8 + 8 : h * 8 + 16], high)
        result = jnp.sum(low * first + high * second, axis=0, keepdims=True)
        if so_far and cycles < TR:
            result = result + so_far[0][k : k + 1, :]
        out[k : k + 1, :] = result


def read_points(points, begin, slots, tiles, tile_specs, cycles, place_rows, so_far):
    total, n = points[0].shape
    given = [] if so_far is None else [so_far]
    specs = point_specs(lambda i, at: at[0] + i, n)
    given_spec = pl.BlockSpec(memory_space=pl.ANY) if cycles == TR else specs[0]
    return pl.pallas_call(
        functools.partial(read_kernel, len(tile_specs), cycles, place_rows),
        grid_spec=pltpu.PrefetchScalarGridSpec(
            num_scalar_prefetch=1,
            grid=(slots // STEP_SLOTS,),
            in_specs=specs[1:] + tile_specs + [given_spec] * len(given),
            out_specs=specs[0],
            scratch_shapes=[pltpu.VMEM((STEP_SLOTS, cycles * GROUPS, LANES), f32)],
        ),
        out_shape=jax.ShapeDtypeStruct((total, n), f32),
        input_output_aliases={5 + len(tile_specs): 0} if given else {},
        compiler_params=pltpu.CompilerParams(vmem_limit_bytes=VMEM_LIMIT),
        cost_estimate=pl.CostEstimate(
            flops=slots * 2 * 3 * 256 * 8 * cycles * n, bytes_accessed=slots * (19 + cycles) * n * 4, transcendentals=0
        ),
        name="read_back",
    )(begin, *points[1:], *tiles, *given)


def pick_far_kernel(tile_list, *refs):
    filtered, out = refs[:-1], refs[-1]
    step = pl.program_id(0)
    blocks, columns, per_column = tile_list.shape
    first = filtered[0].shape[1]

    def one(d, carry):
        block = step * out.shape[0] + d
        other = (1 - block // (blocks // 2)) * (columns // 2)
        for c in range(columns // 2):
            for k in range(per_column):
                j = tile_list[block, other + c, k]
                early = filtered[0][other + c, jnp.minimum(j, first - 1)]
                late = filtered[1][other + c, jnp.maximum(j - first, 0)]
                out[d, c * per_column + k] = jnp.where(j < first, early, late)
        return carry

    lax.fori_loop(0, out.shape[0], one, 0)


def pick_far(filtered, tile_list):
    blocks, columns, per_column = tile_list.shape
    shape = (blocks, columns // 2 * per_column, 8, LANES)
    step = 4
    return pl.pallas_call(
        pick_far_kernel,
        grid=(blocks // step,),
        in_specs=[pl.BlockSpec(memory_space=pltpu.SMEM)]
        + [pl.BlockSpec(part.shape, lambda i: (0, 0, 0, 0)) for part in filtered],
        out_specs=pl.BlockSpec((step,) + shape[1:], lambda i: (i, 0, 0, 0)),
        out_shape=jax.ShapeDtypeStruct(shape, f32),
        compiler_params=pltpu.CompilerParams(vmem_limit_bytes=VMEM_LIMIT),
        cost_estimate=pl.CostEstimate(flops=0, bytes_accessed=12 * 2**20, transcendentals=0),
        name="pick_far",
    )(tile_list, *filtered)


def outs_by_device(outs):
    return [(out, share) for share in range(outs[0].shape[0]) for out in outs]


def pick_own_kernel(place, tile_list, *refs):
    filtered, outs = refs[:2], refs[2:]
    columns, per_column = tile_list.shape[1:]
    first = filtered[0].shape[1]

    for d, (out, share) in enumerate(outs_by_device(outs)):
        block = place[0] + (place[2] ^ d)

        def one(c, carry):
            column = place[4] + c
            for k in range(per_column):
                j = tile_list[block, column, k]
                inside, beyond = jnp.minimum(j, first - 1), jnp.maximum(j - first, 0)
                tile = jnp.where(j < first, filtered[0][column, inside], filtered[1][column, beyond])
                out[share, c * per_column + k] = tile
            return carry

        lax.fori_loop(0, columns // 2, one, 0)


def pick_own(filtered, place, tile_list, part_count):
    blocks, columns, per_column = tile_list.shape
    shape = (blocks // 2 // part_count, columns // 2 * per_column, 8, LANES)
    return pl.pallas_call(
        pick_own_kernel,
        grid=(1,),
        in_specs=[pl.BlockSpec(memory_space=pltpu.SMEM)] * 2
        + [pl.BlockSpec(part.shape, lambda i: (0, 0, 0, 0)) for part in filtered],
        out_specs=[pl.BlockSpec(shape, lambda i: (0, 0, 0, 0))] * part_count,
        out_shape=[jax.ShapeDtypeStruct(shape, f32)] * part_count,
        compiler_params=pltpu.CompilerParams(vmem_limit_bytes=VMEM_LIMIT),
        cost_estimate=pl.CostEstimate(flops=0, bytes_accessed=10 * 2**20, transcendentals=0),
        name="pick_own",
    )(place, tile_list, *filtered)


def pick_near_kernel(place, tile_list, *refs):
    shares, outs = refs[:2], refs[2:]
    per_column = tile_list.shape[2]
    first = shares[0].shape[1]
    rows = outs[0].shape[2]

    for d, (out, share) in enumerate(outs_by_device(outs)):
        block = place[0] + (place[2] ^ d)

        def one(k, carry):
            j = tile_list[block, place[1], k]
            inside, beyond = jnp.minimum(j, first - 1), jnp.maximum(j - first, 0)
            for row in range(rows):
                at = place[3] + row
                out[share, k, row] = jnp.where(j < first, shares[0][at, inside], shares[1][at, beyond])
            return carry

        lax.fori_loop(0, per_column, one, 0)


def pick_near(shares, place, tile_list, part_count):
    blocks, columns, per_column = tile_list.shape
    shape = (blocks // 2 // part_count, per_column, shares[0].shape[0] // 2, 8, LANES)
    return pl.pallas_call(
        pick_near_kernel,
        grid=(1,),
        in_specs=[pl.BlockSpec(memory_space=pltpu.SMEM)] * 2
        + [pl.BlockSpec(part.shape, lambda i: (0, 0, 0, 0)) for part in shares],
        out_specs=[pl.BlockSpec(shape, lambda i: (0, 0, 0, 0, 0))] * part_count,
        out_shape=[jax.ShapeDtypeStruct(shape, f32)] * part_count,
        compiler_params=pltpu.CompilerParams(vmem_limit_bytes=VMEM_LIMIT),
        cost_estimate=pl.CostEstimate(flops=0, bytes_accessed=12 * 2**20, transcendentals=0),
        name="pick_near",
    )(place, tile_list, *shares)


def merge_kernel(arrived, *rest):
    out = rest[-1]
    rows, blocks = arrived.shape[:2]
    for c in range(8):
        for j in range(blocks):
            out[j, :, c * LANES : (c + 1) * LANES] = arrived[:, j, c, :]


def merge_rows(arrived, first, cycle_blocks, so_far):
    rows, blocks = arrived.shape[:2]
    step = 32
    begin = first // step
    given = [] if so_far is None else [so_far]
    return pl.pallas_call(
        merge_kernel,
        grid=(blocks // step,),
        in_specs=[pl.BlockSpec((rows, step, 8, LANES), lambda i: (0, i, 0, 0))]
        + [pl.BlockSpec(memory_space=pl.ANY)] * len(given),
        out_specs=pl.BlockSpec((step, rows, 8 * LANES), lambda i: (begin + i, 0, 0)),
        out_shape=jax.ShapeDtypeStruct((cycle_blocks, rows, 8 * LANES), f32),
        input_output_aliases={1: 0} if given else {},
        compiler_params=pltpu.CompilerParams(vmem_limit_bytes=VMEM_LIMIT),
        cost_estimate=pl.CostEstimate(flops=0, bytes_accessed=8 * blocks * rows * 1024, transcendentals=0),
        name="merge_rows",
    )(arrived, *given)


@functools.cache
def dft_tables():
    a = np.arange(RADIX)
    b = np.arange(LANES)
    first = 2.0 * np.pi / RADIX * (np.outer(a, a) % RADIX)
    twist = 2.0 * np.pi / NPHI * np.outer(a, b)
    second = 2.0 * np.pi / LANES * (np.outer(b, b) % LANES)
    c1, s1, c2, s2 = np.cos(first), np.sin(first), np.cos(second), np.sin(second)
    ahead_first = np.block([[c1, s1], [-s1, c1]])
    back_first = np.block([[c1, -s1], [s1, c1]])
    ahead_second = np.block([[c2, -s2], [s2, c2]])
    back_second = np.block([[c2, s2], [-s2, c2]])

    def pair(table):
        high = np.asarray(table, np.float32).astype(bf16)
        low = (table - high.astype(np.float64)).astype(np.float32).astype(bf16)
        return high, low

    def wide(table):
        high, low = pair(table)
        return np.concatenate([high, high, low], axis=1)

    def stacked(table):
        high, low = pair(table)
        return np.concatenate([high, high, low], axis=0)

    return (
        wide(ahead_first),
        wide(back_first),
        stacked(ahead_second),
        stacked(back_second),
        np.cos(twist).astype(np.float32),
        np.sin(twist).astype(np.float32),
    )


def dot(lhs, rhs):
    return lax.dot_general(lhs, rhs, (((1,), (0,)), ((), ())), preferred_element_type=f32)


def first_dots(table, cells):
    turned = []
    for at in range(0, len(cells), 2):
        high, low = split(jnp.concatenate(cells[at : at + 2], axis=1))
        both = dot(table, jnp.concatenate([high, low, high], axis=0))
        turned += [both[:, :LANES], both[:, LANES:]]
    return turned


def filter_block(tables, cells):
    ahead_first, back_first, ahead_second, back_second, cos_twist, sin_twist, gain = tables
    count = len(cells)
    cos_t, sin_t = cos_twist[...], sin_twist[...]
    middle = []
    for turned in first_dots(ahead_first[...], cells):
        real, imag = turned[:RADIX], turned[RADIX:]
        middle.append(jnp.concatenate([real * cos_t + imag * sin_t, imag * cos_t - real * sin_t], axis=1))
    middle = jnp.concatenate(middle, axis=0)

    def second(x, table):
        high, low = split(x)
        return dot(jnp.concatenate([high, low, high], axis=1), table[...])

    spectrum = second(middle, ahead_second)
    spectrum = (spectrum.reshape(count, RADIX, 2 * LANES) * gain[...][None]).reshape(count * RADIX, 2 * LANES)
    middle = second(spectrum, back_second)
    cells = []
    for c in range(count):
        real, imag = middle[c * RADIX : (c + 1) * RADIX, :LANES], middle[c * RADIX : (c + 1) * RADIX, LANES:]
        cells.append(jnp.concatenate([real * cos_t - imag * sin_t, imag * cos_t + real * sin_t], axis=0))
    return first_dots(back_first[...], cells)


FILTER_STEP = 32


def filter_into(tables, grid, first, out):
    cells = [grid[first + j].reshape(RADIX, LANES) for j in range(FILTER_STEP)]
    cells = [jnp.concatenate(cells[j : j + 2], axis=0) for j in range(0, FILTER_STEP, 2)]
    for p, turned in enumerate(filter_block(tables, cells)):
        for part in range(2):
            for c in range(8):
                at = part * RADIX + c * 8
                out[c, 2 * p + part] = turned[at : at + 8]


def filter_kernel(*refs):
    filter_into(refs[:7], refs[7], 0, refs[8])


def whole_specs(arrays):
    return [pl.BlockSpec(x.shape, functools.partial(lambda nd, i: (0,) * nd, x.ndim)) for x in arrays]


def filter_cost(blocks):
    return pl.CostEstimate(
        flops=blocks * 3 * 2 * (128 * 128 * 128 + 64 * 256 * 256), bytes_accessed=blocks * 2**16, transcendentals=0
    )


def filter_cycles(grid, tables):
    blocks, columns = grid.shape[:2]
    return pl.pallas_call(
        filter_kernel,
        grid=(blocks // FILTER_STEP,),
        in_specs=whole_specs(tables) + [pl.BlockSpec((FILTER_STEP, columns, 8, LANES), lambda i: (i, 0, 0, 0))],
        out_specs=pl.BlockSpec((columns, FILTER_STEP, 8, LANES), lambda i: (0, i, 0, 0)),
        out_shape=jax.ShapeDtypeStruct((columns, blocks, 8, LANES), f32),
        compiler_params=pltpu.CompilerParams(vmem_limit_bytes=VMEM_LIMIT),
        cost_estimate=filter_cost(blocks),
        name="filter_cycles",
    )(*tables, grid)


COLLECT_STEP = 4
COLLECT_BATCH = 32


def collect_kernel(chunks, tile_list, *refs):
    arrived, rest = refs[: len(chunks)], refs[len(chunks) :]
    tables, (out, others, total, sem) = rest[:7], rest[7:]
    step = pl.program_id(0)
    per_column = tile_list.shape[2]
    cycle_blocks = total.shape[0]
    collecting = tile_list.shape[0] // COLLECT_STEP
    first = cycle_blocks - others.shape[0]

    @pl.when(step == 0)
    def _():
        def clear(j, carry):
            total[j] = jnp.zeros(total.shape[1:], f32)
            return carry

        lax.fori_loop(0, cycle_blocks, clear, 0, unroll=8)

    @pl.when(step < collecting)
    def _():
        for d in range(COLLECT_STEP):
            for ref, begin in zip(arrived, chunks):
                for c in range(0, ref.shape[1], COLLECT_BATCH):
                    where = []
                    for slot in range(begin + c, min(begin + c + COLLECT_BATCH, begin + ref.shape[1])):
                        q, k = slot // per_column, slot % per_column
                        where.append((tile_list[step * COLLECT_STEP + d, q, k], q))
                    sums = [total[j, q] + ref[d, c + at] for at, (j, q) in enumerate(where)]
                    for (j, q), x in zip(where, sums):
                        total[j, q] = x

    hand_over = pltpu.make_async_copy(total.at[pl.ds(first, others.shape[0])], others, sem)

    @pl.when(step >= collecting)
    def _():
        @pl.when(step == collecting)
        def _():
            hand_over.start()

        filter_into(tables, total, (step - collecting) * FILTER_STEP, out)

        @pl.when(step == pl.num_programs(0) - 1)
        def _():
            hand_over.wait()


def collect_and_filter(arrived, chunks, tile_list, tables, cycle_blocks, part):
    blocks, columns, per_column = tile_list.shape
    collecting = blocks // COLLECT_STEP
    steps = part // FILTER_STEP
    return pl.pallas_call(
        functools.partial(collect_kernel, chunks),
        grid=(collecting + steps,),
        in_specs=[pl.BlockSpec(memory_space=pltpu.SMEM)]
        + [
            pl.BlockSpec((COLLECT_STEP,) + x.shape[1:], lambda i: (jnp.minimum(i, collecting - 1), 0, 0, 0))
            for x in arrived
        ]
        + whole_specs(tables),
        out_specs=[
            pl.BlockSpec((columns, FILTER_STEP, 8, LANES), lambda i: (0, jnp.maximum(i - collecting, 0), 0, 0)),
            pl.BlockSpec(memory_space=pl.ANY),
        ],
        out_shape=[
            jax.ShapeDtypeStruct((columns, part, 8, LANES), f32),
            jax.ShapeDtypeStruct((cycle_blocks - part, columns, 8, LANES), f32),
        ],
        scratch_shapes=[pltpu.VMEM((cycle_blocks, columns, 8, LANES), f32), pltpu.SemaphoreType.DMA],
        compiler_params=pltpu.CompilerParams(vmem_limit_bytes=VMEM_LIMIT),
        cost_estimate=filter_cost(part + 64),
        name="collect_filter",
    )(tile_list, *arrived, *tables)


def gain_table(response):
    full = jnp.concatenate([response, response[-2:0:-1]])
    gain = full.reshape(LANES, RADIX).T * (1.0 / NPHI)
    return jnp.concatenate([gain, gain], axis=1)


SLOT_CHUNKS = (8, 56)
FILTER_FIRST = 32
AXES = ("half", "share", "tile")


def after(x, *others):
    return lax.optimization_barrier((x, *others))[0]


def row_owner_plan(values, cycle_taps, phi_taps, cycle_start, phi_start, tile_list, response):
    half, share = lax.axis_index("half"), lax.axis_index("share")
    shares, part_count = lax.axis_size("share"), lax.axis_size("tile")
    blocks, columns, per_column = tile_list.shape
    near_slots = shares * per_column
    cycle_blocks = 256
    points = [x[0] for x in (values, cycle_taps, phi_taps, cycle_start, phi_start)]
    tables = [jnp.asarray(t) for t in dft_tables()] + [gain_table(response)]
    index = share * part_count + lax.axis_index("tile")
    place = jnp.stack(
        [half * (blocks // 2), half * shares + share, index, (1 - half) * shares, half * shares]
    ).astype(jnp.int32)

    def exchange(x, axes):
        return lax.all_to_all(x, axes, 0, 0, tiled=True)

    arrived, begins, at = [], [], 0
    for extent in SLOT_CHUNKS:
        tiles = spread_tiles(points, columns, part_count, at, extent)
        arrived.append(exchange(tiles.reshape(blocks, extent, 8, LANES), AXES))
        begins.append(at)
        at += extent
    early, others = collect_and_filter(arrived, begins, tile_list, tables, cycle_blocks, FILTER_FIRST)
    late = filter_cycles(others, tables)

    def pass_on(parts):
        def step(x, axis, size, d):
            return lax.ppermute(x, axis, [(i, i ^ d) for i in range(size)]) if d else x

        here = [step(x, AXES[2], part_count, d) for d, x in enumerate(parts)]
        return [
            step(jnp.stack([x[d] for x in here]), AXES[1], shares, d) for d in range(shares)
        ]

    early_share = exchange(early, AXES[:2])
    far = pick_far([early, late], tile_list)
    late_share = exchange(after(late, early_share), AXES[:2])
    own = pass_on(pick_own([after(early, far), late], place, tile_list, part_count))
    far_tiles = exchange(after(far, late_share, *own[1:]), AXES)
    near = pass_on(pick_near([early_share, late_share], place, tile_list, part_count))

    far_tiles = far_tiles.reshape(columns, part_count, near_slots, 8, LANES)
    far_spec = pl.BlockSpec((columns, part_count, STEP_SLOTS, 8, LANES), lambda i, at: (0, 0, i, 0, 0))

    def far_rows(begin, tiles, k):
        return [(r, tiles[0][r % columns, r // columns, k]) for r in range(TR)]

    def own_rows(begin, tiles, k):
        step = pl.program_id(0)
        for t in range(part_count):
            for p in range(shares):
                source = begin[1] ^ (p * part_count + t)
                yield t * shares + p, tiles[0][source, step * STEP_SLOTS + k]

    def near_rows(begin, tiles, k):
        apart = begin[1] // part_count ^ pl.program_id(0)
        for t in range(part_count):
            source = begin[1] % part_count ^ t
            for p in range(shares):
                row = tiles[0][source, k, p]
                for d in range(1, shares):
                    row = jnp.where(apart == d, tiles[d][source, k, p], row)
                yield t * shares + p, row

    def whole_specs_at(arrays):
        return [pl.BlockSpec(x.shape, functools.partial(lambda nd, i, at: (0,) * nd, x.ndim)) for x in arrays]

    def begin_at(which, upper):
        return jnp.stack([which * shares, index, upper]).astype(jnp.int32)

    own = [jnp.concatenate(own)]
    gradient = read_points(points, begin_at(half, half), near_slots, own, whole_specs_at(own), TR // 2, own_rows, None)
    gradient = read_points(points, begin_at(1 - half, half), near_slots, [far_tiles], [far_spec], TR, far_rows, gradient)
    near = [after(x, gradient) for x in near]
    gradient = read_points(
        points, begin_at(half, 1 - half), near_slots, near, whole_specs_at(near), TR // 2, near_rows, gradient
    )
    whole = merge_rows(early_share, 0, cycle_blocks, None)
    whole = merge_rows(late_share, FILTER_FIRST, cycle_blocks, whole)
    return whole, gradient[None]


precise = lax.Precision.HIGHEST


def contract(formula, lhs_array, rhs_array):
    return jnp.einsum(formula, lhs_array, rhs_array, precision=precise)


def spread_matrix(weights, starts, extent):
    offsets = lax.broadcasted_iota(jnp.int32, (1, 1, extent), 2) - starts[:, :, None]
    result = jnp.zeros(starts.shape + (extent,), jnp.float32)
    for tap_index in range(weights.shape[1]):
        result = result + jnp.where(offsets == tap_index, weights[:, tap_index, :, None], 0.0)
    return result


def angle_table(rows_count, cols_count, modulus):
    left_index = lax.broadcasted_iota(jnp.int32, (rows_count, cols_count), 0)
    right_index = lax.broadcasted_iota(jnp.int32, (rows_count, cols_count), 1)
    phase_int = left_index * right_index % modulus
    angles = phase_int.astype(jnp.float32) * (2.0 * math.pi / modulus)
    return (jnp.cos(angles), jnp.sin(angles))


def filter_by_einsum(cycle_rows, response):
    length = cycle_rows.shape[-1]
    second = length // RADIX
    cos_first, sin_first = angle_table(RADIX, RADIX, RADIX)
    cos_twist, sin_twist = angle_table(RADIX, second, length)
    cos_second, sin_second = angle_table(second, second, second)
    blocks = cycle_rows.reshape(cycle_rows.shape[:2] + (RADIX, second))
    real_one = contract("giab,ak->gikb", blocks, cos_first)
    imag_one = -contract("giab,ak->gikb", blocks, sin_first)
    real_two = real_one * cos_twist + imag_one * sin_twist
    imag_two = imag_one * cos_twist - real_one * sin_twist
    real_freq = contract("gikb,bm->gikm", real_two, cos_second) + contract(
        "gikb,bm->gikm", imag_two, sin_second
    )
    imag_freq = contract("gikb,bm->gikm", imag_two, cos_second) - contract(
        "gikb,bm->gikm", real_two, sin_second
    )
    full_response = jnp.concatenate([response, response[-2:0:-1]])
    gain_table = full_response.reshape(second, RADIX).T
    real_freq = real_freq * gain_table
    imag_freq = imag_freq * gain_table
    real_back = contract("gikm,bm->gikb", real_freq, cos_second) - contract(
        "gikm,bm->gikb", imag_freq, sin_second
    )
    imag_back = contract("gikm,bm->gikb", imag_freq, cos_second) + contract(
        "gikm,bm->gikb", real_freq, sin_second
    )
    real_turn = real_back * cos_twist - imag_back * sin_twist
    imag_turn = imag_back * cos_twist + real_back * sin_twist
    spatial = contract("gikb,ka->giab", real_turn, cos_first) - contract(
        "gikb,ka->giab", imag_turn, sin_first
    )
    return (spatial / length).reshape(cycle_rows.shape)


def accumulate(arrived, wanted, cycle_blocks):
    selector = (
        lax.broadcasted_iota(jnp.int32, (cycle_blocks, wanted.size), 0) == wanted.reshape(1, -1)
    ).astype(jnp.float32)
    flattened = arrived.reshape(wanted.size, -1)
    return jnp.dot(selector, flattened, precision=precise).reshape(
        (cycle_blocks,) + arrived.shape[2:]
    )


def column_owner_plan(values, cycle_taps, phi_taps, cycle_start, phi_start, tile_list, response):
    columns = lax.axis_size("pts")
    part_count = lax.axis_size("tile")
    column = lax.axis_index("pts")
    per_column = values.shape[1] // columns
    tile_width = NPHI // columns
    cycle_part = TR // part_count
    cycle_weights = spread_matrix(cycle_taps[0], cycle_start[0], TR)
    phi_weights = spread_matrix(phi_taps[0], phi_start[0], tile_width)
    loaded = cycle_weights * values[0][:, :, None]
    cycle_split = cycle_weights.reshape(columns, per_column, values.shape[2], part_count, cycle_part)
    loaded_split = loaded.reshape(columns, per_column, values.shape[2], part_count, cycle_part)
    phi_split = phi_weights.reshape(columns, per_column, values.shape[2], tile_width)
    partial_value = contract("qkitr,qkic->qtkrc", loaded_split, phi_split)
    partial_value = partial_value.reshape(columns * part_count, per_column, cycle_part, tile_width)
    arrived = lax.all_to_all(
        partial_value, ("pts", "tile"), split_axis=0, concat_axis=0, tiled=True
    )
    wanted = lax.dynamic_index_in_dim(tile_list, column, 1, keepdims=False)
    owned_tiles = accumulate(arrived, wanted, 256)
    whole_cycles = filter_by_einsum(
        lax.all_to_all(owned_tiles, "pts", split_axis=0, concat_axis=2, tiled=True), response
    )
    filtered = lax.all_to_all(whole_cycles, "pts", split_axis=2, concat_axis=0, tiled=True)
    picked = jnp.take(filtered, wanted.reshape(-1), axis=0)
    picked = picked.reshape(columns * part_count, per_column, cycle_part, tile_width)
    returned = lax.all_to_all(picked, ("pts", "tile"), split_axis=0, concat_axis=0, tiled=True)
    returned = returned.reshape(columns, part_count, per_column, cycle_part, tile_width)
    rows_read = contract("qkitr,qtkrc->qkic", cycle_split, returned)
    gradient = jnp.sum(rows_read * phi_split, axis=-1).reshape(values.shape[1], values.shape[2])
    return (filtered, gradient[None])


def solution(mesh):
    columns, part_count = mesh.shape["pts"], mesh.shape["tile"]
    step, pts, tile = column_owner_plan, "pts", "tile"
    if columns * part_count == TR and columns % 2 == 0 and NPHI // columns == GROUPS * LANES:
        mesh = Mesh(mesh.devices.reshape(2, columns // 2, part_count), AXES)
        step, pts = row_owner_plan, ("half", "share")
    block = (pts, tile) if pts == "pts" else AXES
    return jax.shard_map(
        step,
        mesh=mesh,
        in_specs=(
            P(block, None, None),
            P(block, None, None, None),
            P(block, None, None, None),
            P(block, None, None),
            P(block, None, None),
            P(),
            P(),
        ),
        out_specs=(P(None, tile, pts), P(block, None, None)),
        check_vma=False,
    )
```

```python
import functools
import math

import jax
import jax.numpy as jnp
import numpy as np
from jax import lax
from jax.experimental import pallas as pl
from jax.experimental.pallas import tpu as pltpu
from jax.sharding import Mesh
from jax.sharding import PartitionSpec as P

NPHI = 8192
TR = 32
TAPS = 8
LANES = 128
GROUPS = 8
RADIX = 64
STEP_SLOTS = 8
VMEM_LIMIT = 60 * 1024 * 1024

f32 = jnp.float32
bf16 = jnp.bfloat16


def split(x):
    high = x.astype(bf16)
    low = (x - high.astype(f32)).astype(bf16)
    return high, low


def split_f32(x):
    high = x.astype(bf16).astype(f32)
    return high, x - high


def shifted_window(taps, shift):
    n = taps.shape[1]
    window = jnp.concatenate([taps, jnp.zeros((8, n), f32)], axis=0)
    both = jnp.concatenate([shift, shift], axis=0)
    for bit in (1, 2, 4):
        moved = pltpu.roll(window, bit, 0)
        window = jnp.where((both & bit) != 0, moved, window)
    return window[:8], window[8:]


def twice(x):
    return jnp.concatenate([x, x], axis=0)


def half_rows(groups, upper):
    first = lax.broadcasted_iota(jnp.int32, groups[0].shape, 0) < 4
    merged = []
    for at in range(0, len(groups), 2):
        left, right = groups[at : at + 2]
        lower = jnp.where(first, left, pltpu.roll(right, 4, 0))
        merged.append(jnp.where(upper, jnp.where(first, pltpu.roll(left, 4, 0), right), lower))
    return merged


def cycle_factor(taps, cycle_start, phi_start, upper=None):
    first, second = shifted_window(taps, cycle_start & 7)
    block = cycle_start >> 3
    rows = []
    for h in range(TR // 8):
        rows.append(jnp.where(block == h, first, jnp.where(block == h - 1, second, 0.0)))
    if upper is not None:
        rows = half_rows(rows, upper)
    group = twice((phi_start >> 7).astype(f32)).astype(bf16)
    masks = [group == g for g in range(GROUPS)]
    zero = jnp.zeros(group.shape, bf16)
    parts = []
    for part in split(jnp.concatenate(rows, axis=0)):
        pieces = []
        for mask in masks:
            pieces += [jnp.where(mask, part[at : at + 16], zero) for at in range(0, part.shape[0], 16)]
        parts.append(jnp.concatenate(pieces, axis=0))
    return parts


def phi_factor(taps, phi_start):
    first, second = shifted_window(taps, phi_start & 7)
    odd = (phi_start & 8) != 0
    zero = jnp.zeros(first.shape, f32)
    near = jnp.concatenate([jnp.where(odd, zero, first), jnp.where(odd, first, second)], axis=0)
    far = jnp.concatenate([jnp.where(odd, second, zero), zero], axis=0)
    block = twice(((phi_start & 127) >> 4).astype(f32)).astype(bf16)
    masks = [block == h for h in range(8)]
    zero = jnp.zeros(block.shape, bf16)
    parts = []
    for low, high in zip(split(near), split(far)):
        pieces = [jnp.where(masks[0], low, zero)]
        for h in range(1, 8):
            pieces.append(jnp.where(masks[h], low, jnp.where(masks[h - 1], high, zero)))
        pieces.append(jnp.where(masks[7], high, zero))
        parts.append(jnp.concatenate(pieces, axis=0))
    return parts


def rows_dot(lhs, rhs):
    return lax.dot_general(lhs, rhs, (((1,), (1,)), ((), ())), preferred_element_type=f32)


def spread_kernel(values, cycle_taps, phi_taps, cycle_start, phi_start, out, turn):
    n = values.shape[1]
    shares, parts, rows = out.shape[:3]
    for k in range(STEP_SLOTS):
        cycle_at = jnp.broadcast_to(cycle_start[k : k + 1, :], (8, n))
        phi_at = jnp.broadcast_to(phi_start[k : k + 1, :], (8, n))
        loaded = cycle_taps[k] * values[k : k + 1, :]
        left_high, left_low = cycle_factor(loaded, cycle_at, phi_at)
        empty = jnp.zeros((256 - 144, n), bf16)
        right_high, right_low = [jnp.concatenate([x, empty], axis=0) for x in phi_factor(phi_taps[k], phi_at)]
        product = rows_dot(jnp.concatenate([left_high, left_low], axis=0), right_high)
        product = product[: TR * GROUPS] + product[TR * GROUPS :] + rows_dot(left_high, right_low)
        for g in range(GROUPS):
            tile = product[g * TR : (g + 1) * TR, :LANES]
            if g:
                tile = tile + product[(g - 1) * TR : g * TR, LANES:]
            for at in range(0, TR, 8):
                turn[k, pl.ds(at * GROUPS + g, 8, stride=GROUPS), :] = tile[at : at + 8]
        for r in range(TR):
            t, p, row = r // (shares * rows), r // rows % shares, r % rows
            out[p, t, row, k] = turn[k, r * GROUPS : (r + 1) * GROUPS, :]


def point_specs(place, n):
    flat = pl.BlockSpec((STEP_SLOTS, n), lambda *at: (place(*at), 0))
    taps = pl.BlockSpec((STEP_SLOTS, TAPS, n), lambda *at: (place(*at), 0, 0))
    return [flat, taps, taps, flat, flat]


def spread_tiles(points, shares, part_count, first, slots):
    n = points[0].shape[1]
    begin = first // STEP_SLOTS
    heads = (shares, part_count, TR // (shares * part_count))
    return pl.pallas_call(
        spread_kernel,
        grid=(slots // STEP_SLOTS,),
        in_specs=point_specs(lambda i: begin + i, n),
        out_specs=pl.BlockSpec(heads + (STEP_SLOTS, 8, LANES), lambda i: (0, 0, 0, i, 0, 0)),
        out_shape=jax.ShapeDtypeStruct(heads + (slots, 8, LANES), f32),
        scratch_shapes=[pltpu.VMEM((STEP_SLOTS, TR * GROUPS, LANES), f32)],
        compiler_params=pltpu.CompilerParams(vmem_limit_bytes=VMEM_LIMIT),
        cost_estimate=pl.CostEstimate(
            flops=slots * 2 * 3 * 256 * 256 * n, bytes_accessed=slots * (19 + 32) * n * 4, transcendentals=0
        ),
        name="spread",
    )(*points)


def read_kernel(count, cycles, place_rows, begin, cycle_taps, phi_taps, cycle_start, phi_start, *rest):
    tiles, so_far, (out, turn) = rest[:count], rest[count:-2], rest[-2:]
    n = cycle_start.shape[1]
    upper = None if cycles == TR else begin[2] != 0
    for k in range(STEP_SLOTS):
        cycle_at = jnp.broadcast_to(cycle_start[k : k + 1, :], (8, n))
        phi_at = jnp.broadcast_to(phi_start[k : k + 1, :], (8, n))
        right_high, right_low = cycle_factor(cycle_taps[k], cycle_at, phi_at, upper)
        for r, row in place_rows(begin, tiles, k):
            turn[k, r * GROUPS : (r + 1) * GROUPS, :] = row
        pieces = [
            turn[k, pl.ds(at * GROUPS + g, 8, stride=GROUPS), :] for g in range(GROUPS) for at in range(0, cycles, 8)
        ]
        tile = jnp.concatenate(pieces, axis=0).T
        following = pltpu.roll(tile[:16], cycles * (GROUPS - 1), 1)
        left_high, left_low = split(jnp.concatenate([tile, following], axis=0))
        picked = dot(left_high, right_high) + dot(left_low, right_high) + dot(left_high, right_low)
        lane = phi_at & 127
        first, second = shifted_window(phi_taps[k], lane & 7)
        block = lane >> 3
        low = picked[:8]
        high = picked[8:16]
        for h in range(1, 16):
            here = block == h
            low = jnp.where(here, picked[h * 8 : h * 8 + 8], low)
            high = jnp.where(here, picked[h * 8 + 8 : h * 8 + 16], high)
        result = jnp.sum(low * first + high * second, axis=0, keepdims=True)
        if so_far and cycles < TR:
            result = result + so_far[0][k : k + 1, :]
        out[k : k + 1, :] = result


def read_points(points, begin, slots, tiles, tile_specs, cycles, place_rows, so_far):
    total, n = points[0].shape
    given = [] if so_far is None else [so_far]
    specs = point_specs(lambda i, at: at[0] + i, n)
    given_spec = pl.BlockSpec(memory_space=pl.ANY) if cycles == TR else specs[0]
    return pl.pallas_call(
        functools.partial(read_kernel, len(tile_specs), cycles, place_rows),
        grid_spec=pltpu.PrefetchScalarGridSpec(
            num_scalar_prefetch=1,
            grid=(slots // STEP_SLOTS,),
            in_specs=specs[1:] + tile_specs + [given_spec] * len(given),
            out_specs=specs[0],
            scratch_shapes=[pltpu.VMEM((STEP_SLOTS, cycles * GROUPS, LANES), f32)],
        ),
        out_shape=jax.ShapeDtypeStruct((total, n), f32),
        input_output_aliases={5 + len(tile_specs): 0} if given else {},
        compiler_params=pltpu.CompilerParams(vmem_limit_bytes=VMEM_LIMIT),
        cost_estimate=pl.CostEstimate(
            flops=slots * 2 * 3 * 256 * 8 * cycles * n, bytes_accessed=slots * (19 + cycles) * n * 4, transcendentals=0
        ),
        name="read_back",
    )(begin, *points[1:], *tiles, *given)


def pick_far_kernel(tile_list, *refs):
    filtered, out = refs[:-1], refs[-1]
    step = pl.program_id(0)
    blocks, columns, per_column = tile_list.shape
    first = filtered[0].shape[1]

    def one(d, carry):
        block = step * out.shape[0] + d
        other = (1 - block // (blocks // 2)) * (columns // 2)
        for c in range(columns // 2):
            for k in range(per_column):
                j = tile_list[block, other + c, k]
                early = filtered[0][other + c, jnp.minimum(j, first - 1)]
                late = filtered[1][other + c, jnp.maximum(j - first, 0)]
                out[d, c * per_column + k] = jnp.where(j < first, early, late)
        return carry

    lax.fori_loop(0, out.shape[0], one, 0)


def pick_far(filtered, tile_list):
    blocks, columns, per_column = tile_list.shape
    shape = (blocks, columns // 2 * per_column, 8, LANES)
    step = 4
    return pl.pallas_call(
        pick_far_kernel,
        grid=(blocks // step,),
        in_specs=[pl.BlockSpec(memory_space=pltpu.SMEM)]
        + [pl.BlockSpec(part.shape, lambda i: (0, 0, 0, 0)) for part in filtered],
        out_specs=pl.BlockSpec((step,) + shape[1:], lambda i: (i, 0, 0, 0)),
        out_shape=jax.ShapeDtypeStruct(shape, f32),
        compiler_params=pltpu.CompilerParams(vmem_limit_bytes=VMEM_LIMIT),
        cost_estimate=pl.CostEstimate(flops=0, bytes_accessed=12 * 2**20, transcendentals=0),
        name="pick_far",
    )(tile_list, *filtered)


def outs_by_device(outs):
    return [(out, share) for share in range(outs[0].shape[0]) for out in outs]


def pick_own_kernel(place, tile_list, *refs):
    filtered, outs = refs[:2], refs[2:]
    columns, per_column = tile_list.shape[1:]
    first = filtered[0].shape[1]

    for d, (out, share) in enumerate(outs_by_device(outs)):
        block = place[0] + (place[2] ^ d)

        def one(c, carry):
            column = place[4] + c
            for k in range(per_column):
                j = tile_list[block, column, k]
                inside, beyond = jnp.minimum(j, first - 1), jnp.maximum(j - first, 0)
                tile = jnp.where(j < first, filtered[0][column, inside], filtered[1][column, beyond])
                out[share, c * per_column + k] = tile
            return carry

        lax.fori_loop(0, columns // 2, one, 0)


def pick_own(filtered, place, tile_list, part_count):
    blocks, columns, per_column = tile_list.shape
    shape = (blocks // 2 // part_count, columns // 2 * per_column, 8, LANES)
    return pl.pallas_call(
        pick_own_kernel,
        grid=(1,),
        in_specs=[pl.BlockSpec(memory_space=pltpu.SMEM)] * 2
        + [pl.BlockSpec(part.shape, lambda i: (0, 0, 0, 0)) for part in filtered],
        out_specs=[pl.BlockSpec(shape, lambda i: (0, 0, 0, 0))] * part_count,
        out_shape=[jax.ShapeDtypeStruct(shape, f32)] * part_count,
        compiler_params=pltpu.CompilerParams(vmem_limit_bytes=VMEM_LIMIT),
        cost_estimate=pl.CostEstimate(flops=0, bytes_accessed=10 * 2**20, transcendentals=0),
        name="pick_own",
    )(place, tile_list, *filtered)


def pick_near_kernel(place, tile_list, *refs):
    shares, outs = refs[:2], refs[2:]
    per_column = tile_list.shape[2]
    first = shares[0].shape[1]
    rows = outs[0].shape[1]

    for d, out in enumerate(outs):
        block = place[0] + (place[2] ^ d)

        def one(k, carry):
            j = tile_list[block, place[1], k]
            inside, beyond = jnp.minimum(j, first - 1), jnp.maximum(j - first, 0)
            for row in range(rows):
                at = place[3] + row
                out[k, row] = jnp.where(j < first, shares[0][at, inside], shares[1][at, beyond])
            return carry

        lax.fori_loop(0, per_column, one, 0)


def pick_near(shares, place, tile_list):
    blocks, columns, per_column = tile_list.shape
    shape = (per_column, shares[0].shape[0] // 2, 8, LANES)
    return pl.pallas_call(
        pick_near_kernel,
        grid=(1,),
        in_specs=[pl.BlockSpec(memory_space=pltpu.SMEM)] * 2
        + [pl.BlockSpec(part.shape, lambda i: (0, 0, 0, 0)) for part in shares],
        out_specs=[pl.BlockSpec(shape, lambda i: (0, 0, 0, 0))] * (blocks // 2),
        out_shape=[jax.ShapeDtypeStruct(shape, f32)] * (blocks // 2),
        compiler_params=pltpu.CompilerParams(vmem_limit_bytes=VMEM_LIMIT),
        cost_estimate=pl.CostEstimate(flops=0, bytes_accessed=12 * 2**20, transcendentals=0),
        name="pick_near",
    )(place, tile_list, *shares)


def merge_kernel(arrived, *rest):
    out = rest[-1]
    rows, blocks = arrived.shape[:2]
    for c in range(8):
        for j in range(blocks):
            out[j, :, c * LANES : (c + 1) * LANES] = arrived[:, j, c, :]


def merge_rows(arrived, first, cycle_blocks, so_far):
    rows, blocks = arrived.shape[:2]
    step = 32
    begin = first // step
    given = [] if so_far is None else [so_far]
    return pl.pallas_call(
        merge_kernel,
        grid=(blocks // step,),
        in_specs=[pl.BlockSpec((rows, step, 8, LANES), lambda i: (0, i, 0, 0))]
        + [pl.BlockSpec(memory_space=pl.ANY)] * len(given),
        out_specs=pl.BlockSpec((step, rows, 8 * LANES), lambda i: (begin + i, 0, 0)),
        out_shape=jax.ShapeDtypeStruct((cycle_blocks, rows, 8 * LANES), f32),
        input_output_aliases={1: 0} if given else {},
        compiler_params=pltpu.CompilerParams(vmem_limit_bytes=VMEM_LIMIT),
        cost_estimate=pl.CostEstimate(flops=0, bytes_accessed=8 * blocks * rows * 1024, transcendentals=0),
        name="merge_rows",
    )(arrived, *given)


@functools.cache
def dft_tables():
    a = np.arange(RADIX)
    b = np.arange(LANES)
    first = 2.0 * np.pi / RADIX * (np.outer(a, a) % RADIX)
    twist = 2.0 * np.pi / NPHI * np.outer(a, b)
    second = 2.0 * np.pi / LANES * (np.outer(b, b) % LANES)
    c1, s1, c2, s2 = np.cos(first), np.sin(first), np.cos(second), np.sin(second)
    ahead_first = np.block([[c1, s1], [-s1, c1]])
    back_first = np.block([[c1, -s1], [s1, c1]])
    ahead_second = np.block([[c2, -s2], [s2, c2]])
    back_second = np.block([[c2, s2], [-s2, c2]])

    def pair(table):
        high = np.asarray(table, np.float32).astype(bf16)
        low = (table - high.astype(np.float64)).astype(np.float32).astype(bf16)
        return high, low

    def wide(table):
        high, low = pair(table)
        return np.concatenate([high, high, low], axis=1)

    def stacked(table):
        high, low = pair(table)
        return np.concatenate([high, high, low], axis=0)

    return (
        wide(ahead_first),
        wide(back_first),
        stacked(ahead_second),
        stacked(back_second),
        np.cos(twist).astype(np.float32),
        np.sin(twist).astype(np.float32),
    )


def dot(lhs, rhs):
    return lax.dot_general(lhs, rhs, (((1,), (0,)), ((), ())), preferred_element_type=f32)


def first_dots(table, cells):
    turned = []
    for at in range(0, len(cells), 2):
        high, low = split(jnp.concatenate(cells[at : at + 2], axis=1))
        both = dot(table, jnp.concatenate([high, low, high], axis=0))
        turned += [both[:, :LANES], both[:, LANES:]]
    return turned


def filter_block(tables, cells):
    ahead_first, back_first, ahead_second, back_second, cos_twist, sin_twist, gain = tables
    count = len(cells)
    cos_t, sin_t = cos_twist[...], sin_twist[...]
    middle = []
    for turned in first_dots(ahead_first[...], cells):
        real, imag = turned[:RADIX], turned[RADIX:]
        middle.append(jnp.concatenate([real * cos_t + imag * sin_t, imag * cos_t - real * sin_t], axis=1))
    middle = jnp.concatenate(middle, axis=0)

    def second(x, table):
        high, low = split(x)
        return dot(jnp.concatenate([high, low, high], axis=1), table[...])

    spectrum = second(middle, ahead_second)
    spectrum = (spectrum.reshape(count, RADIX, 2 * LANES) * gain[...][None]).reshape(count * RADIX, 2 * LANES)
    middle = second(spectrum, back_second)
    cells = []
    for c in range(count):
        real, imag = middle[c * RADIX : (c + 1) * RADIX, :LANES], middle[c * RADIX : (c + 1) * RADIX, LANES:]
        cells.append(jnp.concatenate([real * cos_t - imag * sin_t, imag * cos_t + real * sin_t], axis=0))
    return first_dots(back_first[...], cells)


FILTER_STEP = 32


def filter_into(tables, grid, first, out):
    cells = [grid[first + j].reshape(RADIX, LANES) for j in range(FILTER_STEP)]
    cells = [jnp.concatenate(cells[j : j + 2], axis=0) for j in range(0, FILTER_STEP, 2)]
    for p, turned in enumerate(filter_block(tables, cells)):
        for part in range(2):
            for c in range(8):
                at = part * RADIX + c * 8
                out[c, 2 * p + part] = turned[at : at + 8]


def filter_kernel(*refs):
    filter_into(refs[:7], refs[7], 0, refs[8])


def whole_specs(arrays):
    return [pl.BlockSpec(x.shape, functools.partial(lambda nd, i: (0,) * nd, x.ndim)) for x in arrays]


def filter_cost(blocks):
    return pl.CostEstimate(
        flops=blocks * 3 * 2 * (128 * 128 * 128 + 64 * 256 * 256), bytes_accessed=blocks * 2**16, transcendentals=0
    )


def filter_cycles(grid, tables):
    blocks, columns = grid.shape[:2]
    return pl.pallas_call(
        filter_kernel,
        grid=(blocks // FILTER_STEP,),
        in_specs=whole_specs(tables) + [pl.BlockSpec((FILTER_STEP, columns, 8, LANES), lambda i: (i, 0, 0, 0))],
        out_specs=pl.BlockSpec((columns, FILTER_STEP, 8, LANES), lambda i: (0, i, 0, 0)),
        out_shape=jax.ShapeDtypeStruct((columns, blocks, 8, LANES), f32),
        compiler_params=pltpu.CompilerParams(vmem_limit_bytes=VMEM_LIMIT),
        cost_estimate=filter_cost(blocks),
        name="filter_cycles",
    )(*tables, grid)


COLLECT_STEP = 4
COLLECT_BATCH = 32


def collect_kernel(begins, tile_list, *refs):
    count = len(begins)
    arrived, tables, (out, others) = refs[:count], refs[count : count + 7], refs[count + 7 : count + 9]
    total, given_sem, sem = refs[count + 9 : count + 12]
    given = refs[count + 12 :]
    blocks, _, per_column = tile_list.shape
    cycle_blocks = total.shape[0]
    first = cycle_blocks - others.shape[0]
    stretches = [pl.ds(at, COLLECT_STEP) for at in range(0, blocks, COLLECT_STEP)]
    fetches = [
        [pltpu.make_async_copy(x.at[part], g.at[part], given_sem.at[i, c]) for i, (x, g) in enumerate(zip(arrived, given))]
        for c, part in enumerate(stretches)
    ]
    for fetch in fetches:
        for copy in fetch:
            copy.start()

    def clear(j, carry):
        total[j] = jnp.zeros(total.shape[1:], f32)
        return carry

    lax.fori_loop(0, cycle_blocks, clear, 0, unroll=8)
    for c, fetch in enumerate(fetches):
        for copy in fetch:
            copy.wait()

        def one(d, carry):
            for ref, begin in zip(given, begins):
                extent = ref.shape[1]
                for at in range(0, extent, COLLECT_BATCH):
                    where = []
                    for slot in range(begin + at, begin + min(at + COLLECT_BATCH, extent)):
                        q, k = slot // per_column, slot % per_column
                        where.append((tile_list[d, q, k], q))
                    sums = [total[j, q] + ref[d, at + i] for i, (j, q) in enumerate(where)]
                    for (j, q), x in zip(where, sums):
                        total[j, q] = x
            return carry

        lax.fori_loop(c * COLLECT_STEP, (c + 1) * COLLECT_STEP, one, 0)
    hand_over = pltpu.make_async_copy(total.at[pl.ds(first, others.shape[0])], others, sem)
    hand_over.start()
    filter_into(tables, total, 0, out)
    hand_over.wait()


def collect_and_filter(arrived, begins, tile_list, tables, cycle_blocks):
    blocks, columns, per_column = tile_list.shape
    return pl.pallas_call(
        functools.partial(collect_kernel, begins),
        grid=(1,),
        in_specs=[pl.BlockSpec(memory_space=pltpu.SMEM)]
        + [pl.BlockSpec(memory_space=pl.ANY)] * len(arrived)
        + whole_specs(tables),
        out_specs=[
            pl.BlockSpec((columns, FILTER_STEP, 8, LANES), lambda i: (0, 0, 0, 0)),
            pl.BlockSpec(memory_space=pl.ANY),
        ],
        out_shape=[
            jax.ShapeDtypeStruct((columns, FILTER_STEP, 8, LANES), f32),
            jax.ShapeDtypeStruct((cycle_blocks - FILTER_STEP, columns, 8, LANES), f32),
        ],
        scratch_shapes=[
            pltpu.VMEM((cycle_blocks, columns, 8, LANES), f32),
            pltpu.SemaphoreType.DMA((len(arrived), blocks // COLLECT_STEP)),
            pltpu.SemaphoreType.DMA,
        ]
        + [pltpu.VMEM(x.shape, f32) for x in arrived],
        compiler_params=pltpu.CompilerParams(vmem_limit_bytes=VMEM_LIMIT),
        cost_estimate=filter_cost(FILTER_STEP + 64),
        name="collect_filter",
    )(tile_list, *arrived, *tables)


def gain_table(response):
    full = jnp.concatenate([response, response[-2:0:-1]])
    gain = full.reshape(LANES, RADIX).T * (1.0 / NPHI)
    return jnp.concatenate([gain, gain], axis=1)


SLOT_CHUNKS = (8, 56)
AXES = ("half", "share", "tile")


def after(x, *others):
    return lax.optimization_barrier((x, *others))[0]


def row_owner_plan(values, cycle_taps, phi_taps, cycle_start, phi_start, tile_list, response):
    half, share = lax.axis_index("half"), lax.axis_index("share")
    shares, part_count = lax.axis_size("share"), lax.axis_size("tile")
    blocks, columns, per_column = tile_list.shape
    near_slots = shares * per_column
    cycle_blocks = 256
    points = [x[0] for x in (values, cycle_taps, phi_taps, cycle_start, phi_start)]
    tables = [jnp.asarray(t) for t in dft_tables()] + [gain_table(response)]
    index = share * part_count + lax.axis_index("tile")
    place = jnp.stack(
        [half * (blocks // 2), half * shares + share, index, (1 - half) * shares, half * shares]
    ).astype(jnp.int32)

    def exchange(x, axes):
        return lax.all_to_all(x, axes, 0, 0, tiled=True)

    arrived, begins, at = [], [], 0
    for extent in SLOT_CHUNKS:
        tiles = spread_tiles(points, columns, part_count, at, extent)
        arrived.append(exchange(tiles.reshape(blocks, extent, 8, LANES), AXES))
        begins.append(at)
        at += extent
    early, others = collect_and_filter(arrived, begins, tile_list, tables, cycle_blocks)
    late = filter_cycles(others, tables)

    def pass_on(parts):
        def step(x, axis, size, d):
            return lax.ppermute(x, axis, [(i, i ^ d) for i in range(size)]) if d else x

        here = [step(x, AXES[2], part_count, d) for d, x in enumerate(parts)]
        return [
            step(jnp.stack([x[d] for x in here]), AXES[1], shares, d) for d in range(shares)
        ]

    early_share = exchange(early, AXES[:2])
    far = pick_far([early, late], tile_list)
    late_share = exchange(after(late, early_share), AXES[:2])
    own = pass_on(pick_own([after(early, far), late], place, tile_list, part_count))

    def own_rows(begin, tiles, k):
        step = pl.program_id(0)
        for t in range(part_count):
            for p in range(shares):
                source = begin[1] ^ (p * part_count + t)
                yield t * shares + p, tiles[0][source, step * STEP_SLOTS + k]

    def whole_specs_at(arrays):
        return [pl.BlockSpec(x.shape, functools.partial(lambda nd, i, at: (0,) * nd, x.ndim)) for x in arrays]

    def begin_at(which, upper):
        return jnp.stack([which * shares, index, upper]).astype(jnp.int32)

    own = [jnp.concatenate(own)]
    gradient = read_points(points, begin_at(half, half), near_slots, own, whole_specs_at(own), TR // 2, own_rows, None)
    whole = merge_rows(early_share, 0, cycle_blocks, None)
    far_tiles = exchange(after(far, late_share, gradient, whole), AXES)
    near = list(pick_near([early_share, late_share], place, tile_list))
    for d in range(1, blocks // 2):
        near[d] = lax.ppermute(near[d], AXES[1:], [(i, i ^ d) for i in range(blocks // 2)])

    far_tiles = far_tiles.reshape(columns, part_count, near_slots, 8, LANES)
    far_spec = pl.BlockSpec((columns, part_count, STEP_SLOTS, 8, LANES), lambda i, at: (0, 0, i, 0, 0))

    def far_rows(begin, tiles, k):
        return [(r, tiles[0][r % columns, r // columns, k]) for r in range(TR)]

    def near_rows(begin, tiles, k):
        for t in range(part_count):
            source = begin[1] ^ (pl.program_id(0) * part_count + t)
            for p in range(shares):
                yield t * shares + p, tiles[0][source, k, p]

    moved = near[5]
    near = [jnp.stack(near)]
    gradient = read_points(
        points, begin_at(half, 1 - half), near_slots, near, whole_specs_at(near), TR // 2, near_rows, gradient
    )
    gradient = read_points(points, begin_at(1 - half, half), near_slots, [far_tiles], [far_spec], TR, far_rows, gradient)
    whole = merge_rows(after(late_share, moved), FILTER_STEP, cycle_blocks, whole)
    return whole, gradient[None]


precise = lax.Precision.HIGHEST


def contract(formula, lhs_array, rhs_array):
    return jnp.einsum(formula, lhs_array, rhs_array, precision=precise)


def spread_matrix(weights, starts, extent):
    offsets = lax.broadcasted_iota(jnp.int32, (1, 1, extent), 2) - starts[:, :, None]
    result = jnp.zeros(starts.shape + (extent,), jnp.float32)
    for tap_index in range(weights.shape[1]):
        result = result + jnp.where(offsets == tap_index, weights[:, tap_index, :, None], 0.0)
    return result


def angle_table(rows_count, cols_count, modulus):
    left_index = lax.broadcasted_iota(jnp.int32, (rows_count, cols_count), 0)
    right_index = lax.broadcasted_iota(jnp.int32, (rows_count, cols_count), 1)
    phase_int = left_index * right_index % modulus
    angles = phase_int.astype(jnp.float32) * (2.0 * math.pi / modulus)
    return (jnp.cos(angles), jnp.sin(angles))


def filter_by_einsum(cycle_rows, response):
    length = cycle_rows.shape[-1]
    second = length // RADIX
    cos_first, sin_first = angle_table(RADIX, RADIX, RADIX)
    cos_twist, sin_twist = angle_table(RADIX, second, length)
    cos_second, sin_second = angle_table(second, second, second)
    blocks = cycle_rows.reshape(cycle_rows.shape[:2] + (RADIX, second))
    real_one = contract("giab,ak->gikb", blocks, cos_first)
    imag_one = -contract("giab,ak->gikb", blocks, sin_first)
    real_two = real_one * cos_twist + imag_one * sin_twist
    imag_two = imag_one * cos_twist - real_one * sin_twist
    real_freq = contract("gikb,bm->gikm", real_two, cos_second) + contract(
        "gikb,bm->gikm", imag_two, sin_second
    )
    imag_freq = contract("gikb,bm->gikm", imag_two, cos_second) - contract(
        "gikb,bm->gikm", real_two, sin_second
    )
    full_response = jnp.concatenate([response, response[-2:0:-1]])
    gain_table = full_response.reshape(second, RADIX).T
    real_freq = real_freq * gain_table
    imag_freq = imag_freq * gain_table
    real_back = contract("gikm,bm->gikb", real_freq, cos_second) - contract(
        "gikm,bm->gikb", imag_freq, sin_second
    )
    imag_back = contract("gikm,bm->gikb", imag_freq, cos_second) + contract(
        "gikm,bm->gikb", real_freq, sin_second
    )
    real_turn = real_back * cos_twist - imag_back * sin_twist
    imag_turn = imag_back * cos_twist + real_back * sin_twist
    spatial = contract("gikb,ka->giab", real_turn, cos_first) - contract(
        "gikb,ka->giab", imag_turn, sin_first
    )
    return (spatial / length).reshape(cycle_rows.shape)


def accumulate(arrived, wanted, cycle_blocks):
    selector = (
        lax.broadcasted_iota(jnp.int32, (cycle_blocks, wanted.size), 0) == wanted.reshape(1, -1)
    ).astype(jnp.float32)
    flattened = arrived.reshape(wanted.size, -1)
    return jnp.dot(selector, flattened, precision=precise).reshape(
        (cycle_blocks,) + arrived.shape[2:]
    )


def column_owner_plan(values, cycle_taps, phi_taps, cycle_start, phi_start, tile_list, response):
    columns = lax.axis_size("pts")
    part_count = lax.axis_size("tile")
    column = lax.axis_index("pts")
    per_column = values.shape[1] // columns
    tile_width = NPHI // columns
    cycle_part = TR // part_count
    cycle_weights = spread_matrix(cycle_taps[0], cycle_start[0], TR)
    phi_weights = spread_matrix(phi_taps[0], phi_start[0], tile_width)
    loaded = cycle_weights * values[0][:, :, None]
    cycle_split = cycle_weights.reshape(columns, per_column, values.shape[2], part_count, cycle_part)
    loaded_split = loaded.reshape(columns, per_column, values.shape[2], part_count, cycle_part)
    phi_split = phi_weights.reshape(columns, per_column, values.shape[2], tile_width)
    partial_value = contract("qkitr,qkic->qtkrc", loaded_split, phi_split)
    partial_value = partial_value.reshape(columns * part_count, per_column, cycle_part, tile_width)
    arrived = lax.all_to_all(
        partial_value, ("pts", "tile"), split_axis=0, concat_axis=0, tiled=True
    )
    wanted = lax.dynamic_index_in_dim(tile_list, column, 1, keepdims=False)
    owned_tiles = accumulate(arrived, wanted, 256)
    whole_cycles = filter_by_einsum(
        lax.all_to_all(owned_tiles, "pts", split_axis=0, concat_axis=2, tiled=True), response
    )
    filtered = lax.all_to_all(whole_cycles, "pts", split_axis=2, concat_axis=0, tiled=True)
    picked = jnp.take(filtered, wanted.reshape(-1), axis=0)
    picked = picked.reshape(columns * part_count, per_column, cycle_part, tile_width)
    returned = lax.all_to_all(picked, ("pts", "tile"), split_axis=0, concat_axis=0, tiled=True)
    returned = returned.reshape(columns, part_count, per_column, cycle_part, tile_width)
    rows_read = contract("qkitr,qtkrc->qkic", cycle_split, returned)
    gradient = jnp.sum(rows_read * phi_split, axis=-1).reshape(values.shape[1], values.shape[2])
    return (filtered, gradient[None])


def solution(mesh):
    columns, part_count = mesh.shape["pts"], mesh.shape["tile"]
    step, pts, tile = column_owner_plan, "pts", "tile"
    if columns * part_count == TR and columns % 2 == 0 and NPHI // columns == GROUPS * LANES:
        mesh = Mesh(mesh.devices.reshape(2, columns // 2, part_count), AXES)
        step, pts = row_owner_plan, ("half", "share")
    block = (pts, tile) if pts == "pts" else AXES
    return jax.shard_map(
        step,
        mesh=mesh,
        in_specs=(
            P(block, None, None),
            P(block, None, None, None),
            P(block, None, None, None),
            P(block, None, None),
            P(block, None, None),
            P(),
            P(),
        ),
        out_specs=(P(None, tile, pts), P(block, None, None)),
        check_vma=False,
    )
```

```python
import functools
import math

import jax
import jax.numpy as jnp
import numpy as np
from jax import lax
from jax.experimental import pallas as pl
from jax.experimental.pallas import tpu as pltpu
from jax.sharding import Mesh
from jax.sharding import PartitionSpec as P

NPHI = 8192
TR = 32
TAPS = 8
LANES = 128
GROUPS = 8
RADIX = 64
STEP_SLOTS = 8
VMEM_LIMIT = 60 * 1024 * 1024

f32 = jnp.float32
bf16 = jnp.bfloat16


def split(x):
    high = x.astype(bf16)
    low = (x - high.astype(f32)).astype(bf16)
    return high, low


def split_f32(x):
    high = x.astype(bf16).astype(f32)
    return high, x - high


def shifted_window(taps, shift):
    n = taps.shape[1]
    window = jnp.concatenate([taps, jnp.zeros((8, n), f32)], axis=0)
    both = jnp.concatenate([shift, shift], axis=0)
    for bit in (1, 2, 4):
        moved = pltpu.roll(window, bit, 0)
        window = jnp.where((both & bit) != 0, moved, window)
    return window[:8], window[8:]


def twice(x):
    return jnp.concatenate([x, x], axis=0)


def half_rows(groups, upper):
    first = lax.broadcasted_iota(jnp.int32, groups[0].shape, 0) < 4
    merged = []
    for at in range(0, len(groups), 2):
        left, right = groups[at : at + 2]
        lower = jnp.where(first, left, pltpu.roll(right, 4, 0))
        merged.append(jnp.where(upper, jnp.where(first, pltpu.roll(left, 4, 0), right), lower))
    return merged


def cycle_factor(taps, cycle_start, phi_start, upper=None):
    first, second = shifted_window(taps, cycle_start & 7)
    block = cycle_start >> 3
    rows = []
    for h in range(TR // 8):
        rows.append(jnp.where(block == h, first, jnp.where(block == h - 1, second, 0.0)))
    if upper is not None:
        rows = half_rows(rows, upper)
    group = twice((phi_start >> 7).astype(f32)).astype(bf16)
    masks = [group == g for g in range(GROUPS)]
    zero = jnp.zeros(group.shape, bf16)
    parts = []
    for part in split(jnp.concatenate(rows, axis=0)):
        pieces = []
        for mask in masks:
            pieces += [jnp.where(mask, part[at : at + 16], zero) for at in range(0, part.shape[0], 16)]
        parts.append(jnp.concatenate(pieces, axis=0))
    return parts


def phi_factor(taps, phi_start):
    first, second = shifted_window(taps, phi_start & 7)
    odd = (phi_start & 8) != 0
    zero = jnp.zeros(first.shape, f32)
    near = jnp.concatenate([jnp.where(odd, zero, first), jnp.where(odd, first, second)], axis=0)
    far = jnp.concatenate([jnp.where(odd, second, zero), zero], axis=0)
    block = twice(((phi_start & 127) >> 4).astype(f32)).astype(bf16)
    masks = [block == h for h in range(8)]
    zero = jnp.zeros(block.shape, bf16)
    parts = []
    for low, high in zip(split(near), split(far)):
        pieces = [jnp.where(masks[0], low, zero)]
        for h in range(1, 8):
            pieces.append(jnp.where(masks[h], low, jnp.where(masks[h - 1], high, zero)))
        pieces.append(jnp.where(masks[7], high, zero))
        parts.append(jnp.concatenate(pieces, axis=0))
    return parts


def rows_dot(lhs, rhs):
    return lax.dot_general(lhs, rhs, (((1,), (1,)), ((), ())), preferred_element_type=f32)


def spread_kernel(values, cycle_taps, phi_taps, cycle_start, phi_start, out, turn):
    n = values.shape[1]
    shares, parts, rows = out.shape[:3]
    for k in range(STEP_SLOTS):
        cycle_at = jnp.broadcast_to(cycle_start[k : k + 1, :], (8, n))
        phi_at = jnp.broadcast_to(phi_start[k : k + 1, :], (8, n))
        loaded = cycle_taps[k] * values[k : k + 1, :]
        left_high, left_low = cycle_factor(loaded, cycle_at, phi_at)
        empty = jnp.zeros((256 - 144, n), bf16)
        right_high, right_low = [jnp.concatenate([x, empty], axis=0) for x in phi_factor(phi_taps[k], phi_at)]
        product = rows_dot(jnp.concatenate([left_high, left_low], axis=0), right_high)
        product = product[: TR * GROUPS] + product[TR * GROUPS :] + rows_dot(left_high, right_low)
        for g in range(GROUPS):
            tile = product[g * TR : (g + 1) * TR, :LANES]
            if g:
                tile = tile + product[(g - 1) * TR : g * TR, LANES:]
            for at in range(0, TR, 8):
                turn[k, pl.ds(at * GROUPS + g, 8, stride=GROUPS), :] = tile[at : at + 8]
        for r in range(TR):
            t, p, row = r // (shares * rows), r // rows % shares, r % rows
            out[p, t, row, k] = turn[k, r * GROUPS : (r + 1) * GROUPS, :]


def point_specs(place, n):
    flat = pl.BlockSpec((STEP_SLOTS, n), lambda *at: (place(*at), 0))
    taps = pl.BlockSpec((STEP_SLOTS, TAPS, n), lambda *at: (place(*at), 0, 0))
    return [flat, taps, taps, flat, flat]


def spread_tiles(points, shares, part_count, first, slots):
    n = points[0].shape[1]
    begin = first // STEP_SLOTS
    heads = (shares, part_count, TR // (shares * part_count))
    return pl.pallas_call(
        spread_kernel,
        grid=(slots // STEP_SLOTS,),
        in_specs=point_specs(lambda i: begin + i, n),
        out_specs=pl.BlockSpec(heads + (STEP_SLOTS, 8, LANES), lambda i: (0, 0, 0, i, 0, 0)),
        out_shape=jax.ShapeDtypeStruct(heads + (slots, 8, LANES), f32),
        scratch_shapes=[pltpu.VMEM((STEP_SLOTS, TR * GROUPS, LANES), f32)],
        compiler_params=pltpu.CompilerParams(vmem_limit_bytes=VMEM_LIMIT),
        cost_estimate=pl.CostEstimate(
            flops=slots * 2 * 3 * 256 * 256 * n, bytes_accessed=slots * (19 + 32) * n * 4, transcendentals=0
        ),
        name="spread",
    )(*points)


def read_kernel(count, cycles, place_rows, begin, cycle_taps, phi_taps, cycle_start, phi_start, *rest):
    tiles, so_far, (out, turn) = rest[:count], rest[count:-2], rest[-2:]
    n = cycle_start.shape[1]
    upper = None if cycles == TR else begin[2] != 0
    for k in range(STEP_SLOTS):
        cycle_at = jnp.broadcast_to(cycle_start[k : k + 1, :], (8, n))
        phi_at = jnp.broadcast_to(phi_start[k : k + 1, :], (8, n))
        right_high, right_low = cycle_factor(cycle_taps[k], cycle_at, phi_at, upper)
        for r, row in place_rows(begin, tiles, k):
            turn[k, r * GROUPS : (r + 1) * GROUPS, :] = row
        pieces = [
            turn[k, pl.ds(at * GROUPS + g, 8, stride=GROUPS), :] for g in range(GROUPS) for at in range(0, cycles, 8)
        ]
        tile = jnp.concatenate(pieces, axis=0).T
        following = pltpu.roll(tile[:16], cycles * (GROUPS - 1), 1)
        left_high, left_low = split(jnp.concatenate([tile, following], axis=0))
        picked = dot(left_high, right_high) + dot(left_low, right_high) + dot(left_high, right_low)
        lane = phi_at & 127
        first, second = shifted_window(phi_taps[k], lane & 7)
        block = lane >> 3
        low = picked[:8]
        high = picked[8:16]
        for h in range(1, 16):
            here = block == h
            low = jnp.where(here, picked[h * 8 : h * 8 + 8], low)
            high = jnp.where(here, picked[h * 8 + 8 : h * 8 + 16], high)
        result = jnp.sum(low * first + high * second, axis=0, keepdims=True)
        if so_far and cycles < TR:
            result = result + so_far[0][k : k + 1, :]
        out[k : k + 1, :] = result


def read_points(points, begin, slots, tiles, tile_specs, cycles, place_rows, so_far):
    total, n = points[0].shape
    given = [] if so_far is None else [so_far]
    specs = point_specs(lambda i, at: at[0] + i, n)
    given_spec = pl.BlockSpec(memory_space=pl.ANY) if cycles == TR else specs[0]
    return pl.pallas_call(
        functools.partial(read_kernel, len(tile_specs), cycles, place_rows),
        grid_spec=pltpu.PrefetchScalarGridSpec(
            num_scalar_prefetch=1,
            grid=(slots // STEP_SLOTS,),
            in_specs=specs[1:] + tile_specs + [given_spec] * len(given),
            out_specs=specs[0],
            scratch_shapes=[pltpu.VMEM((STEP_SLOTS, cycles * GROUPS, LANES), f32)],
        ),
        out_shape=jax.ShapeDtypeStruct((total, n), f32),
        input_output_aliases={5 + len(tile_specs): 0} if given else {},
        compiler_params=pltpu.CompilerParams(vmem_limit_bytes=VMEM_LIMIT),
        cost_estimate=pl.CostEstimate(
            flops=slots * 2 * 3 * 256 * 8 * cycles * n, bytes_accessed=slots * (19 + cycles) * n * 4, transcendentals=0
        ),
        name="read_back",
    )(begin, *points[1:], *tiles, *given)


def pick_far_kernel(tile_list, *refs):
    filtered, out = refs[:-1], refs[-1]
    step = pl.program_id(0)
    blocks, columns, per_column = tile_list.shape
    first = filtered[0].shape[1]

    def one(d, carry):
        block = step * out.shape[0] + d
        other = (1 - block // (blocks // 2)) * (columns // 2)
        for c in range(columns // 2):
            for k in range(per_column):
                j = tile_list[block, other + c, k]
                early = filtered[0][other + c, jnp.minimum(j, first - 1)]
                late = filtered[1][other + c, jnp.maximum(j - first, 0)]
                out[d, c * per_column + k] = jnp.where(j < first, early, late)
        return carry

    lax.fori_loop(0, out.shape[0], one, 0)


def pick_far(filtered, tile_list):
    blocks, columns, per_column = tile_list.shape
    shape = (blocks, columns // 2 * per_column, 8, LANES)
    step = 4
    return pl.pallas_call(
        pick_far_kernel,
        grid=(blocks // step,),
        in_specs=[pl.BlockSpec(memory_space=pltpu.SMEM)]
        + [pl.BlockSpec(part.shape, lambda i: (0, 0, 0, 0)) for part in filtered],
        out_specs=pl.BlockSpec((step,) + shape[1:], lambda i: (i, 0, 0, 0)),
        out_shape=jax.ShapeDtypeStruct(shape, f32),
        compiler_params=pltpu.CompilerParams(vmem_limit_bytes=VMEM_LIMIT),
        cost_estimate=pl.CostEstimate(flops=0, bytes_accessed=12 * 2**20, transcendentals=0),
        name="pick_far",
    )(tile_list, *filtered)


def outs_by_device(outs):
    return [(out, share) for share in range(outs[0].shape[0]) for out in outs]


def pick_own_kernel(place, tile_list, *refs):
    filtered, outs = refs[:2], refs[2:]
    columns, per_column = tile_list.shape[1:]
    first = filtered[0].shape[1]

    for d, (out, share) in enumerate(outs_by_device(outs)):
        block = place[0] + (place[2] ^ d)

        def one(c, carry):
            column = place[4] + c
            for k in range(per_column):
                j = tile_list[block, column, k]
                inside, beyond = jnp.minimum(j, first - 1), jnp.maximum(j - first, 0)
                tile = jnp.where(j < first, filtered[0][column, inside], filtered[1][column, beyond])
                out[share, c * per_column + k] = tile
            return carry

        lax.fori_loop(0, columns // 2, one, 0)


def pick_own(filtered, place, tile_list, part_count):
    blocks, columns, per_column = tile_list.shape
    shape = (blocks // 2 // part_count, columns // 2 * per_column, 8, LANES)
    return pl.pallas_call(
        pick_own_kernel,
        grid=(1,),
        in_specs=[pl.BlockSpec(memory_space=pltpu.SMEM)] * 2
        + [pl.BlockSpec(part.shape, lambda i: (0, 0, 0, 0)) for part in filtered],
        out_specs=[pl.BlockSpec(shape, lambda i: (0, 0, 0, 0))] * part_count,
        out_shape=[jax.ShapeDtypeStruct(shape, f32)] * part_count,
        compiler_params=pltpu.CompilerParams(vmem_limit_bytes=VMEM_LIMIT),
        cost_estimate=pl.CostEstimate(flops=0, bytes_accessed=10 * 2**20, transcendentals=0),
        name="pick_own",
    )(place, tile_list, *filtered)


def pick_near_kernel(place, tile_list, *refs):
    shares, outs = refs[:2], refs[2:]
    per_column = tile_list.shape[2]
    first = shares[0].shape[1]
    rows = outs[0].shape[1]

    for d, out in enumerate(outs):
        block = place[0] + (place[2] ^ d)

        def one(k, carry):
            j = tile_list[block, place[1], k]
            inside, beyond = jnp.minimum(j, first - 1), jnp.maximum(j - first, 0)
            for row in range(rows):
                at = place[3] + row
                out[k, row] = jnp.where(j < first, shares[0][at, inside], shares[1][at, beyond])
            return carry

        lax.fori_loop(0, per_column, one, 0)


def pick_near(shares, place, tile_list):
    blocks, columns, per_column = tile_list.shape
    shape = (per_column, shares[0].shape[0] // 2, 8, LANES)
    return pl.pallas_call(
        pick_near_kernel,
        grid=(1,),
        in_specs=[pl.BlockSpec(memory_space=pltpu.SMEM)] * 2
        + [pl.BlockSpec(part.shape, lambda i: (0, 0, 0, 0)) for part in shares],
        out_specs=[pl.BlockSpec(shape, lambda i: (0, 0, 0, 0))] * (blocks // 2),
        out_shape=[jax.ShapeDtypeStruct(shape, f32)] * (blocks // 2),
        compiler_params=pltpu.CompilerParams(vmem_limit_bytes=VMEM_LIMIT),
        cost_estimate=pl.CostEstimate(flops=0, bytes_accessed=12 * 2**20, transcendentals=0),
        name="pick_near",
    )(place, tile_list, *shares)


def merge_kernel(arrived, *rest):
    out = rest[-1]
    rows, blocks = arrived.shape[:2]
    for c in range(8):
        for j in range(blocks):
            out[j, :, c * LANES : (c + 1) * LANES] = arrived[:, j, c, :]


def merge_rows(arrived, first, cycle_blocks, so_far):
    rows, blocks = arrived.shape[:2]
    step = 32
    begin = first // step
    given = [] if so_far is None else [so_far]
    return pl.pallas_call(
        merge_kernel,
        grid=(blocks // step,),
        in_specs=[pl.BlockSpec((rows, step, 8, LANES), lambda i: (0, i, 0, 0))]
        + [pl.BlockSpec(memory_space=pl.ANY)] * len(given),
        out_specs=pl.BlockSpec((step, rows, 8 * LANES), lambda i: (begin + i, 0, 0)),
        out_shape=jax.ShapeDtypeStruct((cycle_blocks, rows, 8 * LANES), f32),
        input_output_aliases={1: 0} if given else {},
        compiler_params=pltpu.CompilerParams(vmem_limit_bytes=VMEM_LIMIT),
        cost_estimate=pl.CostEstimate(flops=0, bytes_accessed=8 * blocks * rows * 1024, transcendentals=0),
        name="merge_rows",
    )(arrived, *given)


@functools.cache
def dft_tables():
    a = np.arange(RADIX)
    b = np.arange(LANES)
    first = 2.0 * np.pi / RADIX * (np.outer(a, a) % RADIX)
    twist = 2.0 * np.pi / NPHI * np.outer(a, b)
    second = 2.0 * np.pi / LANES * (np.outer(b, b) % LANES)
    c1, s1, c2, s2 = np.cos(first), np.sin(first), np.cos(second), np.sin(second)
    ahead_first = np.block([[c1, s1], [-s1, c1]])
    back_first = np.block([[c1, -s1], [s1, c1]])
    ahead_second = np.block([[c2, -s2], [s2, c2]])
    back_second = np.block([[c2, s2], [-s2, c2]])

    def pair(table):
        high = np.asarray(table, np.float32).astype(bf16)
        low = (table - high.astype(np.float64)).astype(np.float32).astype(bf16)
        return high, low

    def wide(table):
        high, low = pair(table)
        return np.concatenate([high, high, low], axis=1)

    def stacked(table):
        high, low = pair(table)
        return np.concatenate([high, high, low], axis=0)

    return (
        wide(ahead_first),
        wide(back_first),
        stacked(ahead_second),
        stacked(back_second),
        np.cos(twist).astype(np.float32),
        np.sin(twist).astype(np.float32),
    )


def dot(lhs, rhs):
    return lax.dot_general(lhs, rhs, (((1,), (0,)), ((), ())), preferred_element_type=f32)


def first_dots(table, cells):
    turned = []
    for at in range(0, len(cells), 2):
        high, low = split(jnp.concatenate(cells[at : at + 2], axis=1))
        both = dot(table, jnp.concatenate([high, low, high], axis=0))
        turned += [both[:, :LANES], both[:, LANES:]]
    return turned


def filter_block(tables, cells):
    ahead_first, back_first, ahead_second, back_second, cos_twist, sin_twist, gain = tables
    count = len(cells)
    cos_t, sin_t = cos_twist[...], sin_twist[...]
    middle = []
    for turned in first_dots(ahead_first[...], cells):
        real, imag = turned[:RADIX], turned[RADIX:]
        middle.append(jnp.concatenate([real * cos_t + imag * sin_t, imag * cos_t - real * sin_t], axis=1))
    middle = jnp.concatenate(middle, axis=0)

    def second(x, table):
        high, low = split(x)
        return dot(jnp.concatenate([high, low, high], axis=1), table[...])

    spectrum = second(middle, ahead_second)
    spectrum = (spectrum.reshape(count, RADIX, 2 * LANES) * gain[...][None]).reshape(count * RADIX, 2 * LANES)
    middle = second(spectrum, back_second)
    cells = []
    for c in range(count):
        real, imag = middle[c * RADIX : (c + 1) * RADIX, :LANES], middle[c * RADIX : (c + 1) * RADIX, LANES:]
        cells.append(jnp.concatenate([real * cos_t - imag * sin_t, imag * cos_t + real * sin_t], axis=0))
    return first_dots(back_first[...], cells)


FILTER_STEP = 32


def filter_into(tables, grid, first, out):
    cells = [grid[first + j].reshape(RADIX, LANES) for j in range(FILTER_STEP)]
    cells = [jnp.concatenate(cells[j : j + 2], axis=0) for j in range(0, FILTER_STEP, 2)]
    for p, turned in enumerate(filter_block(tables, cells)):
        for part in range(2):
            for c in range(8):
                at = part * RADIX + c * 8
                out[c, 2 * p + part] = turned[at : at + 8]


def filter_kernel(*refs):
    filter_into(refs[:7], refs[7], 0, refs[8])


def whole_specs(arrays):
    return [pl.BlockSpec(x.shape, functools.partial(lambda nd, i: (0,) * nd, x.ndim)) for x in arrays]


def filter_cost(blocks):
    return pl.CostEstimate(
        flops=blocks * 3 * 2 * (128 * 128 * 128 + 64 * 256 * 256), bytes_accessed=blocks * 2**16, transcendentals=0
    )


def filter_cycles(grid, tables):
    blocks, columns = grid.shape[:2]
    return pl.pallas_call(
        filter_kernel,
        grid=(blocks // FILTER_STEP,),
        in_specs=whole_specs(tables) + [pl.BlockSpec((FILTER_STEP, columns, 8, LANES), lambda i: (i, 0, 0, 0))],
        out_specs=pl.BlockSpec((columns, FILTER_STEP, 8, LANES), lambda i: (0, i, 0, 0)),
        out_shape=jax.ShapeDtypeStruct((columns, blocks, 8, LANES), f32),
        compiler_params=pltpu.CompilerParams(vmem_limit_bytes=VMEM_LIMIT),
        cost_estimate=filter_cost(blocks),
        name="filter_cycles",
    )(*tables, grid)


COLLECT_STEP = 4
COLLECT_BATCH = 32


def collect_kernel(begins, tile_list, *refs):
    count = len(begins)
    arrived, tables, (out, others) = refs[:count], refs[count : count + 7], refs[count + 7 : count + 9]
    total, given_sem, sem = refs[count + 9 : count + 12]
    given = refs[count + 12 :]
    blocks, _, per_column = tile_list.shape
    cycle_blocks = total.shape[0]
    first = cycle_blocks - others.shape[0]
    stretches = [pl.ds(at, COLLECT_STEP) for at in range(0, blocks, COLLECT_STEP)]
    fetches = [
        [pltpu.make_async_copy(x.at[part], g.at[part], given_sem.at[i, c]) for i, (x, g) in enumerate(zip(arrived, given))]
        for c, part in enumerate(stretches)
    ]
    for fetch in fetches:
        for copy in fetch:
            copy.start()

    def clear(j, carry):
        total[j] = jnp.zeros(total.shape[1:], f32)
        return carry

    lax.fori_loop(0, cycle_blocks, clear, 0, unroll=8)
    for c, fetch in enumerate(fetches):
        for copy in fetch:
            copy.wait()

        def one(d, carry):
            for ref, begin in zip(given, begins):
                extent = ref.shape[1]
                for at in range(0, extent, COLLECT_BATCH):
                    where = []
                    for slot in range(begin + at, begin + min(at + COLLECT_BATCH, extent)):
                        q, k = slot // per_column, slot % per_column
                        where.append((tile_list[d, q, k], q))
                    sums = [total[j, q] + ref[d, at + i] for i, (j, q) in enumerate(where)]
                    for (j, q), x in zip(where, sums):
                        total[j, q] = x
            return carry

        lax.fori_loop(c * COLLECT_STEP, (c + 1) * COLLECT_STEP, one, 0)
    hand_over = pltpu.make_async_copy(total.at[pl.ds(first, others.shape[0])], others, sem)
    hand_over.start()
    filter_into(tables, total, 0, out)
    hand_over.wait()


def collect_and_filter(arrived, begins, tile_list, tables, cycle_blocks):
    blocks, columns, per_column = tile_list.shape
    return pl.pallas_call(
        functools.partial(collect_kernel, begins),
        grid=(1,),
        in_specs=[pl.BlockSpec(memory_space=pltpu.SMEM)]
        + [pl.BlockSpec(memory_space=pl.ANY)] * len(arrived)
        + whole_specs(tables),
        out_specs=[
            pl.BlockSpec((columns, FILTER_STEP, 8, LANES), lambda i: (0, 0, 0, 0)),
            pl.BlockSpec(memory_space=pl.ANY),
        ],
        out_shape=[
            jax.ShapeDtypeStruct((columns, FILTER_STEP, 8, LANES), f32),
            jax.ShapeDtypeStruct((cycle_blocks - FILTER_STEP, columns, 8, LANES), f32),
        ],
        scratch_shapes=[
            pltpu.VMEM((cycle_blocks, columns, 8, LANES), f32),
            pltpu.SemaphoreType.DMA((len(arrived), blocks // COLLECT_STEP)),
            pltpu.SemaphoreType.DMA,
        ]
        + [pltpu.VMEM(x.shape, f32) for x in arrived],
        compiler_params=pltpu.CompilerParams(vmem_limit_bytes=VMEM_LIMIT),
        cost_estimate=filter_cost(FILTER_STEP + 64),
        name="collect_filter",
    )(tile_list, *arrived, *tables)


def gain_table(response):
    full = jnp.concatenate([response, response[-2:0:-1]])
    gain = full.reshape(LANES, RADIX).T * (1.0 / NPHI)
    return jnp.concatenate([gain, gain], axis=1)


SLOT_CHUNKS = (8, 56)
AXES = ("half", "share", "tile")


def after(x, *others):
    return lax.optimization_barrier((x, *others))[0]


def row_owner_plan(values, cycle_taps, phi_taps, cycle_start, phi_start, tile_list, response):
    half, share = lax.axis_index("half"), lax.axis_index("share")
    shares, part_count = lax.axis_size("share"), lax.axis_size("tile")
    blocks, columns, per_column = tile_list.shape
    near_slots = shares * per_column
    cycle_blocks = 256
    points = [x[0] for x in (values, cycle_taps, phi_taps, cycle_start, phi_start)]
    tables = [jnp.asarray(t) for t in dft_tables()] + [gain_table(response)]
    index = share * part_count + lax.axis_index("tile")
    place = jnp.stack(
        [half * (blocks // 2), half * shares + share, index, (1 - half) * shares, half * shares]
    ).astype(jnp.int32)

    def exchange(x, axes):
        return lax.all_to_all(x, axes, 0, 0, tiled=True)

    arrived, begins, at = [], [], 0
    for extent in SLOT_CHUNKS:
        tiles = spread_tiles(points, columns, part_count, at, extent)
        arrived.append(exchange(tiles.reshape(blocks, extent, 8, LANES), AXES))
        begins.append(at)
        at += extent
    early, others = collect_and_filter(arrived, begins, tile_list, tables, cycle_blocks)
    late = filter_cycles(others, tables)

    def pass_on(parts):
        def step(x, axis, size, d):
            return lax.ppermute(x, axis, [(i, i ^ d) for i in range(size)]) if d else x

        here = [step(x, AXES[2], part_count, d) for d, x in enumerate(parts)]
        return [
            step(jnp.stack([x[d] for x in here]), AXES[1], shares, d) for d in range(shares)
        ]

    early_share = exchange(early, AXES[:2])
    far = pick_far([early, late], tile_list)
    late_share = exchange(after(late, early_share), AXES[:2])
    own = pass_on(pick_own([after(early, far), late], place, tile_list, part_count))

    def own_rows(begin, tiles, k):
        step = pl.program_id(0)
        for t in range(part_count):
            for p in range(shares):
                source = begin[1] ^ (p * part_count + t)
                yield t * shares + p, tiles[0][source, step * STEP_SLOTS + k]

    def whole_specs_at(arrays):
        return [pl.BlockSpec(x.shape, functools.partial(lambda nd, i, at: (0,) * nd, x.ndim)) for x in arrays]

    def begin_at(which, upper):
        return jnp.stack([which * shares, index, upper]).astype(jnp.int32)

    own = [jnp.concatenate(own)]
    gradient = read_points(points, begin_at(half, half), near_slots, own, whole_specs_at(own), TR // 2, own_rows, None)
    whole = merge_rows(early_share, 0, cycle_blocks, None)
    far_tiles = exchange(after(far, late_share, gradient, whole), AXES)
    near = list(pick_near([early_share, late_share], place, tile_list))
    for d in range(1, blocks // 2):
        near[d] = lax.ppermute(near[d], AXES[1:], [(i, i ^ d) for i in range(blocks // 2)])

    far_tiles = far_tiles.reshape(columns, part_count, near_slots, 8, LANES)
    far_spec = pl.BlockSpec((columns, part_count, STEP_SLOTS, 8, LANES), lambda i, at: (0, 0, i, 0, 0))

    def far_rows(begin, tiles, k):
        return [(r, tiles[0][r % columns, r // columns, k]) for r in range(TR)]

    def near_rows(begin, tiles, k):
        for t in range(part_count):
            for p in range(shares):
                yield t * shares + p, tiles[t][k, p]

    moved = near[5]
    near = jnp.stack(near)

    def near_spec(t):
        return pl.BlockSpec((None,) + near.shape[1:], lambda i, at: (at[1] ^ (i * part_count + t), 0, 0, 0, 0))

    near_specs = [near_spec(t) for t in range(part_count)]
    gradient = read_points(
        points, begin_at(half, 1 - half), near_slots, [near] * part_count, near_specs, TR // 2, near_rows, gradient
    )
    gradient = read_points(points, begin_at(1 - half, half), near_slots, [far_tiles], [far_spec], TR, far_rows, gradient)
    whole = merge_rows(after(late_share, moved), FILTER_STEP, cycle_blocks, whole)
    return whole, gradient[None]


precise = lax.Precision.HIGHEST


def contract(formula, lhs_array, rhs_array):
    return jnp.einsum(formula, lhs_array, rhs_array, precision=precise)


def spread_matrix(weights, starts, extent):
    offsets = lax.broadcasted_iota(jnp.int32, (1, 1, extent), 2) - starts[:, :, None]
    result = jnp.zeros(starts.shape + (extent,), jnp.float32)
    for tap_index in range(weights.shape[1]):
        result = result + jnp.where(offsets == tap_index, weights[:, tap_index, :, None], 0.0)
    return result


def angle_table(rows_count, cols_count, modulus):
    left_index = lax.broadcasted_iota(jnp.int32, (rows_count, cols_count), 0)
    right_index = lax.broadcasted_iota(jnp.int32, (rows_count, cols_count), 1)
    phase_int = left_index * right_index % modulus
    angles = phase_int.astype(jnp.float32) * (2.0 * math.pi / modulus)
    return (jnp.cos(angles), jnp.sin(angles))


def filter_by_einsum(cycle_rows, response):
    length = cycle_rows.shape[-1]
    second = length // RADIX
    cos_first, sin_first = angle_table(RADIX, RADIX, RADIX)
    cos_twist, sin_twist = angle_table(RADIX, second, length)
    cos_second, sin_second = angle_table(second, second, second)
    blocks = cycle_rows.reshape(cycle_rows.shape[:2] + (RADIX, second))
    real_one = contract("giab,ak->gikb", blocks, cos_first)
    imag_one = -contract("giab,ak->gikb", blocks, sin_first)
    real_two = real_one * cos_twist + imag_one * sin_twist
    imag_two = imag_one * cos_twist - real_one * sin_twist
    real_freq = contract("gikb,bm->gikm", real_two, cos_second) + contract(
        "gikb,bm->gikm", imag_two, sin_second
    )
    imag_freq = contract("gikb,bm->gikm", imag_two, cos_second) - contract(
        "gikb,bm->gikm", real_two, sin_second
    )
    full_response = jnp.concatenate([response, response[-2:0:-1]])
    gain_table = full_response.reshape(second, RADIX).T
    real_freq = real_freq * gain_table
    imag_freq = imag_freq * gain_table
    real_back = contract("gikm,bm->gikb", real_freq, cos_second) - contract(
        "gikm,bm->gikb", imag_freq, sin_second
    )
    imag_back = contract("gikm,bm->gikb", imag_freq, cos_second) + contract(
        "gikm,bm->gikb", real_freq, sin_second
    )
    real_turn = real_back * cos_twist - imag_back * sin_twist
    imag_turn = imag_back * cos_twist + real_back * sin_twist
    spatial = contract("gikb,ka->giab", real_turn, cos_first) - contract(
        "gikb,ka->giab", imag_turn, sin_first
    )
    return (spatial / length).reshape(cycle_rows.shape)


def accumulate(arrived, wanted, cycle_blocks):
    selector = (
        lax.broadcasted_iota(jnp.int32, (cycle_blocks, wanted.size), 0) == wanted.reshape(1, -1)
    ).astype(jnp.float32)
    flattened = arrived.reshape(wanted.size, -1)
    return jnp.dot(selector, flattened, precision=precise).reshape(
        (cycle_blocks,) + arrived.shape[2:]
    )


def column_owner_plan(values, cycle_taps, phi_taps, cycle_start, phi_start, tile_list, response):
    columns = lax.axis_size("pts")
    part_count = lax.axis_size("tile")
    column = lax.axis_index("pts")
    per_column = values.shape[1] // columns
    tile_width = NPHI // columns
    cycle_part = TR // part_count
    cycle_weights = spread_matrix(cycle_taps[0], cycle_start[0], TR)
    phi_weights = spread_matrix(phi_taps[0], phi_start[0], tile_width)
    loaded = cycle_weights * values[0][:, :, None]
    cycle_split = cycle_weights.reshape(columns, per_column, values.shape[2], part_count, cycle_part)
    loaded_split = loaded.reshape(columns, per_column, values.shape[2], part_count, cycle_part)
    phi_split = phi_weights.reshape(columns, per_column, values.shape[2], tile_width)
    partial_value = contract("qkitr,qkic->qtkrc", loaded_split, phi_split)
    partial_value = partial_value.reshape(columns * part_count, per_column, cycle_part, tile_width)
    arrived = lax.all_to_all(
        partial_value, ("pts", "tile"), split_axis=0, concat_axis=0, tiled=True
    )
    wanted = lax.dynamic_index_in_dim(tile_list, column, 1, keepdims=False)
    owned_tiles = accumulate(arrived, wanted, 256)
    whole_cycles = filter_by_einsum(
        lax.all_to_all(owned_tiles, "pts", split_axis=0, concat_axis=2, tiled=True), response
    )
    filtered = lax.all_to_all(whole_cycles, "pts", split_axis=2, concat_axis=0, tiled=True)
    picked = jnp.take(filtered, wanted.reshape(-1), axis=0)
    picked = picked.reshape(columns * part_count, per_column, cycle_part, tile_width)
    returned = lax.all_to_all(picked, ("pts", "tile"), split_axis=0, concat_axis=0, tiled=True)
    returned = returned.reshape(columns, part_count, per_column, cycle_part, tile_width)
    rows_read = contract("qkitr,qtkrc->qkic", cycle_split, returned)
    gradient = jnp.sum(rows_read * phi_split, axis=-1).reshape(values.shape[1], values.shape[2])
    return (filtered, gradient[None])


def solution(mesh):
    columns, part_count = mesh.shape["pts"], mesh.shape["tile"]
    step, pts, tile = column_owner_plan, "pts", "tile"
    if columns * part_count == TR and columns % 2 == 0 and NPHI // columns == GROUPS * LANES:
        mesh = Mesh(mesh.devices.reshape(2, columns // 2, part_count), AXES)
        step, pts = row_owner_plan, ("half", "share")
    block = (pts, tile) if pts == "pts" else AXES
    return jax.shard_map(
        step,
        mesh=mesh,
        in_specs=(
            P(block, None, None),
            P(block, None, None, None),
            P(block, None, None, None),
            P(block, None, None),
            P(block, None, None),
            P(),
            P(),
        ),
        out_specs=(P(None, tile, pts), P(block, None, None)),
        check_vma=False,
    )
```

```python
import functools
import math

import jax
import jax.numpy as jnp
import numpy as np
from jax import lax
from jax.experimental import pallas as pl
from jax.experimental.pallas import tpu as pltpu
from jax.sharding import Mesh
from jax.sharding import PartitionSpec as P

NPHI = 8192
TR = 32
TAPS = 8
LANES = 128
GROUPS = 8
RADIX = 64
STEP_SLOTS = 8
VMEM_LIMIT = 60 * 1024 * 1024

f32 = jnp.float32
bf16 = jnp.bfloat16


def split(x):
    high = x.astype(bf16)
    low = (x - high.astype(f32)).astype(bf16)
    return high, low


def split_f32(x):
    high = x.astype(bf16).astype(f32)
    return high, x - high


def shifted_window(taps, shift):
    n = taps.shape[1]
    window = jnp.concatenate([taps, jnp.zeros((8, n), f32)], axis=0)
    both = jnp.concatenate([shift, shift], axis=0)
    for bit in (1, 2, 4):
        moved = pltpu.roll(window, bit, 0)
        window = jnp.where((both & bit) != 0, moved, window)
    return window[:8], window[8:]


def twice(x):
    return jnp.concatenate([x, x], axis=0)


def half_rows(groups, upper):
    first = lax.broadcasted_iota(jnp.int32, groups[0].shape, 0) < 4
    merged = []
    for at in range(0, len(groups), 2):
        left, right = groups[at : at + 2]
        lower = jnp.where(first, left, pltpu.roll(right, 4, 0))
        merged.append(jnp.where(upper, jnp.where(first, pltpu.roll(left, 4, 0), right), lower))
    return merged


def cycle_factor(taps, cycle_start, phi_start, upper=None):
    first, second = shifted_window(taps, cycle_start & 7)
    block = cycle_start >> 3
    rows = []
    for h in range(TR // 8):
        rows.append(jnp.where(block == h, first, jnp.where(block == h - 1, second, 0.0)))
    if upper is not None:
        rows = half_rows(rows, upper)
    group = twice((phi_start >> 7).astype(f32)).astype(bf16)
    masks = [group == g for g in range(GROUPS)]
    zero = jnp.zeros(group.shape, bf16)
    parts = []
    for part in split(jnp.concatenate(rows, axis=0)):
        pieces = []
        for mask in masks:
            pieces += [jnp.where(mask, part[at : at + 16], zero) for at in range(0, part.shape[0], 16)]
        parts.append(jnp.concatenate(pieces, axis=0))
    return parts


def phi_factor(taps, phi_start):
    first, second = shifted_window(taps, phi_start & 7)
    odd = (phi_start & 8) != 0
    zero = jnp.zeros(first.shape, f32)
    near = jnp.concatenate([jnp.where(odd, zero, first), jnp.where(odd, first, second)], axis=0)
    far = jnp.concatenate([jnp.where(odd, second, zero), zero], axis=0)
    block = twice(((phi_start & 127) >> 4).astype(f32)).astype(bf16)
    masks = [block == h for h in range(8)]
    zero = jnp.zeros(block.shape, bf16)
    parts = []
    for low, high in zip(split(near), split(far)):
        pieces = [jnp.where(masks[0], low, zero)]
        for h in range(1, 8):
            pieces.append(jnp.where(masks[h], low, jnp.where(masks[h - 1], high, zero)))
        pieces.append(jnp.where(masks[7], high, zero))
        parts.append(jnp.concatenate(pieces, axis=0))
    return parts


def rows_dot(lhs, rhs):
    return lax.dot_general(lhs, rhs, (((1,), (1,)), ((), ())), preferred_element_type=f32)


def spread_kernel(values, cycle_taps, phi_taps, cycle_start, phi_start, out, turn):
    n = values.shape[1]
    shares, parts, rows = out.shape[:3]
    for k in range(STEP_SLOTS):
        cycle_at = jnp.broadcast_to(cycle_start[k : k + 1, :], (8, n))
        phi_at = jnp.broadcast_to(phi_start[k : k + 1, :], (8, n))
        loaded = cycle_taps[k] * values[k : k + 1, :]
        left_high, left_low = cycle_factor(loaded, cycle_at, phi_at)
        empty = jnp.zeros((256 - 144, n), bf16)
        right_high, right_low = [jnp.concatenate([x, empty], axis=0) for x in phi_factor(phi_taps[k], phi_at)]
        product = rows_dot(jnp.concatenate([left_high, left_low], axis=0), right_high)
        product = product[: TR * GROUPS] + product[TR * GROUPS :] + rows_dot(left_high, right_low)
        for g in range(GROUPS):
            tile = product[g * TR : (g + 1) * TR, :LANES]
            if g:
                tile = tile + product[(g - 1) * TR : g * TR, LANES:]
            for at in range(0, TR, 8):
                turn[k, pl.ds(at * GROUPS + g, 8, stride=GROUPS), :] = tile[at : at + 8]
        for r in range(TR):
            t, p, row = r // (shares * rows), r // rows % shares, r % rows
            out[p, t, row, k] = turn[k, r * GROUPS : (r + 1) * GROUPS, :]


def point_specs(place, n):
    flat = pl.BlockSpec((STEP_SLOTS, n), lambda *at: (place(*at), 0))
    taps = pl.BlockSpec((STEP_SLOTS, TAPS, n), lambda *at: (place(*at), 0, 0))
    return [flat, taps, taps, flat, flat]


def spread_tiles(points, shares, part_count, first, slots):
    n = points[0].shape[1]
    begin = first // STEP_SLOTS
    heads = (shares, part_count, TR // (shares * part_count))
    return pl.pallas_call(
        spread_kernel,
        grid=(slots // STEP_SLOTS,),
        in_specs=point_specs(lambda i: begin + i, n),
        out_specs=pl.BlockSpec(heads + (STEP_SLOTS, 8, LANES), lambda i: (0, 0, 0, i, 0, 0)),
        out_shape=jax.ShapeDtypeStruct(heads + (slots, 8, LANES), f32),
        scratch_shapes=[pltpu.VMEM((STEP_SLOTS, TR * GROUPS, LANES), f32)],
        compiler_params=pltpu.CompilerParams(vmem_limit_bytes=VMEM_LIMIT),
        cost_estimate=pl.CostEstimate(
            flops=slots * 2 * 3 * 256 * 256 * n, bytes_accessed=slots * (19 + 32) * n * 4, transcendentals=0
        ),
        name="spread",
    )(*points)


def read_kernel(count, cycles, place_rows, begin, cycle_taps, phi_taps, cycle_start, phi_start, *rest):
    tiles, so_far, (out, turn) = rest[:count], rest[count:-2], rest[-2:]
    n = cycle_start.shape[1]
    upper = None if cycles == TR else begin[2] != 0
    for k in range(STEP_SLOTS):
        cycle_at = jnp.broadcast_to(cycle_start[k : k + 1, :], (8, n))
        phi_at = jnp.broadcast_to(phi_start[k : k + 1, :], (8, n))
        right_high, right_low = cycle_factor(cycle_taps[k], cycle_at, phi_at, upper)
        for r, row in place_rows(begin, tiles, k):
            turn[k, r * GROUPS : (r + 1) * GROUPS, :] = row
        pieces = [
            turn[k, pl.ds(at * GROUPS + g, 8, stride=GROUPS), :] for g in range(GROUPS) for at in range(0, cycles, 8)
        ]
        tile = jnp.concatenate(pieces, axis=0).T
        following = pltpu.roll(tile[:16], cycles * (GROUPS - 1), 1)
        left_high, left_low = split(jnp.concatenate([tile, following], axis=0))
        picked = dot(left_high, right_high) + dot(left_low, right_high) + dot(left_high, right_low)
        lane = phi_at & 127
        first, second = shifted_window(phi_taps[k], lane & 7)
        block = lane >> 3
        low = picked[:8]
        high = picked[8:16]
        for h in range(1, 16):
            here = block == h
            low = jnp.where(here, picked[h * 8 : h * 8 + 8], low)
            high = jnp.where(here, picked[h * 8 + 8 : h * 8 + 16], high)
        result = jnp.sum(low * first + high * second, axis=0, keepdims=True)
        if so_far and cycles < TR:
            result = result + so_far[0][k : k + 1, :]
        out[k : k + 1, :] = result


def read_points(points, begin, slots, tiles, tile_specs, cycles, place_rows, so_far):
    total, n = points[0].shape
    given = [] if so_far is None else [so_far]
    specs = point_specs(lambda i, at: at[0] + i, n)
    given_spec = pl.BlockSpec(memory_space=pl.ANY) if cycles == TR else specs[0]
    return pl.pallas_call(
        functools.partial(read_kernel, len(tile_specs), cycles, place_rows),
        grid_spec=pltpu.PrefetchScalarGridSpec(
            num_scalar_prefetch=1,
            grid=(slots // STEP_SLOTS,),
            in_specs=specs[1:] + tile_specs + [given_spec] * len(given),
            out_specs=specs[0],
            scratch_shapes=[pltpu.VMEM((STEP_SLOTS, cycles * GROUPS, LANES), f32)],
        ),
        out_shape=jax.ShapeDtypeStruct((total, n), f32),
        input_output_aliases={5 + len(tile_specs): 0} if given else {},
        compiler_params=pltpu.CompilerParams(vmem_limit_bytes=VMEM_LIMIT),
        cost_estimate=pl.CostEstimate(
            flops=slots * 2 * 3 * 256 * 8 * cycles * n, bytes_accessed=slots * (19 + cycles) * n * 4, transcendentals=0
        ),
        name="read_back",
    )(begin, *points[1:], *tiles, *given)


def pick_far_kernel(tile_list, *refs):
    filtered, out = refs[:-1], refs[-1]
    step = pl.program_id(0)
    blocks, columns, per_column = tile_list.shape
    first = filtered[0].shape[1]

    def one(d, carry):
        block = step * out.shape[0] + d
        other = (1 - block // (blocks // 2)) * (columns // 2)
        for c in range(columns // 2):
            for k in range(per_column):
                j = tile_list[block, other + c, k]
                early = filtered[0][other + c, jnp.minimum(j, first - 1)]
                late = filtered[1][other + c, jnp.maximum(j - first, 0)]
                out[d, c * per_column + k] = jnp.where(j < first, early, late)
        return carry

    lax.fori_loop(0, out.shape[0], one, 0)


def pick_far(filtered, tile_list):
    blocks, columns, per_column = tile_list.shape
    shape = (blocks, columns // 2 * per_column, 8, LANES)
    step = 4
    return pl.pallas_call(
        pick_far_kernel,
        grid=(blocks // step,),
        in_specs=[pl.BlockSpec(memory_space=pltpu.SMEM)]
        + [pl.BlockSpec(part.shape, lambda i: (0, 0, 0, 0)) for part in filtered],
        out_specs=pl.BlockSpec((step,) + shape[1:], lambda i: (i, 0, 0, 0)),
        out_shape=jax.ShapeDtypeStruct(shape, f32),
        compiler_params=pltpu.CompilerParams(vmem_limit_bytes=VMEM_LIMIT),
        cost_estimate=pl.CostEstimate(flops=0, bytes_accessed=12 * 2**20, transcendentals=0),
        name="pick_far",
    )(tile_list, *filtered)


def outs_by_device(outs):
    return [(out, share) for share in range(outs[0].shape[0]) for out in outs]


def pick_own_kernel(place, tile_list, *refs):
    filtered, outs = refs[:2], refs[2:]
    columns, per_column = tile_list.shape[1:]
    first = filtered[0].shape[1]

    for d, (out, share) in enumerate(outs_by_device(outs)):
        block = place[0] + (place[2] ^ d)

        def one(c, carry):
            column = place[4] + c
            for k in range(per_column):
                j = tile_list[block, column, k]
                inside, beyond = jnp.minimum(j, first - 1), jnp.maximum(j - first, 0)
                tile = jnp.where(j < first, filtered[0][column, inside], filtered[1][column, beyond])
                out[share, c * per_column + k] = tile
            return carry

        lax.fori_loop(0, columns // 2, one, 0)


def pick_own(filtered, place, tile_list, part_count):
    blocks, columns, per_column = tile_list.shape
    shape = (blocks // 2 // part_count, columns // 2 * per_column, 8, LANES)
    return pl.pallas_call(
        pick_own_kernel,
        grid=(1,),
        in_specs=[pl.BlockSpec(memory_space=pltpu.SMEM)] * 2
        + [pl.BlockSpec(part.shape, lambda i: (0, 0, 0, 0)) for part in filtered],
        out_specs=[pl.BlockSpec(shape, lambda i: (0, 0, 0, 0))] * part_count,
        out_shape=[jax.ShapeDtypeStruct(shape, f32)] * part_count,
        compiler_params=pltpu.CompilerParams(vmem_limit_bytes=VMEM_LIMIT),
        cost_estimate=pl.CostEstimate(flops=0, bytes_accessed=10 * 2**20, transcendentals=0),
        name="pick_own",
    )(place, tile_list, *filtered)


def pick_near_kernel(place, tile_list, *refs):
    shares, outs = refs[:2], refs[2:]
    per_column = tile_list.shape[2]
    first = shares[0].shape[1]
    rows = outs[0].shape[1]

    for d, out in enumerate(outs):
        block = place[0] + (place[2] ^ d)

        def one(k, carry):
            j = tile_list[block, place[1], k]
            inside, beyond = jnp.minimum(j, first - 1), jnp.maximum(j - first, 0)
            for row in range(rows):
                at = place[3] + row
                out[k, row] = jnp.where(j < first, shares[0][at, inside], shares[1][at, beyond])
            return carry

        lax.fori_loop(0, per_column, one, 0)


def pick_near(shares, place, tile_list):
    blocks, columns, per_column = tile_list.shape
    shape = (per_column, shares[0].shape[0] // 2, 8, LANES)
    return pl.pallas_call(
        pick_near_kernel,
        grid=(1,),
        in_specs=[pl.BlockSpec(memory_space=pltpu.SMEM)] * 2
        + [pl.BlockSpec(part.shape, lambda i: (0, 0, 0, 0)) for part in shares],
        out_specs=[pl.BlockSpec(shape, lambda i: (0, 0, 0, 0))] * (blocks // 2),
        out_shape=[jax.ShapeDtypeStruct(shape, f32)] * (blocks // 2),
        compiler_params=pltpu.CompilerParams(vmem_limit_bytes=VMEM_LIMIT),
        cost_estimate=pl.CostEstimate(flops=0, bytes_accessed=12 * 2**20, transcendentals=0),
        name="pick_near",
    )(place, tile_list, *shares)


def merge_kernel(arrived, *rest):
    out = rest[-1]
    rows, blocks = arrived.shape[:2]
    for c in range(8):
        for j in range(blocks):
            out[j, :, c * LANES : (c + 1) * LANES] = arrived[:, j, c, :]


def merge_rows(arrived, first, cycle_blocks, so_far):
    rows, blocks = arrived.shape[:2]
    step = 32
    begin = first // step
    given = [] if so_far is None else [so_far]
    return pl.pallas_call(
        merge_kernel,
        grid=(blocks // step,),
        in_specs=[pl.BlockSpec((rows, step, 8, LANES), lambda i: (0, i, 0, 0))]
        + [pl.BlockSpec(memory_space=pl.ANY)] * len(given),
        out_specs=pl.BlockSpec((step, rows, 8 * LANES), lambda i: (begin + i, 0, 0)),
        out_shape=jax.ShapeDtypeStruct((cycle_blocks, rows, 8 * LANES), f32),
        input_output_aliases={1: 0} if given else {},
        compiler_params=pltpu.CompilerParams(vmem_limit_bytes=VMEM_LIMIT),
        cost_estimate=pl.CostEstimate(flops=0, bytes_accessed=8 * blocks * rows * 1024, transcendentals=0),
        name="merge_rows",
    )(arrived, *given)


@functools.cache
def dft_tables():
    a = np.arange(RADIX)
    b = np.arange(LANES)
    first = 2.0 * np.pi / RADIX * (np.outer(a, a) % RADIX)
    twist = 2.0 * np.pi / NPHI * np.outer(a, b)
    second = 2.0 * np.pi / LANES * (np.outer(b, b) % LANES)
    c1, s1, c2, s2 = np.cos(first), np.sin(first), np.cos(second), np.sin(second)
    ahead_first = np.block([[c1, s1], [-s1, c1]])
    back_first = np.block([[c1, -s1], [s1, c1]])
    ahead_second = np.block([[c2, -s2], [s2, c2]])
    back_second = np.block([[c2, s2], [-s2, c2]])

    def pair(table):
        high = np.asarray(table, np.float32).astype(bf16)
        low = (table - high.astype(np.float64)).astype(np.float32).astype(bf16)
        return high, low

    def wide(table):
        high, low = pair(table)
        return np.concatenate([high, high, low], axis=1)

    def stacked(table):
        high, low = pair(table)
        return np.concatenate([high, high, low], axis=0)

    return (
        wide(ahead_first),
        wide(back_first),
        stacked(ahead_second),
        stacked(back_second),
        np.cos(twist).astype(np.float32),
        np.sin(twist).astype(np.float32),
    )


def dot(lhs, rhs):
    return lax.dot_general(lhs, rhs, (((1,), (0,)), ((), ())), preferred_element_type=f32)


def first_dots(table, cells):
    turned = []
    for at in range(0, len(cells), 2):
        high, low = split(jnp.concatenate(cells[at : at + 2], axis=1))
        both = dot(table, jnp.concatenate([high, low, high], axis=0))
        turned += [both[:, :LANES], both[:, LANES:]]
    return turned


def filter_block(tables, cells):
    ahead_first, back_first, ahead_second, back_second, cos_twist, sin_twist, gain = tables
    count = len(cells)
    cos_t, sin_t = cos_twist[...], sin_twist[...]
    middle = []
    for turned in first_dots(ahead_first[...], cells):
        real, imag = turned[:RADIX], turned[RADIX:]
        middle.append(jnp.concatenate([real * cos_t + imag * sin_t, imag * cos_t - real * sin_t], axis=1))
    middle = jnp.concatenate(middle, axis=0)

    def second(x, table):
        high, low = split(x)
        return dot(jnp.concatenate([high, low, high], axis=1), table[...])

    spectrum = second(middle, ahead_second)
    spectrum = (spectrum.reshape(count, RADIX, 2 * LANES) * gain[...][None]).reshape(count * RADIX, 2 * LANES)
    middle = second(spectrum, back_second)
    cells = []
    for c in range(count):
        real, imag = middle[c * RADIX : (c + 1) * RADIX, :LANES], middle[c * RADIX : (c + 1) * RADIX, LANES:]
        cells.append(jnp.concatenate([real * cos_t - imag * sin_t, imag * cos_t + real * sin_t], axis=0))
    return first_dots(back_first[...], cells)


FILTER_STEP = 32


def filter_into(tables, grid, first, out):
    cells = [grid[first + j].reshape(RADIX, LANES) for j in range(FILTER_STEP)]
    cells = [jnp.concatenate(cells[j : j + 2], axis=0) for j in range(0, FILTER_STEP, 2)]
    for p, turned in enumerate(filter_block(tables, cells)):
        for part in range(2):
            for c in range(8):
                at = part * RADIX + c * 8
                out[c, 2 * p + part] = turned[at : at + 8]


def filter_kernel(*refs):
    filter_into(refs[:7], refs[7], 0, refs[8])


def whole_specs(arrays):
    return [pl.BlockSpec(x.shape, functools.partial(lambda nd, i: (0,) * nd, x.ndim)) for x in arrays]


def filter_cost(blocks):
    return pl.CostEstimate(
        flops=blocks * 3 * 2 * (128 * 128 * 128 + 64 * 256 * 256), bytes_accessed=blocks * 2**16, transcendentals=0
    )


def filter_cycles(grid, tables):
    blocks, columns = grid.shape[:2]
    return pl.pallas_call(
        filter_kernel,
        grid=(blocks // FILTER_STEP,),
        in_specs=whole_specs(tables) + [pl.BlockSpec((FILTER_STEP, columns, 8, LANES), lambda i: (i, 0, 0, 0))],
        out_specs=pl.BlockSpec((columns, FILTER_STEP, 8, LANES), lambda i: (0, i, 0, 0)),
        out_shape=jax.ShapeDtypeStruct((columns, blocks, 8, LANES), f32),
        compiler_params=pltpu.CompilerParams(vmem_limit_bytes=VMEM_LIMIT),
        cost_estimate=filter_cost(blocks),
        name="filter_cycles",
    )(*tables, grid)


COLLECT_STEP = 4
COLLECT_BATCH = 32


def collect_kernel(begins, tile_list, *refs):
    count = len(begins)
    arrived, tables, (out, others) = refs[:count], refs[count : count + 7], refs[count + 7 : count + 9]
    total, given_sem, sem = refs[count + 9 : count + 12]
    given = refs[count + 12 :]
    blocks, _, per_column = tile_list.shape
    cycle_blocks = total.shape[0]
    first = cycle_blocks - others.shape[0]
    stretches = [pl.ds(at, COLLECT_STEP) for at in range(0, blocks, COLLECT_STEP)]
    fetches = [
        [pltpu.make_async_copy(x.at[part], g.at[part], given_sem.at[i, c]) for i, (x, g) in enumerate(zip(arrived, given))]
        for c, part in enumerate(stretches)
    ]
    for fetch in fetches:
        for copy in fetch:
            copy.start()

    def clear(j, carry):
        total[j] = jnp.zeros(total.shape[1:], f32)
        return carry

    lax.fori_loop(0, cycle_blocks, clear, 0, unroll=8)
    for c, fetch in enumerate(fetches):
        for copy in fetch:
            copy.wait()

        def one(d, carry):
            for ref, begin in zip(given, begins):
                extent = ref.shape[1]
                for at in range(0, extent, COLLECT_BATCH):
                    where = []
                    for slot in range(begin + at, begin + min(at + COLLECT_BATCH, extent)):
                        q, k = slot // per_column, slot % per_column
                        where.append((tile_list[d, q, k], q))
                    sums = [total[j, q] + ref[d, at + i] for i, (j, q) in enumerate(where)]
                    for (j, q), x in zip(where, sums):
                        total[j, q] = x
            return carry

        lax.fori_loop(c * COLLECT_STEP, (c + 1) * COLLECT_STEP, one, 0)
    hand_over = pltpu.make_async_copy(total.at[pl.ds(first, others.shape[0])], others, sem)
    hand_over.start()
    filter_into(tables, total, 0, out)
    hand_over.wait()


def collect_and_filter(arrived, begins, tile_list, tables, cycle_blocks):
    blocks, columns, per_column = tile_list.shape
    return pl.pallas_call(
        functools.partial(collect_kernel, begins),
        grid=(1,),
        in_specs=[pl.BlockSpec(memory_space=pltpu.SMEM)]
        + [pl.BlockSpec(memory_space=pl.ANY)] * len(arrived)
        + whole_specs(tables),
        out_specs=[
            pl.BlockSpec((columns, FILTER_STEP, 8, LANES), lambda i: (0, 0, 0, 0)),
            pl.BlockSpec(memory_space=pl.ANY),
        ],
        out_shape=[
            jax.ShapeDtypeStruct((columns, FILTER_STEP, 8, LANES), f32),
            jax.ShapeDtypeStruct((cycle_blocks - FILTER_STEP, columns, 8, LANES), f32),
        ],
        scratch_shapes=[
            pltpu.VMEM((cycle_blocks, columns, 8, LANES), f32),
            pltpu.SemaphoreType.DMA((len(arrived), blocks // COLLECT_STEP)),
            pltpu.SemaphoreType.DMA,
        ]
        + [pltpu.VMEM(x.shape, f32) for x in arrived],
        compiler_params=pltpu.CompilerParams(vmem_limit_bytes=VMEM_LIMIT),
        cost_estimate=filter_cost(FILTER_STEP + 64),
        name="collect_filter",
    )(tile_list, *arrived, *tables)


def gain_table(response):
    full = jnp.concatenate([response, response[-2:0:-1]])
    gain = full.reshape(LANES, RADIX).T * (1.0 / NPHI)
    return jnp.concatenate([gain, gain], axis=1)


SLOT_CHUNKS = (8, 56)
AXES = ("half", "share", "tile")


def after(x, *others):
    return lax.optimization_barrier((x, *others))[0]


def row_owner_plan(values, cycle_taps, phi_taps, cycle_start, phi_start, tile_list, response):
    half, share = lax.axis_index("half"), lax.axis_index("share")
    shares, part_count = lax.axis_size("share"), lax.axis_size("tile")
    blocks, columns, per_column = tile_list.shape
    near_slots = shares * per_column
    cycle_blocks = 256
    points = [x[0] for x in (values, cycle_taps, phi_taps, cycle_start, phi_start)]
    tables = [jnp.asarray(t) for t in dft_tables()] + [gain_table(response)]
    index = share * part_count + lax.axis_index("tile")
    place = jnp.stack(
        [half * (blocks // 2), half * shares + share, index, (1 - half) * shares, half * shares]
    ).astype(jnp.int32)

    def exchange(x, axes):
        return lax.all_to_all(x, axes, 0, 0, tiled=True)

    arrived, begins, at = [], [], 0
    for extent in SLOT_CHUNKS:
        tiles = spread_tiles(points, columns, part_count, at, extent)
        arrived.append(exchange(tiles.reshape(blocks, extent, 8, LANES), AXES))
        begins.append(at)
        at += extent
    early, others = collect_and_filter(arrived, begins, tile_list, tables, cycle_blocks)
    late = filter_cycles(others, tables)

    def pass_on(parts):
        def step(x, axis, size, d):
            return lax.ppermute(x, axis, [(i, i ^ d) for i in range(size)]) if d else x

        here = [step(x, AXES[2], part_count, d) for d, x in enumerate(parts)]
        return [
            step(jnp.stack([x[d] for x in here]), AXES[1], shares, d) for d in range(shares)
        ]

    early_share = exchange(early, AXES[:2])
    far = pick_far([early, late], tile_list)
    late_share = exchange(after(late, early_share), AXES[:2])
    own = pass_on(pick_own([after(early, far), late], place, tile_list, part_count))

    def own_rows(begin, tiles, k):
        step = pl.program_id(0)
        for t in range(part_count):
            for p in range(shares):
                source = begin[1] ^ (p * part_count + t)
                yield t * shares + p, tiles[0][source, step * STEP_SLOTS + k]

    def whole_specs_at(arrays):
        return [pl.BlockSpec(x.shape, functools.partial(lambda nd, i, at: (0,) * nd, x.ndim)) for x in arrays]

    def begin_at(which, upper):
        return jnp.stack([which * shares, index, upper]).astype(jnp.int32)

    own = [jnp.concatenate(own)]
    gradient = read_points(points, begin_at(half, half), near_slots, own, whole_specs_at(own), TR // 2, own_rows, None)
    whole = merge_rows(early_share, 0, cycle_blocks, None)
    far_tiles = exchange(after(far, late_share, gradient), AXES)
    near = list(pick_near([early_share, late_share], place, tile_list))
    for d in range(1, blocks // 2):
        near[d] = lax.ppermute(near[d], AXES[1:], [(i, i ^ d) for i in range(blocks // 2)])

    far_tiles = far_tiles.reshape(columns, part_count, near_slots, 8, LANES)
    far_spec = pl.BlockSpec((columns, part_count, STEP_SLOTS, 8, LANES), lambda i, at: (0, 0, i, 0, 0))

    def far_rows(begin, tiles, k):
        return [(r, tiles[0][r % columns, r // columns, k]) for r in range(TR)]

    def near_rows(begin, tiles, k):
        for t in range(part_count):
            for p in range(shares):
                yield t * shares + p, tiles[t][k, p]

    moved = near[5]
    near = jnp.stack(near)

    def near_spec(t):
        return pl.BlockSpec((None,) + near.shape[1:], lambda i, at: (at[1] ^ (i * part_count + t), 0, 0, 0, 0))

    near_specs = [near_spec(t) for t in range(part_count)]
    gradient = read_points(
        points, begin_at(half, 1 - half), near_slots, [near] * part_count, near_specs, TR // 2, near_rows, gradient
    )
    gradient = read_points(points, begin_at(1 - half, half), near_slots, [far_tiles], [far_spec], TR, far_rows, gradient)
    whole = merge_rows(after(late_share, moved), FILTER_STEP, cycle_blocks, whole)
    return whole, gradient[None]


precise = lax.Precision.HIGHEST


def contract(formula, lhs_array, rhs_array):
    return jnp.einsum(formula, lhs_array, rhs_array, precision=precise)


def spread_matrix(weights, starts, extent):
    offsets = lax.broadcasted_iota(jnp.int32, (1, 1, extent), 2) - starts[:, :, None]
    result = jnp.zeros(starts.shape + (extent,), jnp.float32)
    for tap_index in range(weights.shape[1]):
        result = result + jnp.where(offsets == tap_index, weights[:, tap_index, :, None], 0.0)
    return result


def angle_table(rows_count, cols_count, modulus):
    left_index = lax.broadcasted_iota(jnp.int32, (rows_count, cols_count), 0)
    right_index = lax.broadcasted_iota(jnp.int32, (rows_count, cols_count), 1)
    phase_int = left_index * right_index % modulus
    angles = phase_int.astype(jnp.float32) * (2.0 * math.pi / modulus)
    return (jnp.cos(angles), jnp.sin(angles))


def filter_by_einsum(cycle_rows, response):
    length = cycle_rows.shape[-1]
    second = length // RADIX
    cos_first, sin_first = angle_table(RADIX, RADIX, RADIX)
    cos_twist, sin_twist = angle_table(RADIX, second, length)
    cos_second, sin_second = angle_table(second, second, second)
    blocks = cycle_rows.reshape(cycle_rows.shape[:2] + (RADIX, second))
    real_one = contract("giab,ak->gikb", blocks, cos_first)
    imag_one = -contract("giab,ak->gikb", blocks, sin_first)
    real_two = real_one * cos_twist + imag_one * sin_twist
    imag_two = imag_one * cos_twist - real_one * sin_twist
    real_freq = contract("gikb,bm->gikm", real_two, cos_second) + contract(
        "gikb,bm->gikm", imag_two, sin_second
    )
    imag_freq = contract("gikb,bm->gikm", imag_two, cos_second) - contract(
        "gikb,bm->gikm", real_two, sin_second
    )
    full_response = jnp.concatenate([response, response[-2:0:-1]])
    gain_table = full_response.reshape(second, RADIX).T
    real_freq = real_freq * gain_table
    imag_freq = imag_freq * gain_table
    real_back = contract("gikm,bm->gikb", real_freq, cos_second) - contract(
        "gikm,bm->gikb", imag_freq, sin_second
    )
    imag_back = contract("gikm,bm->gikb", imag_freq, cos_second) + contract(
        "gikm,bm->gikb", real_freq, sin_second
    )
    real_turn = real_back * cos_twist - imag_back * sin_twist
    imag_turn = imag_back * cos_twist + real_back * sin_twist
    spatial = contract("gikb,ka->giab", real_turn, cos_first) - contract(
        "gikb,ka->giab", imag_turn, sin_first
    )
    return (spatial / length).reshape(cycle_rows.shape)


def accumulate(arrived, wanted, cycle_blocks):
    selector = (
        lax.broadcasted_iota(jnp.int32, (cycle_blocks, wanted.size), 0) == wanted.reshape(1, -1)
    ).astype(jnp.float32)
    flattened = arrived.reshape(wanted.size, -1)
    return jnp.dot(selector, flattened, precision=precise).reshape(
        (cycle_blocks,) + arrived.shape[2:]
    )


def column_owner_plan(values, cycle_taps, phi_taps, cycle_start, phi_start, tile_list, response):
    columns = lax.axis_size("pts")
    part_count = lax.axis_size("tile")
    column = lax.axis_index("pts")
    per_column = values.shape[1] // columns
    tile_width = NPHI // columns
    cycle_part = TR // part_count
    cycle_weights = spread_matrix(cycle_taps[0], cycle_start[0], TR)
    phi_weights = spread_matrix(phi_taps[0], phi_start[0], tile_width)
    loaded = cycle_weights * values[0][:, :, None]
    cycle_split = cycle_weights.reshape(columns, per_column, values.shape[2], part_count, cycle_part)
    loaded_split = loaded.reshape(columns, per_column, values.shape[2], part_count, cycle_part)
    phi_split = phi_weights.reshape(columns, per_column, values.shape[2], tile_width)
    partial_value = contract("qkitr,qkic->qtkrc", loaded_split, phi_split)
    partial_value = partial_value.reshape(columns * part_count, per_column, cycle_part, tile_width)
    arrived = lax.all_to_all(
        partial_value, ("pts", "tile"), split_axis=0, concat_axis=0, tiled=True
    )
    wanted = lax.dynamic_index_in_dim(tile_list, column, 1, keepdims=False)
    owned_tiles = accumulate(arrived, wanted, 256)
    whole_cycles = filter_by_einsum(
        lax.all_to_all(owned_tiles, "pts", split_axis=0, concat_axis=2, tiled=True), response
    )
    filtered = lax.all_to_all(whole_cycles, "pts", split_axis=2, concat_axis=0, tiled=True)
    picked = jnp.take(filtered, wanted.reshape(-1), axis=0)
    picked = picked.reshape(columns * part_count, per_column, cycle_part, tile_width)
    returned = lax.all_to_all(picked, ("pts", "tile"), split_axis=0, concat_axis=0, tiled=True)
    returned = returned.reshape(columns, part_count, per_column, cycle_part, tile_width)
    rows_read = contract("qkitr,qtkrc->qkic", cycle_split, returned)
    gradient = jnp.sum(rows_read * phi_split, axis=-1).reshape(values.shape[1], values.shape[2])
    return (filtered, gradient[None])


def solution(mesh):
    columns, part_count = mesh.shape["pts"], mesh.shape["tile"]
    step, pts, tile = column_owner_plan, "pts", "tile"
    if columns * part_count == TR and columns % 2 == 0 and NPHI // columns == GROUPS * LANES:
        mesh = Mesh(mesh.devices.reshape(2, columns // 2, part_count), AXES)
        step, pts = row_owner_plan, ("half", "share")
    block = (pts, tile) if pts == "pts" else AXES
    return jax.shard_map(
        step,
        mesh=mesh,
        in_specs=(
            P(block, None, None),
            P(block, None, None, None),
            P(block, None, None, None),
            P(block, None, None),
            P(block, None, None),
            P(),
            P(),
        ),
        out_specs=(P(None, tile, pts), P(block, None, None)),
        check_vma=False,
    )
```
